128 devices in a mesh: gx: 8 (over y, core), gy: 16 (over z, x).
Axes of the slice: x: 4, y: 4, z: 4, core: 2. Of those that a mesh axis runs over, the one named last changes fastest.
Arguments:
- rhs: float32 [3, 20, 64, 2048], P(None, None, 'gx', 'gy'), may hold values from -6 to 6
- diag_block: bfloat16 [9, 20, 64, 2048], P(None, None, 'gx', 'gy'), may hold values from -0.5625 to 4.75
- mobility: bfloat16 [9, 20, 64, 2048], P(None, None, 'gx', 'gy'), may hold values from -0.34375 to 1.375
- trans: bfloat16 [3, 20, 64, 2048], P(None, None, 'gx', 'gy'), may hold values from 0.5 to 1
- perf_cell: int32 [128, 8, 128], P(('gx', 'gy')), may hold values from 0 to 20479, as said below
- perf_pi: float32 [128, 8, 128], P(('gx', 'gy')), may hold values from 0 to 0.6, as said below
- perf_seg: int32 [128, 8, 128], P(('gx', 'gy')), may hold values from 0 to 255
- seg_parent: int32 [32768], P(('gx', 'gy')), may hold values from -1 to 254, as said below
- seg_trans: float32 [32768], P(('gx', 'gy')), may hold values from 0.5 to 2
- seg_rhs: float32 [32768], P(('gx', 'gy')), may hold values from -6 to 6
Outputs:
- solution: float32 [3, 20, 64, 2048], P(None, None, 'gx', 'gy')
- seg_pressure: float32 [32768], P(('gx', 'gy'))
The draws below stay inside these ranges and needn't reach their ends.
Inputs may be any that keep to these rules, and one draw needn't show every extreme that they name: `perf_cell`: the 8 slots of a sender-owner pair name consecutive cells along y in one layer and one x column. `perf_pi`: live slots of a sender-owner pair come first among its 8; every sender has one owner with all 8 slots live, and one owner receives all 8 from every sender; some of the owners, drawn from the seed, receive many more than the rest. `seg_parent`: A parent comes just before its segment on the same owner; segment 0 of every owner is at a well head.
All inputs are finite; a program needn't handle non-finite values.
Results may differ from the reference program's by a relative error of at most 0.0003.
Values may be sent and summed in bfloat16 or wider, within the bound.
No kernel may reach another device: no remote copies, remote signals or barrier semaphores. Data moves between devices by JAX's collectives and lax.ppermute only.
A program may use at most 128 MiB of HBM per device.

```python
import math
import jax
import jax.numpy as jnp

COMP = 3
CX = 8
CY = 128
NZ = 20
CAP = 8
SEG_DEV = 256
SWEEPS = 4
OUTER = 2
OWNERS = 128
NX = 64
NY = 2048
SEGS = 32768
N_GY = 16


def draw_rhs(key, part):
    shape = (COMP, NZ, NX, NY)
    base = jax.random.truncated_normal(jax.random.fold_in(key, 7), -6.0, 6.0, shape, jnp.float32)
    return base


def draw_diag_block(key, part):
    first, second = jax.random.split(key)
    shape = (COMP * COMP, NZ, NX, NY)
    ondiag = jax.random.uniform(first, shape, jnp.float32, 3.25, 4.75)
    offdiag = jax.random.uniform(second, shape, jnp.float32, -0.375, 0.375)
    place = (jnp.arange(COMP * COMP) % 4 == 0)[:, None, None, None]
    return jnp.where(place, ondiag, offdiag).astype(jnp.bfloat16)


def draw_mobility(key, part):
    first, second = jax.random.split(jax.random.fold_in(key, 5))
    shape = (COMP * COMP, NZ, NX, NY)
    ondiag = jax.random.uniform(first, shape, jnp.float32, 0.6875, 1.375)
    offdiag = jax.random.uniform(second, shape, jnp.float32, -0.25, 0.25)
    place = (jnp.arange(COMP * COMP) % 4 == 0)[:, None, None, None]
    return jnp.where(place, ondiag, offdiag).astype(jnp.bfloat16)


def draw_perf_cell(key, part):
    keys = jax.random.split(jax.random.fold_in(key, 11), 3)
    layer = jax.random.randint(keys[0], (OWNERS, 1, OWNERS), 0, NZ)
    column = jax.random.randint(keys[1], (OWNERS, 1, OWNERS), 0, CX)
    start = jax.random.randint(keys[2], (OWNERS, 1, OWNERS), 0, CY - CAP + 1)
    sender = jnp.arange(OWNERS)[:, None, None]
    owner = jnp.arange(OWNERS)[None, None, :]
    last_pair = (sender == 0) & (owner == 0)
    first_pair = (sender == 0) & (owner == 1)
    layer = jnp.where(last_pair, NZ - 1, jnp.where(first_pair, 0, layer))
    column = jnp.where(last_pair, CX - 1, jnp.where(first_pair, 0, column))
    start = jnp.where(last_pair, CY - CAP, jnp.where(first_pair, 0, start))
    steps_along = jnp.arange(CAP)[None, :, None]
    return (layer * (CX * CY) + column * CY + start + steps_along).astype(jnp.int32)


def draw_perf_pi(key, part):
    keys = jax.random.split(jax.random.fold_in(key, 3), 6)
    heavy = jax.random.randint(keys[0], (OWNERS,), 0, 4) == 0
    light = jax.random.randint(keys[1], (OWNERS, OWNERS), 0, CAP // 4 + 1)
    loaded = jax.random.randint(keys[2], (OWNERS, OWNERS), CAP // 2, CAP + 1)
    count = jnp.where(heavy[None, :], loaded, light)
    offset = jax.random.randint(keys[3], (), 0, OWNERS)
    target = jax.random.randint(keys[4], (), 0, OWNERS)
    sender = jnp.arange(OWNERS)[:, None]
    owner = jnp.arange(OWNERS)[None, :]
    full = (owner == (sender + offset) % OWNERS) | (owner == target)
    count = jnp.where(full, CAP, count)
    live = jnp.arange(CAP)[None, :, None] < count[:, None, :]
    values = jnp.exp(jax.random.uniform(keys[5], (OWNERS, CAP, OWNERS), jnp.float32, jnp.log(0.1), jnp.log(0.6)))
    return jnp.where(live, values, 0.0)


def draw_seg_parent(key, part):
    flags = jax.random.randint(jax.random.fold_in(key, 9), (SEGS,), 0, 6)
    local = jnp.arange(SEGS, dtype=jnp.int32) % SEG_DEV
    head = (flags == 0) & (local != SEG_DEV - 1) | (local == 0)
    return jnp.where(head, -1, local - 1).astype(jnp.int32)


def touch_ends(values, key, low, high):
    longest = values.shape.index(max(values.shape))
    spots = []
    for shift in (0, 1):
        where = [jax.random.randint(jax.random.fold_in(key, axis), (), 0, length) for axis, length in enumerate(values.shape)]
        where[longest] = (where[longest] + shift) % values.shape[longest]
        spots.append(tuple(where))
    return values.at[spots[0]].set(low).at[spots[1]].set(high)


def block_scale(stream_key, dims, shards, smallest, high):
    gain = 1.0
    for dim, parts in shards:
        draws = jax.random.uniform(jax.random.fold_in(jax.random.fold_in(stream_key, 6), dim), (parts,), jnp.float32, smallest / len(shards), high / len(shards))
        gain = gain * jnp.repeat(jnp.exp(draws), dims[dim] // parts).reshape((-1,) + (1,) * (len(dims) - 1 - dim))
    return gain


def bell_draw(stream_key, dims, width, reach, cuts=(), kind=jnp.bfloat16):
    array = jax.random.normal(stream_key, dims, jnp.float32) * width
    if len(cuts) > 0:
        array = block_scale(stream_key, dims, cuts, -0.22, 0.18) * array
    return jnp.clip(array, min=-reach, max=reach).astype(kind)


def setup_inputs(seed: int = 0) -> dict:
    streams_of = jax.random.split(jax.random.key(seed), 11)
    return {
        "rhs": draw_rhs(jax.random.fold_in(streams_of[10], 71), 0),
        "diag_block": draw_diag_block(jax.random.fold_in(streams_of[10], 71), 0),
        "mobility": draw_mobility(jax.random.fold_in(streams_of[10], 71), 0),
        "trans": jnp.clip(jnp.exp(math.log(1.0) - 0.6931472 * jax.random.uniform(streams_of[3], (COMP, NZ, NX, NY), jnp.float32) ** block_scale(streams_of[3], (COMP, NZ, NX, NY), ((2, 8), (3, 16)), -0.2, 0.2)), 0.5, 1.0).astype(jnp.bfloat16),
        "perf_cell": draw_perf_cell(jax.random.fold_in(streams_of[10], 71), 0),
        "perf_pi": draw_perf_pi(jax.random.fold_in(streams_of[10], 71), 0),
        "perf_seg": touch_ends(jax.random.randint(streams_of[6], (OWNERS, CAP, OWNERS), 0, SEG_DEV), jax.random.fold_in(streams_of[6], 1), 0, SEG_DEV - 1).astype(jnp.int32),
        "seg_parent": draw_seg_parent(jax.random.fold_in(streams_of[10], 71), 0),
        "seg_trans": jnp.clip(jnp.exp(math.log(2.0) - 1.3862944 * jax.random.uniform(streams_of[8], (SEGS,), jnp.float32) ** block_scale(streams_of[8], (SEGS,), ((0, 128),), -0.2, 0.2)), 0.5, 2.0),
        "seg_rhs": bell_draw(streams_of[9], (SEGS,), 1.0, 6.0, ((0, 128),), jnp.float32),
    }


def invert_blocks(mat):
    a, b, c, d, e, f, g, h, i = [mat[position] for position in range(9)]
    first = e * i - f * h
    second = f * g - d * i
    third = d * h - e * g
    determinant = a * first + b * second + c * third
    entries = [first, c * h - b * i, b * f - c * e, second, a * i - c * g, c * d - a * f, third, b * g - a * h, a * e - b * d]
    return jnp.stack([entry / determinant for entry in entries])


def block_apply(mat, vec):
    return jnp.stack([mat[3 * row] * vec[0] + mat[3 * row + 1] * vec[1] + mat[3 * row + 2] * vec[2] for row in range(3)])


def reference(rhs, diag_block, mobility, trans, perf_cell, perf_pi, perf_seg, seg_parent, seg_trans, seg_rhs):
    dense = diag_block.astype(jnp.float32)
    mob_full = mobility.astype(jnp.float32)
    trans_f = trans.astype(jnp.float32)
    inverse = invert_blocks(dense)
    face_x = trans_f[0, :, :-1, :] * trans_f[0, :, 1:, :]
    face_y = trans_f[1, :, :, :-1] * trans_f[1, :, :, 1:]
    face_z = trans_f[2, :-1] * trans_f[2, 1:]
    sender = jnp.arange(OWNERS, dtype=jnp.int32)[:, None, None]
    owner = jnp.arange(OWNERS, dtype=jnp.int32)[None, None, :]
    layer = perf_cell // (CX * CY)
    column_x = (sender // N_GY) * CX + (perf_cell // CY) % CX
    column_y = (sender % N_GY) * CY + perf_cell % CY
    cell_flat = (layer * (NX * NY) + column_x * NY + column_y).reshape(-1).astype(jnp.int32)
    seg_flat = (owner * SEG_DEV + jnp.transpose(perf_seg, (2, 1, 0))).reshape(-1).astype(jnp.int32)
    weights = perf_pi.reshape(-1)
    parent = seg_parent.reshape(OWNERS, SEG_DEV)
    seg_tw = seg_trans.reshape(OWNERS, SEG_DEV)

    def child_total(values):
        def one_owner(vals, par):
            return jax.ops.segment_sum(jnp.where(par >= 0, vals, 0.0), jnp.maximum(par, 0), num_segments=SEG_DEV)
        return jax.vmap(one_owner)(values, parent)

    pi_sum = jnp.zeros((SEGS,), jnp.float32).at[seg_flat].add(weights)
    seg_diag = (seg_tw + child_total(seg_tw)).reshape(-1) + pi_sum

    def residuals(field, seg_state):
        mob_vec = block_apply(mob_full, field)
        near = jnp.zeros_like(field)
        near = near.at[:, :, :-1, :].add(face_x * mob_vec[:, :, 1:, :])
        near = near.at[:, :, 1:, :].add(face_x * mob_vec[:, :, :-1, :])
        near = near.at[:, :, :, :-1].add(face_y * mob_vec[:, :, :, 1:])
        near = near.at[:, :, :, 1:].add(face_y * mob_vec[:, :, :, :-1])
        near = near.at[:, :-1].add(face_z * mob_vec[:, 1:])
        near = near.at[:, 1:].add(face_z * mob_vec[:, :-1])
        flows = weights * (field[0].reshape(-1)[cell_flat] - seg_state[seg_flat])
        into_cells = jnp.zeros((NZ * NX * NY,), jnp.float32).at[cell_flat].add(flows).reshape(NZ, NX, NY)
        cell_res = rhs - block_apply(dense, field) + near - mob_full[0::3] * into_cells
        state = seg_state.reshape(OWNERS, SEG_DEV)
        above = jnp.where(parent >= 0, jnp.take_along_axis(state, jnp.maximum(parent, 0), axis=1), 0.0)
        flux = seg_tw * (state - above)
        into_segs = jnp.zeros((SEGS,), jnp.float32).at[seg_flat].add(flows)
        seg_res = seg_rhs - flux.reshape(-1) + child_total(flux).reshape(-1) + into_segs
        return cell_res, seg_res

    solution = jnp.zeros_like(rhs)
    seg_pressure = jnp.zeros_like(seg_rhs)
    cell_res, seg_res = rhs, seg_rhs
    for outer in range(OUTER):
        field, seg_state = solution, seg_pressure
        cell_now, seg_now = cell_res, seg_res
        for sweep in range(SWEEPS):
            field = field + block_apply(inverse, cell_now)
            seg_state = seg_state + seg_now / seg_diag
            cell_now, seg_now = residuals(field, seg_state)
        cell_diff = cell_res - cell_now
        seg_diff = seg_res - seg_now
        numer = jnp.sum(cell_res * cell_diff) + jnp.sum(seg_res * seg_diff)
        denom = jnp.sum(cell_diff * cell_diff) + jnp.sum(seg_diff * seg_diff)
        omega = numer / denom
        solution = solution + omega * (field - solution)
        seg_pressure = seg_pressure + omega * (seg_state - seg_pressure)
        cell_res = cell_res - omega * cell_diff
        seg_res = seg_res - omega * seg_diff
    return solution, seg_pressure
```

```python
import functools

import jax
import jax.numpy as jnp
from jax import lax
from jax.experimental import pallas as pl
from jax.experimental.pallas import tpu as pltpu
from jax.sharding import PartitionSpec as P

F32 = jnp.float32
BF16 = jnp.bfloat16
AXES = ("gx", "gy")
NZ, CX, CY = 20, 8, 128
ROWS = NZ * CX
STEP = 16
CHUNKS = ROWS // STEP
PEERS = 128
CAP = 8


def lanes(shape):
    return lax.broadcasted_iota(jnp.int32, shape, 1)


def subs(shape):
    return lax.broadcasted_iota(jnp.int32, shape, 0)


def split3(x):
    high = x.astype(BF16)
    rest = x - high.astype(F32)
    mid = rest.astype(BF16)
    low = (rest - mid.astype(F32)).astype(BF16)
    return high, mid, low


def pick_rows(onehot, x):
    high, mid, low = split3(x)

    def dot(part):
        return lax.dot_general(onehot, part, (((1,), (0,)), ((), ())), preferred_element_type=F32)

    return (dot(low) + dot(mid)) + dot(high)


def slot_values(rows_of, start, first):
    lane = lanes((PEERS, CY))
    picked = pick_rows(rows_of, first)
    window = jnp.take_along_axis(picked, (start + lane) & (CY - 1), axis=1)
    return jnp.where(lane < CAP, window, 0.0)


def into_cells(rows_to, start, flows):
    lane = lanes((PEERS, CY))
    spread = jnp.take_along_axis(flows, (lane - start) & (CY - 1), axis=1)
    return pick_rows(rows_to, spread)


def segment_values(state, index):
    low = index & 127
    first = jnp.take_along_axis(jnp.broadcast_to(state[0:1], (8, 128)), low, axis=1)
    second = jnp.take_along_axis(jnp.broadcast_to(state[1:2], (8, 128)), low, axis=1)
    return jnp.where(index >= 128, second, first)


def into_segments(values, index, table):
    parts = [part.astype(F32) for part in split3(values)]
    sub = subs((16, 128))
    upper = (index >= 128).astype(jnp.int32)
    tiles = []
    for k in range(CAP):
        row = [jnp.broadcast_to(part[k : k + 1], (16, 128)) for part in parts]
        mine = jnp.broadcast_to(upper[k : k + 1], (16, 128)) == (sub & 1)
        tile = jnp.where(sub < 2, row[0], jnp.where(sub < 4, row[1], row[2]))
        tiles.append(jnp.where(mine & (sub < 6), tile, 0.0).astype(BF16))
    left = jnp.concatenate(tiles, axis=1)
    out = lax.dot_general(left, table, (((1,), (1,)), ((), ())), preferred_element_type=F32)[:8]
    total = (pltpu.roll(out, 4, 0) + pltpu.roll(out, 6, 0)) + out
    return jnp.where(subs((8, 128)) < 2, total, 0.0)


def previous(state):
    moved = pltpu.roll(state, 1, 1)
    return jnp.where(lanes((8, 128)) == 0, pltpu.roll(moved, 1, 0), moved)


def following(state):
    moved = pltpu.roll(state, 127, 1)
    return jnp.where(lanes((8, 128)) == 127, pltpu.roll(moved, 7, 0), moved)


def to_columns(values):
    tall = jnp.concatenate(
        [jnp.zeros((8, 128), F32), values, jnp.zeros((112, 128), F32)], axis=0
    )
    return tall.T


def chunk(t):
    return pl.ds(t * STEP, STEP)


def cell_setup(rhs, diag, cells, pi, inverse, first, message, rows_of, rows_to, start, weight, slots):
    for t in range(CHUNKS):
        rows = chunk(t)
        a, b, c, d, e, f, g, h, i = [diag[n, rows, :].astype(F32) for n in range(9)]
        p, q, s = e * i - f * h, f * g - d * i, d * h - e * g
        scale = 1.0 / (a * p + b * q + c * s)
        entries = [
            p, c * h - b * i, b * f - c * e,
            q, a * i - c * g, c * d - a * f,
            s, b * g - a * h, a * e - b * d,
        ]
        entries = [entry * scale for entry in entries]
        x, y, z = [rhs[n, rows, :] for n in range(3)]
        for n in range(9):
            inverse[n, rows, :] = entries[n]
        for n in range(3):
            first[n, rows, :] = entries[3 * n] * x + entries[3 * n + 1] * y + entries[3 * n + 2] * z
    base = cells[0:1, :]
    row = lax.shift_right_logical(base, 7)
    lane = lanes((PEERS, 128))
    info = jnp.concatenate(
        [pi[...], jnp.broadcast_to(row.astype(F32), (8, 128)),
         jnp.broadcast_to((base & 127).astype(F32), (8, 128)), jnp.zeros((104, 128), F32)],
        axis=0,
    ).T
    rows_to[...] = (subs((ROWS, PEERS)) == jnp.broadcast_to(row, (ROWS, PEERS))).astype(F32).astype(BF16)
    row_column = jnp.broadcast_to(info[:, 8:9], (PEERS, ROWS)).astype(jnp.int32)
    rows_of[...] = (lanes((PEERS, ROWS)) == row_column).astype(F32).astype(BF16)
    begin = jnp.broadcast_to(info[:, 16:17], (PEERS, 128)).astype(jnp.int32)
    start[...] = begin
    weights = jnp.where(lane < CAP, info, 0.0)
    weight[...] = weights
    values = slot_values(rows_of[...], begin, first[0])
    slots[...] = values
    message[...] = values + pltpu.roll(weights, 8, 1)


def well_setup(arrived, slots, index, parent, trans, rhs, message, weight, table, state, at_slots, fixed):
    turned = arrived[...].T
    pi = turned[8:16]
    weight[...] = pi
    number = index[...]
    low = number & 127
    for k in range(CAP):
        hit = subs((128, 128)) == jnp.broadcast_to(low[k : k + 1], (128, 128))
        table[:, 128 * k : 128 * (k + 1)] = hit.astype(F32).astype(BF16)
    zeros = jnp.zeros((6, 128), F32)
    linked = jnp.concatenate([(parent[...] >= 0).astype(F32), zeros], axis=0)
    across = jnp.concatenate([trans[...], zeros], axis=0)
    source = jnp.concatenate([rhs[...], zeros], axis=0)
    diagonal = across + following(linked * across) + into_segments(pi, number, table[...])
    diagonal = jnp.where(subs((8, 128)) < 2, diagonal, 1.0)
    fixed[0] = linked
    fixed[1] = across
    fixed[2] = source
    fixed[3] = diagonal
    now = source / diagonal
    state[...] = now
    values = segment_values(now, number)
    at_slots[...] = values
    message[...] = slots[...] + to_columns(values)


def borders(field, mobility, trans, weighted, toward_low, toward_high, sides, scratch):
    for t in range(CHUNKS):
        rows = chunk(t)
        x, y, z = [field[n, rows, :] for n in range(3)]
        along = trans[0, rows, :].astype(F32)
        for n in range(3):
            value = (
                mobility[3 * n, rows, :].astype(F32) * x
                + mobility[3 * n + 1, rows, :].astype(F32) * y
                + mobility[3 * n + 2, rows, :].astype(F32) * z
            )
            weighted[n, rows, :] = value
            scratch[pl.ds(n * ROWS + t * STEP, STEP), :] = along * value
    toward_low[...] = scratch[pl.ds(0, 3 * NZ, stride=CX), :]
    toward_high[...] = scratch[pl.ds(CX - 1, 3 * NZ, stride=CX), :]
    pair = lax.shift_right_logical(lanes((8, 128)), 1)
    packed = jnp.zeros((8, 128), F32)
    for t in range(CHUNKS):
        across = trans[1, chunk(t), :].astype(F32)
        for n in range(3):
            value = across * weighted[n, chunk(t), :]
            for half in range(2):
                j = n * NZ + 2 * t + half
                moved = pltpu.roll(value[8 * half : 8 * half + 8], (2 * j + 1) % 128, 1)
                packed = jnp.where(pair == j, moved, packed)
    sides[...] = packed


def interior(field, weighted, diag, trans, rhs, base, scratch):
    for n in range(3):
        scratch[n, 0:8, :] = jnp.zeros((8, 128), F32)
        scratch[n, ROWS + 8 : ROWS + 16, :] = jnp.zeros((8, 128), F32)
    for t in range(CHUNKS):
        up = trans[2, chunk(t), :].astype(F32)
        for n in range(3):
            scratch[n, pl.ds(8 + t * STEP, STEP), :] = up * weighted[n, chunk(t), :]
    lane = lanes((STEP, 128))
    sub = subs((STEP, 128)) & 7
    for t in range(CHUNKS):
        rows = chunk(t)
        x, y, z = [field[n, rows, :] for n in range(3)]
        tx, ty, tz = [trans[n, rows, :].astype(F32) for n in range(3)]
        for n in range(3):
            value = weighted[n, rows, :]
            px, py = tx * value, ty * value
            nx = jnp.where(sub == 0, 0.0, pltpu.roll(px, 1, 0)) + jnp.where(
                sub == 7, 0.0, pltpu.roll(px, STEP - 1, 0)
            )
            ny = jnp.where(lane == 0, 0.0, pltpu.roll(py, 1, 1)) + jnp.where(
                lane == 127, 0.0, pltpu.roll(py, 127, 1)
            )
            nz = scratch[n, pl.ds(t * STEP, STEP), :] + scratch[n, pl.ds(t * STEP + 16, STEP), :]
            near = tx * nx + ty * ny + tz * nz
            own = (
                diag[3 * n, rows, :].astype(F32) * x
                + diag[3 * n + 1, rows, :].astype(F32) * y
                + diag[3 * n + 2, rows, :].astype(F32) * z
            )
            base[n, rows, :] = (rhs[n, rows, :] - own) + near


MOVING = ("arrived", "base", "field", "from_low", "from_high", "side_low", "side_high",
          "slots", "at_slots", "state")
STEADY = ("inverse", "mobility", "trans", "rows_of", "rows_to", "start", "weight",
          "own_weight", "table", "index", "fixed")


def extras_of(last, final):
    if final:
        return ("rhs", "residual", "seg_residual", "omega")
    return ("rhs",) if last else ()


def results_of(blend, last, final):
    if final:
        return ("message",)
    names = ("field", "slots", "at_slots", "state", "message")
    return names + (("omega",) if blend else ()) + (("residual", "seg_residual") if last else ())


def spread_pair(two):
    return jnp.concatenate(
        [jnp.broadcast_to(two[h : h + 1], (8, 128)) for h in range(2)], axis=0
    )


def ratio(turned):
    numer = jnp.sum(turned[16:17], axis=1, keepdims=True)
    denom = jnp.sum(turned[17:18], axis=1, keepdims=True)
    return numer / denom


def sweep(blend, last, final, *refs):
    take = iter(refs)
    now = {name: next(take) for name in MOVING}
    early = {name: next(take) for name in MOVING} if blend else None
    fixed = {name: next(take) for name in STEADY}
    extra = {name: next(take) for name in extras_of(last, final)}
    out = {name: next(take) for name in results_of(blend, last, final)}
    if blend:
        omega = ratio(now["arrived"][...].T)
        out["omega"][...] = jnp.broadcast_to(omega, (8, 128))

    def get(name, *where):
        where = where or (Ellipsis,)
        value = now[name][where]
        if blend:
            old = early[name][where]
            value = old + omega * (value - old)
        return value

    arrived = get("arrived")
    turned = arrived.T
    pull = fixed["weight"][...] * (get("slots") - pltpu.roll(arrived, 120, 1))
    perforated = into_cells(fixed["rows_to"][...], fixed["start"][...], pull)

    state = get("state")
    linked, across, source, diagonal = [fixed["fixed"][n] for n in range(4)]
    push = fixed["own_weight"][...] * (turned[0:8] - get("at_slots"))
    number = fixed["index"][...]
    inflow = into_segments(push, number, fixed["table"][...])
    flux = across * (state - linked * previous(state))
    seg_res = source - flux + following(linked * flux) + inflow

    lane = lanes((STEP, 128))
    sub = subs((STEP, 128)) & 7
    odd = (lanes((8, 128)) & 1) == 1
    sides = jnp.where(
        odd, pltpu.roll(get("side_low"), 1, 1), pltpu.roll(get("side_high"), 127, 1)
    )
    numer = jnp.zeros((STEP, 128), F32)
    denom = jnp.zeros((STEP, 128), F32)
    if final:
        omega = extra["omega"][0:1, 0:1]
    for t in range(CHUNKS):
        rows = chunk(t)
        tx, ty = [fixed["trans"][n, rows, :].astype(F32) for n in range(2)]
        residual = []
        for n in range(3):
            j = n * NZ + 2 * t
            low = get("from_low", pl.ds(j, 2), slice(None))
            high = get("from_high", pl.ds(j, 2), slice(None))
            nx = jnp.where(sub == 0, spread_pair(low), jnp.where(sub == 7, spread_pair(high), 0.0))
            side = jnp.concatenate(
                [pltpu.roll(sides, (127 - 2 * (j + h)) % 128, 1) for h in range(2)], axis=0
            )
            ny = jnp.where((lane == 0) | (lane == 127), side, 0.0)
            share = fixed["mobility"][3 * n, rows, :].astype(F32)
            value = get("base", n, rows, slice(None)) + tx * nx + ty * ny
            residual.append(value - share * perforated[t * STEP : (t + 1) * STEP])
        for n in range(3):
            if last or final:
                before = extra["rhs"][n, rows, :]
                if final:
                    before = before + omega * (extra["residual"][n, rows, :] - before)
                change = before - residual[n]
                numer += before * change
                denom += change * change
            if last:
                out["residual"][n, rows, :] = residual[n]
            if not final:
                entry = [fixed["inverse"][3 * n + m, rows, :] for m in range(3)]
                out["field"][n, rows, :] = get("field", n, rows, slice(None)) + (
                    entry[0] * residual[0] + entry[1] * residual[1] + entry[2] * residual[2]
                )
    message = jnp.zeros((PEERS, 128), F32)
    if not final:
        advanced = state + seg_res / diagonal
        out["state"][...] = advanced
        values = segment_values(advanced, number)
        out["at_slots"][...] = values
        cells = slot_values(fixed["rows_of"][...], fixed["start"][...], out["field"][0])
        out["slots"][...] = cells
        message = cells + to_columns(values)
    if last or final:
        before = source
        if final:
            before = before + omega * (extra["seg_residual"][...] - before)
        change = before - seg_res
        above = jnp.sum(numer, keepdims=True) + jnp.sum(before * change, keepdims=True)
        below = jnp.sum(denom, keepdims=True) + jnp.sum(change * change, keepdims=True)
        place = lanes((PEERS, 128))
        message += jnp.where(place == 16, above, jnp.where(place == 17, below, 0.0))
    if last:
        out["seg_residual"][...] = seg_res
    out["message"][...] = message


def finish(arrived, omega, field_one, field_two, state_one, state_two, cells, segments):
    first = omega[0:1, 0:1]
    second = ratio(arrived[...].T)
    for n in range(3):
        for t in range(CHUNKS):
            kept = first * field_one[n, chunk(t), :]
            cells[n, chunk(t), :] = kept + second * (field_two[n, chunk(t), :] - kept)
    kept = first * state_one[0:2]
    segments[...] = kept + second * (state_two[0:2] - kept)


CELLS = ((3, ROWS, 128), F32)
PAIRS = ((PEERS, 128), F32)
TILE = ((8, 128), F32)
EDGE = ((3 * NZ, 128), F32)
SHAPES = {
    "field": CELLS, "residual": CELLS, "message": PAIRS, "slots": PAIRS,
    "at_slots": TILE, "state": TILE, "omega": TILE, "seg_residual": TILE,
}


def call(body, outs, args, scratch=(), name=None):
    moved = sum(a.size * a.dtype.itemsize for a in args)
    return pl.pallas_call(
        body,
        out_shape=[jax.ShapeDtypeStruct(*out) for out in outs],
        in_specs=[pl.BlockSpec(memory_space=pltpu.VMEM)] * len(args),
        out_specs=[pl.BlockSpec(memory_space=pltpu.VMEM)] * len(outs),
        scratch_shapes=list(scratch),
        compiler_params=pltpu.CompilerParams(vmem_limit_bytes=24 * 1024 * 1024),
        cost_estimate=pl.CostEstimate(flops=4_000_000, bytes_accessed=moved, transcendentals=0),
        name=name,
    )(*args)


def exchange(message):
    return lax.all_to_all(message, AXES, split_axis=0, concat_axis=0, tiled=True)


def neighbours(toward_low, toward_high, sides):
    up_x = [(i, i + 1) for i in range(lax.axis_size("gx") - 1)]
    up_y = [(i, i + 1) for i in range(lax.axis_size("gy") - 1)]
    down_x = [(b, a) for a, b in up_x]
    down_y = [(b, a) for a, b in up_y]
    return {
        "from_low": lax.ppermute(toward_high, "gx", up_x),
        "from_high": lax.ppermute(toward_low, "gx", down_x),
        "side_low": lax.ppermute(sides, "gy", up_y),
        "side_high": lax.ppermute(sides, "gy", down_y),
    }


def on_device(
    rhs, diag_block, mobility, trans, perf_cell, perf_pi, perf_seg, seg_parent, seg_trans, seg_rhs
):
    rhs = rhs.reshape(3, ROWS, 128)
    diag = diag_block.reshape(9, ROWS, 128)
    mobility = mobility.reshape(9, ROWS, 128)
    trans = trans.reshape(3, ROWS, 128)
    index = perf_seg[0]

    fixed = {"mobility": mobility, "trans": trans, "index": index}
    inverse, first, message, rows_of, rows_to, start, weight, slots = call(
        cell_setup,
        [((9, ROWS, 128), F32), CELLS, PAIRS, ((PEERS, ROWS), BF16), ((ROWS, PEERS), BF16),
         ((PEERS, 128), jnp.int32), PAIRS, PAIRS],
        [rhs, diag, perf_cell[0], perf_pi[0]],
        name="cell_setup",
    )
    fixed.update(inverse=inverse, rows_of=rows_of, rows_to=rows_to, start=start, weight=weight)
    arrived = exchange(message)

    def prepare(field):
        weighted, toward_low, toward_high, sides = call(
            borders,
            [CELLS, EDGE, EDGE, TILE],
            [field, mobility, trans],
            [pltpu.VMEM((3 * ROWS, 128), F32)],
            name="borders",
        )
        found = neighbours(toward_low, toward_high, sides)
        (found["base"],) = call(
            interior,
            [CELLS],
            [field, weighted, diag, trans, rhs],
            [pltpu.VMEM((3, ROWS + 16, 128), F32)],
            name="interior",
        )
        found["field"] = field
        return found

    now = prepare(first)
    message, own_weight, table, state, at_slots, constants = call(
        well_setup,
        [PAIRS, TILE, ((128, CAP * 128), BF16), TILE, TILE, ((4, 8, 128), F32)],
        [arrived, slots, index, seg_parent.reshape(2, 128), seg_trans.reshape(2, 128),
         seg_rhs.reshape(2, 128)],
        name="well_setup",
    )
    fixed.update(own_weight=own_weight, table=table, fixed=constants)
    now.update(arrived=exchange(message), slots=slots, at_slots=at_slots, state=state)

    def advance(now, early=None, last=False, final=False, extra=None):
        blend = early is not None
        args = [now[name] for name in MOVING]
        if blend:
            args += [early[name] for name in MOVING]
        args += [fixed[name] for name in STEADY]
        args += [extra[name] for name in extras_of(last, final)]
        names = results_of(blend, last, final)
        out = call(
            functools.partial(sweep, blend, last, final),
            [SHAPES[name] for name in names],
            args,
            name="sweep",
        )
        out = dict(zip(names, out))
        out["arrived"] = exchange(out.pop("message"))
        if not final:
            out.update(prepare(out["field"]))
        return out

    early = now
    now = advance(now)
    now = advance(now)
    one = advance(now)
    kept = advance(one, last=True, extra={"rhs": rhs})
    now = advance(kept, early=early)
    kept["omega"] = now["omega"]
    now = advance(now)
    two = advance(now)
    kept["rhs"] = rhs
    sums = advance(two, final=True, extra=kept)
    cells, segments = call(
        finish,
        [CELLS, ((2, 128), F32)],
        [sums["arrived"], kept["omega"], one["field"], two["field"], one["state"], two["state"]],
        name="finish",
    )
    return cells.reshape(3, NZ, CX, CY), segments.reshape(256)


def solution(mesh):
    grid = P(None, None, "gx", "gy")
    pairs = P(AXES, None, None)
    flat = P(AXES)
    return jax.shard_map(
        on_device,
        mesh=mesh,
        in_specs=(grid, grid, grid, grid, pairs, pairs, pairs, flat, flat, flat),
        out_specs=(grid, flat),
        check_vma=False,
    )
```

```python
import functools

import jax
import jax.numpy as jnp
from jax import lax
from jax.experimental import pallas as pl
from jax.experimental.pallas import tpu as pltpu
from jax.sharding import PartitionSpec as P

F32 = jnp.float32
BF16 = jnp.bfloat16
AXES = ("gx", "gy")
NZ, CX, CY = 20, 8, 128
ROWS = NZ * CX
STEP = 16
CHUNKS = ROWS // STEP
PEERS = 128
CAP = 8


def lanes(shape):
    return lax.broadcasted_iota(jnp.int32, shape, 1)


def subs(shape):
    return lax.broadcasted_iota(jnp.int32, shape, 0)


def split3(x):
    high = x.astype(BF16)
    rest = x - high.astype(F32)
    mid = rest.astype(BF16)
    low = (rest - mid.astype(F32)).astype(BF16)
    return high, mid, low


def pick_rows(onehot, x):
    high, mid, low = split3(x)

    def dot(part):
        return lax.dot_general(onehot, part, (((1,), (0,)), ((), ())), preferred_element_type=F32)

    return (dot(low) + dot(mid)) + dot(high)


def is_slot(lane):
    return (lane & 63) >= 60


def slot_values(rows_of, start, first):
    lane = lanes((PEERS, CY))
    number = (lane & 3) + jnp.where(lane >= 64, 4, 0)
    picked = pick_rows(rows_of, first)
    window = jnp.take_along_axis(picked, (start + number) & (CY - 1), axis=1)
    return jnp.where(is_slot(lane), window, 0.0)


def into_cells(rows_to, start, flows):
    number = (lanes((PEERS, CY)) - start) & (CY - 1)
    place = jnp.where(number < 4, number + 60, jnp.where(number < CAP, number + 120, 0))
    return pick_rows(rows_to, jnp.take_along_axis(flows, place, axis=1))


def segment_values(state, index):
    low = index & 127
    first = jnp.take_along_axis(jnp.broadcast_to(state[0:1], (8, 128)), low, axis=1)
    second = jnp.take_along_axis(jnp.broadcast_to(state[1:2], (8, 128)), low, axis=1)
    return jnp.where(index >= 128, second, first)


def into_segments(values, index, table):
    parts = [part.astype(F32) for part in split3(values)]
    sub = subs((16, 128))
    upper = (index >= 128).astype(jnp.int32)
    tiles = []
    for k in range(CAP):
        row = [jnp.broadcast_to(part[k : k + 1], (16, 128)) for part in parts]
        mine = jnp.broadcast_to(upper[k : k + 1], (16, 128)) == (sub & 1)
        tile = jnp.where(sub < 2, row[0], jnp.where(sub < 4, row[1], row[2]))
        tiles.append(jnp.where(mine & (sub < 6), tile, 0.0).astype(BF16))
    left = jnp.concatenate(tiles, axis=1)
    out = lax.dot_general(left, table, (((1,), (1,)), ((), ())), preferred_element_type=F32)[:8]
    total = (pltpu.roll(out, 4, 0) + pltpu.roll(out, 6, 0)) + out
    return jnp.where(subs((8, 128)) < 2, total, 0.0)


def previous(state):
    moved = pltpu.roll(state, 1, 1)
    return jnp.where(lanes((8, 128)) == 0, pltpu.roll(moved, 1, 0), moved)


def following(state):
    moved = pltpu.roll(state, 127, 1)
    return jnp.where(lanes((8, 128)) == 127, pltpu.roll(moved, 7, 0), moved)


def to_columns(values):
    gap = jnp.zeros((60, 128), F32)
    return jnp.concatenate([gap, values[0:4], gap, values[4:8]], axis=0).T


def to_rows(columns):
    turned = columns.T
    return jnp.concatenate([turned[60:64], turned[124:128]], axis=0)


def block(n):
    return pl.ds(n, PEERS, stride=4)


def chunk(t):
    return pl.ds(t * STEP, STEP)


def me():
    return lax.axis_index("gx") * 16 + lax.axis_index("gy")


def peer_rows(shift):
    return pl.ds(4 * ((me() + shift) & (PEERS - 1)), 4)


def tile_to_rows(tile, pad):
    pad[0:8] = tile
    pad[8:16] = pltpu.roll(tile, 64, 1)
    even = pad[pl.ds(0, 4, stride=2), :]
    odd = pad[pl.ds(9, 4, stride=2), :]
    return jnp.where(lanes((4, 128)) < 64, even, odd)


def rows_to_tile(four, pad):
    pad[0:4] = four
    pad[8:16] = pltpu.roll(pad[0:8], 64, 1)
    low, high = pad[0:4], pad[8:12]
    pad[pl.ds(0, 4, stride=2), :] = low
    pad[pl.ds(1, 4, stride=2), :] = high
    return pad[0:8]


def mix(matrix, rows, vector):
    entry = [matrix[n, rows, :].astype(F32) for n in range(9)]
    x, y, z = vector
    return [entry[3 * n] * x + entry[3 * n + 1] * y + entry[3 * n + 2] * z for n in range(3)]


def borders(values, mobility, trans, weighted, along, t):
    rows = chunk(t)
    tx = trans[0, rows, :].astype(F32)
    for n, value in enumerate(mix(mobility, rows, values)):
        weighted[n, pl.ds(8 + t * STEP, STEP), :] = value
        along[pl.ds(n * ROWS + t * STEP, STEP), :] = tx * value


def interior(trans, weighted, along, near, toward_low, toward_high, message, pad):
    toward_low[...] = along[pl.ds(0, 3 * NZ, stride=CX), :]
    toward_high[...] = along[pl.ds(CX - 1, 3 * NZ, stride=CX), :]
    lane = lanes((STEP, 128))
    sub = subs((STEP, 128)) & 7
    small = lanes((8, 128))
    high = jnp.zeros((8, 128), F32)
    low = jnp.zeros((8, 128), F32)
    for n in range(3):
        weighted[n, 0:8, :] = jnp.zeros((8, 128), F32)
        weighted[n, ROWS + 8 : ROWS + 16, :] = jnp.zeros((8, 128), F32)
    up = [trans[2, chunk(t), :].astype(F32) for t in range(CHUNKS)]
    for t in range(CHUNKS):
        rows = chunk(t)
        tx, ty = [trans[n, rows, :].astype(F32) for n in range(2)]
        tz = up[t]
        zero = jnp.zeros((8, 128), F32)
        below = jnp.concatenate([up[t - 1][8:16] if t else zero, tz[0:8]], axis=0)
        above = jnp.concatenate([tz[8:16], up[t + 1][0:8] if t + 1 < CHUNKS else zero], axis=0)
        for n in range(3):
            px = along[pl.ds(n * ROWS + t * STEP, STEP), :]
            py = ty * weighted[n, pl.ds(8 + t * STEP, STEP), :]
            nx = jnp.where(sub == 0, 0.0, pltpu.roll(px, 1, 0)) + jnp.where(
                sub == 7, 0.0, pltpu.roll(px, STEP - 1, 0)
            )
            ny = jnp.where(lane == 0, 0.0, pltpu.roll(py, 1, 1)) + jnp.where(
                lane == 127, 0.0, pltpu.roll(py, 127, 1)
            )
            nz = below * weighted[n, pl.ds(t * STEP, STEP), :] + above * weighted[
                n, pl.ds(t * STEP + 16, STEP), :
            ]
            near[n, rows, :] = tx * nx + ty * ny + tz * nz
            for half in range(2):
                j = n * NZ + 2 * t + half
                moved = pltpu.roll(py[8 * half : 8 * half + 8], j + 1, 1)
                high = jnp.where(small == j, moved, high)
                low = jnp.where(small == j + 1, moved, low)
    low = pltpu.roll(low, 127, 1)
    mine = is_slot(lanes((4, 128)))
    for shift, tile in ((1, high), (-1, low)):
        rows = peer_rows(shift)
        packed = tile_to_rows(tile, pad)
        message[rows, :] = jnp.where(mine, message[rows, :], packed)


def cell_setup(rhs, diag, mobility, trans, cells, pi,
               inverse, first, rows_of, rows_to, start, weight, slots,
               near, toward_low, toward_high, message, weighted, along, pad):
    for t in range(CHUNKS):
        rows = chunk(t)
        a, b, c, d, e, f, g, h, i = [diag[n, rows, :].astype(F32) for n in range(9)]
        p, q, s = e * i - f * h, f * g - d * i, d * h - e * g
        scale = 1.0 / (a * p + b * q + c * s)
        entries = [
            p, c * h - b * i, b * f - c * e,
            q, a * i - c * g, c * d - a * f,
            s, b * g - a * h, a * e - b * d,
        ]
        entries = [entry * scale for entry in entries]
        x, y, z = [rhs[n, rows, :] for n in range(3)]
        for n in range(9):
            inverse[n, rows, :] = entries[n]
        values = [
            entries[3 * n] * x + entries[3 * n + 1] * y + entries[3 * n + 2] * z for n in range(3)
        ]
        for n in range(3):
            first[n, rows, :] = values[n]
        borders(values, mobility, trans, weighted, along, t)
    base = cells[0:1, :]
    row = lax.shift_right_logical(base, 7)
    live = pi[...]
    gap = jnp.zeros((44, 128), F32)
    info = jnp.concatenate(
        [jnp.broadcast_to(row.astype(F32), (8, 128)),
         jnp.broadcast_to((base & 127).astype(F32), (8, 128)),
         gap, live[0:4], gap, jnp.zeros((16, 128), F32), live[4:8]],
        axis=0,
    ).T
    rows_to[...] = (subs((ROWS, PEERS)) == jnp.broadcast_to(row, (ROWS, PEERS))).astype(F32).astype(BF16)
    row_column = jnp.broadcast_to(info[:, 0:1], (PEERS, ROWS)).astype(jnp.int32)
    rows_of[...] = (lanes((PEERS, ROWS)) == row_column).astype(F32).astype(BF16)
    begin = jnp.broadcast_to(info[:, 8:9], (PEERS, 128)).astype(jnp.int32)
    start[...] = begin
    weights = jnp.where(is_slot(lanes((PEERS, 128))), info, 0.0)
    weight[...] = weights
    values = slot_values(rows_of[...], begin, first[0])
    slots[...] = values
    message[block(0), :] = values
    message[block(1), :] = weights
    message[block(2), :] = jnp.zeros((PEERS, 128), F32)
    message[block(3), :] = jnp.zeros((PEERS, 128), F32)
    interior(trans, weighted, along, near, toward_low, toward_high, message, pad)


def well_setup(arrived, index, parent, trans, rhs, message, weight, table, state, at_slots, fixed):
    pi = to_rows(arrived[block(1), :])
    weight[...] = pi
    number = index[...]
    low = number & 127
    for k in range(CAP):
        hit = subs((128, 128)) == jnp.broadcast_to(low[k : k + 1], (128, 128))
        table[:, 128 * k : 128 * (k + 1)] = hit.astype(F32).astype(BF16)
    zeros = jnp.zeros((6, 128), F32)
    linked = jnp.concatenate([(parent[...] >= 0).astype(F32), zeros], axis=0)
    across = jnp.concatenate([trans[...], zeros], axis=0)
    source = jnp.concatenate([rhs[...], zeros], axis=0)
    diagonal = across + following(linked * across) + into_segments(pi, number, table[...])
    diagonal = jnp.where(subs((8, 128)) < 2, diagonal, 1.0)
    fixed[0] = linked
    fixed[1] = across
    fixed[2] = source
    fixed[3] = diagonal
    now = source / diagonal
    state[...] = now
    values = segment_values(now, number)
    at_slots[...] = values
    message[...] = to_columns(values)


def ratio(sums, place):
    total = jnp.sum(sums, axis=0, keepdims=True)
    lane = lanes((1, 128))
    numer = jnp.sum(jnp.where(lane == place, total, 0.0), axis=1, keepdims=True)
    denom = jnp.sum(jnp.where(lane == place + 1, total, 0.0), axis=1, keepdims=True)
    return numer / denom


def spread_pair(two):
    return jnp.concatenate(
        [jnp.broadcast_to(two[h : h + 1], (8, 128)) for h in range(2)], axis=0
    )


STEADY = ("first", "inverse", "mobility", "trans", "rows_of", "rows_to", "start", "weight",
          "own_weight", "table", "index", "fixed")
MOVING = ("arrived", "near", "from_low", "from_high", "slots", "at_slots", "state")
NEXT = ("near", "toward_low", "toward_high", "message", "slots", "at_slots", "state")
MORE_IN = {
    "first": ("pressures",), "plain": (), "keep": (), "last": ("diag", "rhs", "field"), "after": (),
    "final": ("diag", "rhs", "field", "change", "seg_change", "omega"),
}
MORE_OUT = {
    "first": (), "plain": (), "keep": ("field",), "last": ("change", "seg_change"),
    "after": ("omega",), "final": (),
}


def results_of(kind):
    return ("message",) if kind == "final" else NEXT + MORE_OUT[kind]


def sweep(kind, *refs):
    take = iter(refs)
    now = {name: next(take) for name in MOVING}
    fixed = {name: next(take) for name in STEADY}
    extra = {name: next(take) for name in MORE_IN[kind]}
    out = {name: next(take) for name in results_of(kind)}
    weighted, along, pad, forward = take
    final = kind == "final"
    gx, gy = lax.axis_index("gx"), lax.axis_index("gy")

    arrived = now["arrived"]
    pressures = extra["pressures"][...] if kind == "first" else arrived[block(1), :]
    pull = fixed["weight"][...] * (now["slots"][...] - pressures)
    perforated = into_cells(fixed["rows_to"][...], fixed["start"][...], pull)

    side_low = rows_to_tile(arrived[peer_rows(-1), :], pad)
    side_high = rows_to_tile(arrived[peer_rows(1), :], pad)
    side_low = jnp.where(gy == 0, 0.0, side_low)
    side_high = jnp.where(gy == lax.axis_size("gy") - 1, 0.0, side_high)
    open_low, open_high = gx > 0, gx < lax.axis_size("gx") - 1

    state = now["state"][...]
    linked, across, source, diagonal = [fixed["fixed"][n] for n in range(4)]
    push = fixed["own_weight"][...] * (to_rows(arrived[block(0), :]) - now["at_slots"][...])
    number = fixed["index"][...]
    inflow = into_segments(push, number, fixed["table"][...])
    flux = across * (state - linked * previous(state))
    seg_res = source - flux + following(linked * flux) + inflow

    lane = lanes((STEP, 128))
    sub = subs((STEP, 128)) & 7
    numer = jnp.zeros((STEP, 128), F32)
    denom = jnp.zeros((STEP, 128), F32)
    if final:
        omega = extra["omega"][0:1, 0:1]
    for t in range(CHUNKS):
        rows = chunk(t)
        tx, ty = [fixed["trans"][n, rows, :].astype(F32) for n in range(2)]
        terms = []
        for n in range(3):
            j = n * NZ + 2 * t
            low = jnp.where(open_low, now["from_low"][j : j + 2, :], 0.0)
            high = jnp.where(open_high, now["from_high"][j : j + 2, :], 0.0)
            nx = jnp.where(sub == 0, spread_pair(low), jnp.where(sub == 7, spread_pair(high), 0.0))
            before = [pltpu.roll(side_low, (128 - j - h) % 128, 1) for h in range(2)]
            behind = [pltpu.roll(side_high, 127 - j - h, 1) for h in range(2)]
            ny = jnp.where(
                lane == 0, jnp.concatenate(before, axis=0),
                jnp.where(lane == 127, jnp.concatenate(behind, axis=0), 0.0),
            )
            share = fixed["mobility"][3 * n, rows, :].astype(F32)
            value = now["near"][n, rows, :] + tx * nx + ty * ny
            terms.append(value - share * perforated[t * STEP : (t + 1) * STEP])
        if kind in ("last", "final"):
            own = mix(extra["diag"], rows, [extra["field"][n, rows, :] for n in range(3)])
            for n in range(3):
                change = own[n] - terms[n]
                before = extra["rhs"][n, rows, :]
                if final:
                    kept = extra["change"][n, rows, :]
                    before = before - omega * kept
                    change = kept + omega * (change - 2.0 * kept)
                else:
                    out["change"][n, rows, :] = change
                numer += before * change
                denom += change * change
        if not final:
            moves = mix(fixed["inverse"], rows, terms)
            values = [fixed["first"][n, rows, :] + moves[n] for n in range(3)]
            forward[rows, :] = values[0]
            if kind == "keep":
                for n in range(3):
                    out["field"][n, rows, :] = values[n]
            borders(values, fixed["mobility"], fixed["trans"], weighted, along, t)

    if kind in ("last", "final"):
        before = source
        change = source - seg_res
        if final:
            kept = extra["seg_change"][...]
            before = source - omega * kept
            change = kept + omega * (change - 2.0 * kept)
        else:
            out["seg_change"][...] = change
        above = jnp.sum(numer, keepdims=True) + jnp.sum(before * change, keepdims=True)
        below = jnp.sum(denom, keepdims=True) + jnp.sum(change * change, keepdims=True)
        place = lanes((PEERS, 128))
        sums = jnp.where(place == 60, above, jnp.where(place == 61, below, 0.0))
        if final:
            out["message"][...] = sums
            return
    else:
        sums = jnp.zeros((PEERS, 128), F32)
    message = out["message"]
    advanced = state + seg_res / diagonal
    out["state"][...] = advanced
    values = segment_values(advanced, number)
    out["at_slots"][...] = values
    cells = slot_values(fixed["rows_of"][...], fixed["start"][...], forward[...])
    out["slots"][...] = cells
    message[block(0), :] = cells
    message[block(1), :] = to_columns(values)
    message[block(2), :] = sums
    message[block(3), :] = jnp.zeros((PEERS, 128), F32)
    if kind == "after":
        out["omega"][...] = jnp.broadcast_to(ratio(arrived[block(2), :], 60), (8, 128))
    interior(
        fixed["trans"], weighted, along, out["near"], out["toward_low"], out["toward_high"],
        message, pad,
    )


def finish(arrived, omega, field_one, field_two, state_one, state_two, cells, segments):
    first = omega[0:1, 0:1]
    second = ratio(arrived[...], 60)

    def blend(one, two):
        kept = first * one
        return kept + second * (one + first * (two - one) - kept)

    for n in range(3):
        for t in range(CHUNKS):
            rows = chunk(t)
            cells[n, rows, :] = blend(field_one[n, rows, :], field_two[n, rows, :])
    segments[...] = blend(state_one[0:2], state_two[0:2])


CELLS = ((3, ROWS, 128), F32)
PAIRS = ((PEERS, 128), F32)
MESSAGE = ((4 * PEERS, 128), F32)
TILE = ((8, 128), F32)
EDGE = ((3 * NZ, 128), F32)
SHAPES = {
    "near": CELLS, "toward_low": EDGE, "toward_high": EDGE, "message": MESSAGE, "slots": PAIRS,
    "at_slots": TILE, "state": TILE, "omega": TILE, "field": CELLS, "change": CELLS,
    "seg_change": TILE,
}
SCRATCH = (
    pltpu.VMEM((3, ROWS + 16, 128), F32),
    pltpu.VMEM((3 * ROWS, 128), F32),
    pltpu.VMEM((16, 128), F32),
)


def call(body, outs, args, scratch=(), name=None):
    moved = sum(a.size * a.dtype.itemsize for a in args)
    return pl.pallas_call(
        body,
        out_shape=[jax.ShapeDtypeStruct(*out) for out in outs],
        in_specs=[pl.BlockSpec(memory_space=pltpu.VMEM)] * len(args),
        out_specs=[pl.BlockSpec(memory_space=pltpu.VMEM)] * len(outs),
        scratch_shapes=list(scratch),
        compiler_params=pltpu.CompilerParams(vmem_limit_bytes=24 * 1024 * 1024),
        cost_estimate=pl.CostEstimate(flops=4_000_000, bytes_accessed=moved, transcendentals=0),
        name=name,
    )(*args)


def exchange(message):
    return lax.all_to_all(message, AXES, split_axis=0, concat_axis=0, tiled=True)


def neighbours(toward_low, toward_high):
    count = lax.axis_size("gx")
    up = [(i, (i + 1) % count) for i in range(count)]
    down = [(b, a) for a, b in up]
    return {
        "from_low": lax.ppermute(toward_high, "gx", up),
        "from_high": lax.ppermute(toward_low, "gx", down),
    }


def on_device(
    rhs, diag_block, mobility, trans, perf_cell, perf_pi, perf_seg, seg_parent, seg_trans, seg_rhs
):
    rhs = rhs.reshape(3, ROWS, 128)
    diag = diag_block.reshape(9, ROWS, 128)
    mobility = mobility.reshape(9, ROWS, 128)
    trans = trans.reshape(3, ROWS, 128)
    index = perf_seg[0]

    fixed = {"mobility": mobility, "trans": trans, "index": index}
    (inverse, first, rows_of, rows_to, start, weight, slots, near, toward_low, toward_high,
     message) = call(
        cell_setup,
        [((9, ROWS, 128), F32), CELLS, ((PEERS, ROWS), BF16), ((ROWS, PEERS), BF16),
         ((PEERS, 128), jnp.int32), PAIRS, PAIRS, CELLS, EDGE, EDGE, MESSAGE],
        [rhs, diag, mobility, trans, perf_cell[0], perf_pi[0]],
        SCRATCH,
        name="cell_setup",
    )
    fixed.update(
        first=first, inverse=inverse, rows_of=rows_of, rows_to=rows_to, start=start, weight=weight
    )
    arrived = exchange(message)
    now = {"arrived": arrived, "near": near, "slots": slots}
    now.update(neighbours(toward_low, toward_high))
    message, own_weight, table, state, at_slots, constants = call(
        well_setup,
        [PAIRS, TILE, ((128, CAP * 128), BF16), TILE, TILE, ((4, 8, 128), F32)],
        [arrived, index, seg_parent.reshape(2, 128), seg_trans.reshape(2, 128),
         seg_rhs.reshape(2, 128)],
        name="well_setup",
    )
    fixed.update(own_weight=own_weight, table=table, fixed=constants)
    now.update(at_slots=at_slots, state=state)
    saved = {"pressures": exchange(message), "diag": diag, "rhs": rhs}

    def advance(kind, now):
        args = [now[name] for name in MOVING]
        args += [fixed[name] for name in STEADY]
        args += [saved[name] for name in MORE_IN[kind]]
        names = results_of(kind)
        out = call(
            functools.partial(sweep, kind),
            [PAIRS if kind == "final" else SHAPES[name] for name in names],
            args,
            SCRATCH + (pltpu.VMEM((ROWS, 128), F32),),
            name="sweep_" + kind,
        )
        out = dict(zip(names, out))
        out["arrived"] = exchange(out.pop("message"))
        if kind != "final":
            out.update(neighbours(out.pop("toward_low"), out.pop("toward_high")))
        return out

    now = advance("first", now)
    now = advance("plain", now)
    one = advance("keep", now)
    saved["field"] = one["field"]
    now = advance("last", one)
    saved.update(change=now["change"], seg_change=now["seg_change"])
    now = advance("after", now)
    saved["omega"] = now["omega"]
    now = advance("plain", now)
    two = advance("keep", now)
    saved["field"] = two["field"]
    sums = advance("final", two)
    cells, segments = call(
        finish,
        [CELLS, ((2, 128), F32)],
        [sums["arrived"], saved["omega"], one["field"], two["field"], one["state"], two["state"]],
        name="finish",
    )
    return cells.reshape(3, NZ, CX, CY), segments.reshape(256)


def solution(mesh):
    grid = P(None, None, "gx", "gy")
    pairs = P(AXES, None, None)
    flat = P(AXES)
    return jax.shard_map(
        on_device,
        mesh=mesh,
        in_specs=(grid, grid, grid, grid, pairs, pairs, pairs, flat, flat, flat),
        out_specs=(grid, flat),
        check_vma=False,
    )
```

```python
import functools

import jax
import jax.numpy as jnp
from jax import lax
from jax.experimental import pallas as pl
from jax.experimental.pallas import tpu as pltpu
from jax.sharding import PartitionSpec as P

F32 = jnp.float32
BF16 = jnp.bfloat16
AXES = ("gx", "gy")
NZ, CX, CY = 20, 8, 128
ROWS = NZ * CX
STEP = 16
CHUNKS = ROWS // STEP
PEERS = 128
CAP = 8


def lanes(shape):
    return lax.broadcasted_iota(jnp.int32, shape, 1)


def subs(shape):
    return lax.broadcasted_iota(jnp.int32, shape, 0)


def split3(x):
    high = x.astype(BF16)
    rest = x - high.astype(F32)
    mid = rest.astype(BF16)
    low = (rest - mid.astype(F32)).astype(BF16)
    return high, mid, low


def pick_rows(onehot, x):
    high, mid, low = split3(x)

    def dot(part):
        return lax.dot_general(onehot, part, (((1,), (0,)), ((), ())), preferred_element_type=F32)

    return (dot(low) + dot(mid)) + dot(high)


def is_slot(lane):
    return (lane & 63) >= 60


def slot_values(rows_of, start, first):
    lane = lanes((PEERS, CY))
    number = (lane & 3) + jnp.where(lane >= 64, 4, 0)
    picked = pick_rows(rows_of, first)
    window = jnp.take_along_axis(picked, (start + number) & (CY - 1), axis=1)
    return jnp.where(is_slot(lane), window, 0.0)


def into_cells(rows_to, start, flows):
    number = (lanes((PEERS, CY)) - start) & (CY - 1)
    place = jnp.where(number < 4, number + 60, jnp.where(number < CAP, number + 120, 0))
    return pick_rows(rows_to, jnp.take_along_axis(flows, place, axis=1))


def segment_values(state, index):
    low = index & 127
    first = jnp.take_along_axis(jnp.broadcast_to(state[0:1], (8, 128)), low, axis=1)
    second = jnp.take_along_axis(jnp.broadcast_to(state[1:2], (8, 128)), low, axis=1)
    return jnp.where(index >= 128, second, first)


def into_segments(values, index, table):
    parts = [part.astype(F32) for part in split3(values)]
    sub = subs((16, 128))
    upper = (index >= 128).astype(jnp.int32)
    tiles = []
    for k in range(CAP):
        row = [jnp.broadcast_to(part[k : k + 1], (16, 128)) for part in parts]
        mine = jnp.broadcast_to(upper[k : k + 1], (16, 128)) == (sub & 1)
        tile = jnp.where(sub < 2, row[0], jnp.where(sub < 4, row[1], row[2]))
        tiles.append(jnp.where(mine & (sub < 6), tile, 0.0).astype(BF16))
    left = jnp.concatenate(tiles, axis=1)
    out = lax.dot_general(left, table, (((1,), (1,)), ((), ())), preferred_element_type=F32)[:8]
    total = (pltpu.roll(out, 4, 0) + pltpu.roll(out, 6, 0)) + out
    return jnp.where(subs((8, 128)) < 2, total, 0.0)


def previous(state):
    moved = pltpu.roll(state, 1, 1)
    return jnp.where(lanes((8, 128)) == 0, pltpu.roll(moved, 1, 0), moved)


def following(state):
    moved = pltpu.roll(state, 127, 1)
    return jnp.where(lanes((8, 128)) == 127, pltpu.roll(moved, 7, 0), moved)


def to_columns(values):
    gap = jnp.zeros((60, 128), F32)
    return jnp.concatenate([gap, values[0:4], gap, values[4:8]], axis=0).T


def to_rows(columns):
    turned = columns.T
    return jnp.concatenate([turned[60:64], turned[124:128]], axis=0)


def block(n):
    return pl.ds(n, PEERS, stride=4)


def chunk(t):
    return pl.ds(t * STEP, STEP)


def me():
    return lax.axis_index("gx") * 16 + lax.axis_index("gy")


def peer_rows(shift):
    return pl.ds(4 * ((me() + shift) & (PEERS - 1)), 4)


def tile_to_rows(tile, pad):
    pad[0:8] = tile
    pad[8:16] = pltpu.roll(tile, 64, 1)
    even = pad[pl.ds(0, 4, stride=2), :]
    odd = pad[pl.ds(9, 4, stride=2), :]
    return jnp.where(lanes((4, 128)) < 64, even, odd)


def rows_to_tile(four, pad):
    pad[0:4] = four
    pad[8:16] = pltpu.roll(pad[0:8], 64, 1)
    low, high = pad[0:4], pad[8:12]
    pad[pl.ds(0, 4, stride=2), :] = low
    pad[pl.ds(1, 4, stride=2), :] = high
    return pad[0:8]


def mix(matrix, rows, vector):
    entry = [matrix[n, rows, :].astype(F32) for n in range(9)]
    x, y, z = vector
    return [entry[3 * n] * x + entry[3 * n + 1] * y + entry[3 * n + 2] * z for n in range(3)]


def solve(diag, rows, vector):
    a, b, c, d, e, f, g, h, i = [diag[n, rows, :].astype(F32) for n in range(9)]
    x, y, z = vector
    p, q, s = e * i - f * h, f * g - d * i, d * h - e * g
    scale = 1.0 / (a * p + b * q + c * s)
    return [
        (p * x + (c * h - b * i) * y + (b * f - c * e) * z) * scale,
        (q * x + (a * i - c * g) * y + (c * d - a * f) * z) * scale,
        (s * x + (b * g - a * h) * y + (a * e - b * d) * z) * scale,
    ]


def borders(values, mobility, trans, weighted, along, t):
    rows = chunk(t)
    tx = trans[0, rows, :].astype(F32)
    for n, value in enumerate(mix(mobility, rows, values)):
        weighted[n, pl.ds(8 + t * STEP, STEP), :] = value
        along[pl.ds(n * ROWS + t * STEP, STEP), :] = tx * value


def interior(trans, weighted, along, near, toward_low, toward_high, message, pad):
    toward_low[...] = along[pl.ds(0, 3 * NZ, stride=CX), :]
    toward_high[...] = along[pl.ds(CX - 1, 3 * NZ, stride=CX), :]
    lane = lanes((STEP, 128))
    sub = subs((STEP, 128)) & 7
    small = lanes((8, 128))
    high = jnp.zeros((8, 128), F32)
    low = jnp.zeros((8, 128), F32)
    for n in range(3):
        weighted[n, 0:8, :] = jnp.zeros((8, 128), F32)
        weighted[n, ROWS + 8 : ROWS + 16, :] = jnp.zeros((8, 128), F32)
    up = [trans[2, chunk(t), :].astype(F32) for t in range(CHUNKS)]
    for t in range(CHUNKS):
        rows = chunk(t)
        tx, ty = [trans[n, rows, :].astype(F32) for n in range(2)]
        tz = up[t]
        zero = jnp.zeros((8, 128), F32)
        below = jnp.concatenate([up[t - 1][8:16] if t else zero, tz[0:8]], axis=0)
        above = jnp.concatenate([tz[8:16], up[t + 1][0:8] if t + 1 < CHUNKS else zero], axis=0)
        for n in range(3):
            px = along[pl.ds(n * ROWS + t * STEP, STEP), :]
            py = ty * weighted[n, pl.ds(8 + t * STEP, STEP), :]
            nx = jnp.where(sub == 0, 0.0, pltpu.roll(px, 1, 0)) + jnp.where(
                sub == 7, 0.0, pltpu.roll(px, STEP - 1, 0)
            )
            ny = jnp.where(lane == 0, 0.0, pltpu.roll(py, 1, 1)) + jnp.where(
                lane == 127, 0.0, pltpu.roll(py, 127, 1)
            )
            nz = below * weighted[n, pl.ds(t * STEP, STEP), :] + above * weighted[
                n, pl.ds(t * STEP + 16, STEP), :
            ]
            near[n, rows, :] = tx * nx + ty * ny + tz * nz
            for half in range(2):
                j = n * NZ + 2 * t + half
                moved = pltpu.roll(py[8 * half : 8 * half + 8], j + 1, 1)
                high = jnp.where(small == j, moved, high)
                low = jnp.where(small == j + 1, moved, low)
    low = pltpu.roll(low, 127, 1)
    mine = is_slot(lanes((4, 128)))
    for shift, tile in ((1, high), (-1, low)):
        rows = peer_rows(shift)
        packed = tile_to_rows(tile, pad)
        message[rows, :] = jnp.where(mine, message[rows, :], packed)


def cell_setup(rhs_in, diag_in, mobility_in, trans_in, cells_in, pi_in,
               rows_of, rows_to, start, weight, slots,
               near, toward_low, toward_high, message, weighted, along, pad, forward,
               rhs, diag, mobility, trans, cells, pi, sems):
    pairs = ((rhs_in, rhs), (diag_in, diag), (cells_in, cells), (pi_in, pi),
             (mobility_in, mobility), (trans_in, trans))
    copies = [pltpu.make_async_copy(a, b, sems.at[n]) for n, (a, b) in enumerate(pairs)]
    for copy in copies:
        copy.start()
    for copy in copies:
        copy.wait()
    for t in range(CHUNKS):
        rows = chunk(t)
        values = solve(diag, rows, [rhs[n, rows, :] for n in range(3)])
        forward[rows, :] = values[0]
        borders(values, mobility, trans, weighted, along, t)
    base = cells[0:1, :]
    row = lax.shift_right_logical(base, 7)
    live = pi[...]
    gap = jnp.zeros((44, 128), F32)
    info = jnp.concatenate(
        [jnp.broadcast_to(row.astype(F32), (8, 128)),
         jnp.broadcast_to((base & 127).astype(F32), (8, 128)),
         gap, live[0:4], gap, jnp.zeros((16, 128), F32), live[4:8]],
        axis=0,
    ).T
    rows_to[...] = (subs((ROWS, PEERS)) == jnp.broadcast_to(row, (ROWS, PEERS))).astype(F32).astype(BF16)
    row_column = jnp.broadcast_to(info[:, 0:1], (PEERS, ROWS)).astype(jnp.int32)
    rows_of[...] = (lanes((PEERS, ROWS)) == row_column).astype(F32).astype(BF16)
    begin = jnp.broadcast_to(info[:, 8:9], (PEERS, 128)).astype(jnp.int32)
    start[...] = begin
    weights = jnp.where(is_slot(lanes((PEERS, 128))), info, 0.0)
    weight[...] = weights
    values = slot_values(rows_of[...], begin, forward[...])
    slots[...] = values
    message[block(0), :] = values
    message[block(1), :] = weights
    message[block(2), :] = jnp.zeros((PEERS, 128), F32)
    message[block(3), :] = jnp.zeros((PEERS, 128), F32)
    interior(trans, weighted, along, near, toward_low, toward_high, message, pad)


def well_tables(index, parent, trans, rhs, table, fixed):
    low = index[...] & 127
    for k in range(CAP):
        hit = subs((128, 128)) == jnp.broadcast_to(low[k : k + 1], (128, 128))
        table[:, 128 * k : 128 * (k + 1)] = hit.astype(F32).astype(BF16)
    zeros = jnp.zeros((6, 128), F32)
    linked = jnp.concatenate([(parent[...] >= 0).astype(F32), zeros], axis=0)
    across = jnp.concatenate([trans[...], zeros], axis=0)
    fixed[0] = linked
    fixed[1] = across
    fixed[2] = jnp.concatenate([rhs[...], zeros], axis=0)
    fixed[3] = across + following(linked * across)


def well_setup(arrived, index, table, fixed, message, weight, state, at_slots, diagonal):
    pi = to_rows(arrived[block(1), :])
    weight[...] = pi
    number = index[...]
    total = fixed[3] + into_segments(pi, number, table[...])
    total = jnp.where(subs((8, 128)) < 2, total, 1.0)
    diagonal[...] = total
    now = fixed[2] / total
    state[...] = now
    values = segment_values(now, number)
    at_slots[...] = values
    message[...] = to_columns(values)


def ratio(sums, place):
    total = jnp.sum(sums, axis=0, keepdims=True)
    lane = lanes((1, 128))
    numer = jnp.sum(jnp.where(lane == place, total, 0.0), axis=1, keepdims=True)
    denom = jnp.sum(jnp.where(lane == place + 1, total, 0.0), axis=1, keepdims=True)
    return numer / denom


def spread_pair(two):
    return jnp.concatenate(
        [jnp.broadcast_to(two[h : h + 1], (8, 128)) for h in range(2)], axis=0
    )


STEADY = ("rhs", "diag", "mobility", "trans", "rows_of", "rows_to", "start", "weight",
          "own_weight", "table", "index", "fixed", "diagonal")
MOVING = ("arrived", "near", "from_low", "from_high", "slots", "at_slots", "state")
NEXT = ("near", "toward_low", "toward_high", "message", "slots", "at_slots", "state")
MORE_IN = {
    "first": ("pressures",), "plain": (), "keep": (), "last": ("field",), "after": (),
    "final": ("field", "change", "seg_change", "omega"),
}
MORE_OUT = {
    "first": (), "plain": (), "keep": ("field",), "last": ("change", "seg_change"),
    "after": ("omega",), "final": (),
}


def results_of(kind):
    return ("message",) if kind == "final" else NEXT + MORE_OUT[kind]


def sweep(kind, *refs):
    take = iter(refs)
    now = {name: next(take) for name in MOVING}
    fixed = {name: next(take) for name in STEADY}
    extra = {name: next(take) for name in MORE_IN[kind]}
    out = {name: next(take) for name in results_of(kind)}
    weighted, along, pad, forward = take
    final = kind == "final"
    gx, gy = lax.axis_index("gx"), lax.axis_index("gy")

    arrived = now["arrived"]
    pressures = extra["pressures"][...] if kind == "first" else arrived[block(1), :]
    pull = fixed["weight"][...] * (now["slots"][...] - pressures)
    perforated = into_cells(fixed["rows_to"][...], fixed["start"][...], pull)

    side_low = rows_to_tile(arrived[peer_rows(-1), :], pad)
    side_high = rows_to_tile(arrived[peer_rows(1), :], pad)
    side_low = jnp.where(gy == 0, 0.0, side_low)
    side_high = jnp.where(gy == lax.axis_size("gy") - 1, 0.0, side_high)
    open_low, open_high = gx > 0, gx < lax.axis_size("gx") - 1

    state = now["state"][...]
    linked, across, source = [fixed["fixed"][n] for n in range(3)]
    push = fixed["own_weight"][...] * (to_rows(arrived[block(0), :]) - now["at_slots"][...])
    number = fixed["index"][...]
    inflow = into_segments(push, number, fixed["table"][...])
    flux = across * (state - linked * previous(state))
    seg_res = source - flux + following(linked * flux) + inflow

    lane = lanes((STEP, 128))
    sub = subs((STEP, 128)) & 7
    numer = jnp.zeros((STEP, 128), F32)
    denom = jnp.zeros((STEP, 128), F32)
    if final:
        omega = extra["omega"][0:1, 0:1]
    for t in range(CHUNKS):
        rows = chunk(t)
        tx, ty = [fixed["trans"][n, rows, :].astype(F32) for n in range(2)]
        terms = []
        for n in range(3):
            j = n * NZ + 2 * t
            low = jnp.where(open_low, now["from_low"][j : j + 2, :], 0.0)
            high = jnp.where(open_high, now["from_high"][j : j + 2, :], 0.0)
            nx = jnp.where(sub == 0, spread_pair(low), jnp.where(sub == 7, spread_pair(high), 0.0))
            before = [pltpu.roll(side_low, (128 - j - h) % 128, 1) for h in range(2)]
            behind = [pltpu.roll(side_high, 127 - j - h, 1) for h in range(2)]
            ny = jnp.where(
                lane == 0, jnp.concatenate(before, axis=0),
                jnp.where(lane == 127, jnp.concatenate(behind, axis=0), 0.0),
            )
            share = fixed["mobility"][3 * n, rows, :].astype(F32)
            value = now["near"][n, rows, :] + tx * nx + ty * ny
            terms.append(value - share * perforated[t * STEP : (t + 1) * STEP])
        if kind in ("last", "final"):
            own = mix(fixed["diag"], rows, [extra["field"][n, rows, :] for n in range(3)])
            for n in range(3):
                change = own[n] - terms[n]
                before = fixed["rhs"][n, rows, :]
                if final:
                    kept = extra["change"][n, rows, :]
                    before = before - omega * kept
                    change = kept + omega * (change - 2.0 * kept)
                else:
                    out["change"][n, rows, :] = change
                numer += before * change
                denom += change * change
        if not final:
            total = [fixed["rhs"][n, rows, :] + terms[n] for n in range(3)]
            values = solve(fixed["diag"], rows, total)
            forward[rows, :] = values[0]
            if kind == "keep":
                for n in range(3):
                    out["field"][n, rows, :] = values[n]
            borders(values, fixed["mobility"], fixed["trans"], weighted, along, t)

    if kind in ("last", "final"):
        before = source
        change = source - seg_res
        if final:
            kept = extra["seg_change"][...]
            before = source - omega * kept
            change = kept + omega * (change - 2.0 * kept)
        else:
            out["seg_change"][...] = change
        above = jnp.sum(numer, keepdims=True) + jnp.sum(before * change, keepdims=True)
        below = jnp.sum(denom, keepdims=True) + jnp.sum(change * change, keepdims=True)
        place = lanes((PEERS, 128))
        sums = jnp.where(place == 60, above, jnp.where(place == 61, below, 0.0))
        if final:
            out["message"][...] = sums
            return
    else:
        sums = jnp.zeros((PEERS, 128), F32)
    message = out["message"]
    advanced = state + seg_res / fixed["diagonal"][...]
    out["state"][...] = advanced
    values = segment_values(advanced, number)
    out["at_slots"][...] = values
    cells = slot_values(fixed["rows_of"][...], fixed["start"][...], forward[...])
    out["slots"][...] = cells
    message[block(0), :] = cells
    message[block(1), :] = to_columns(values)
    message[block(2), :] = sums
    message[block(3), :] = jnp.zeros((PEERS, 128), F32)
    if kind == "after":
        out["omega"][...] = jnp.broadcast_to(ratio(arrived[block(2), :], 60), (8, 128))
    interior(
        fixed["trans"], weighted, along, out["near"], out["toward_low"], out["toward_high"],
        message, pad,
    )


def finish(arrived, omega, field_one, field_two, state_one, state_two, cells, segments):
    first = omega[0:1, 0:1]
    second = ratio(arrived[...], 60)

    def blend(one, two):
        kept = first * one
        return kept + second * (one + first * (two - one) - kept)

    for n in range(3):
        for t in range(CHUNKS):
            rows = chunk(t)
            cells[n, rows, :] = blend(field_one[n, rows, :], field_two[n, rows, :])
    segments[...] = blend(state_one[0:2], state_two[0:2])


CELLS = ((3, ROWS, 128), F32)
PAIRS = ((PEERS, 128), F32)
MESSAGE = ((4 * PEERS, 128), F32)
TILE = ((8, 128), F32)
EDGE = ((3 * NZ, 128), F32)
SHAPES = {
    "near": CELLS, "toward_low": EDGE, "toward_high": EDGE, "message": MESSAGE, "slots": PAIRS,
    "at_slots": TILE, "state": TILE, "omega": TILE, "field": CELLS, "change": CELLS,
    "seg_change": TILE,
}
SCRATCH = (
    pltpu.VMEM((3, ROWS + 16, 128), F32),
    pltpu.VMEM((3 * ROWS, 128), F32),
    pltpu.VMEM((16, 128), F32),
    pltpu.VMEM((ROWS, 128), F32),
)


def call(body, outs, args, scratch=(), name=None, space=pltpu.VMEM):
    moved = sum(a.size * a.dtype.itemsize for a in args)
    return pl.pallas_call(
        body,
        out_shape=[jax.ShapeDtypeStruct(*out) for out in outs],
        in_specs=[pl.BlockSpec(memory_space=space)] * len(args),
        out_specs=[pl.BlockSpec(memory_space=pltpu.VMEM)] * len(outs),
        scratch_shapes=list(scratch),
        compiler_params=pltpu.CompilerParams(vmem_limit_bytes=24 * 1024 * 1024),
        cost_estimate=pl.CostEstimate(flops=4_000_000, bytes_accessed=moved, transcendentals=0),
        name=name,
    )(*args)


def exchange(message):
    return lax.all_to_all(message, AXES, split_axis=0, concat_axis=0, tiled=True)


def neighbours(toward_low, toward_high):
    count = lax.axis_size("gx")
    up = [(i, (i + 1) % count) for i in range(count)]
    down = [(b, a) for a, b in up]
    return {
        "from_low": lax.ppermute(toward_high, "gx", up),
        "from_high": lax.ppermute(toward_low, "gx", down),
    }


def on_device(
    rhs, diag_block, mobility, trans, perf_cell, perf_pi, perf_seg, seg_parent, seg_trans, seg_rhs
):
    rhs = rhs.reshape(3, ROWS, 128)
    diag = diag_block.reshape(9, ROWS, 128)
    mobility = mobility.reshape(9, ROWS, 128)
    trans = trans.reshape(3, ROWS, 128)
    index = perf_seg[0]

    fixed = {"rhs": rhs, "diag": diag, "mobility": mobility, "trans": trans, "index": index}
    inputs = [rhs, diag, mobility, trans, perf_cell[0], perf_pi[0]]
    (rows_of, rows_to, start, weight, slots, near, toward_low, toward_high, message) = call(
        cell_setup,
        [((PEERS, ROWS), BF16), ((ROWS, PEERS), BF16),
         ((PEERS, 128), jnp.int32), PAIRS, PAIRS, CELLS, EDGE, EDGE, MESSAGE],
        inputs,
        SCRATCH + tuple(pltpu.VMEM(a.shape, a.dtype) for a in inputs)
        + (pltpu.SemaphoreType.DMA((6,)),),
        name="cell_setup",
        space=pltpu.HBM,
    )
    arrived = exchange(message)
    table, constants = call(
        well_tables,
        [((128, CAP * 128), BF16), ((4, 8, 128), F32)],
        [index, seg_parent.reshape(2, 128), seg_trans.reshape(2, 128), seg_rhs.reshape(2, 128)],
        name="well_tables",
    )
    fixed.update(rows_of=rows_of, rows_to=rows_to, start=start, weight=weight)
    now = {"arrived": arrived, "near": near, "slots": slots}
    now.update(neighbours(toward_low, toward_high))
    message, own_weight, state, at_slots, diagonal = call(
        well_setup,
        [PAIRS, TILE, TILE, TILE, TILE],
        [arrived, index, table, constants],
        name="well_setup",
    )
    fixed.update(own_weight=own_weight, table=table, fixed=constants, diagonal=diagonal)
    now.update(at_slots=at_slots, state=state)
    saved = {"pressures": exchange(message)}

    def advance(kind, now):
        args = [now[name] for name in MOVING]
        args += [fixed[name] for name in STEADY]
        args += [saved[name] for name in MORE_IN[kind]]
        names = results_of(kind)
        out = call(
            functools.partial(sweep, kind),
            [PAIRS if kind == "final" else SHAPES[name] for name in names],
            args,
            SCRATCH,
            name="sweep_" + kind,
        )
        out = dict(zip(names, out))
        out["arrived"] = exchange(out.pop("message"))
        if kind != "final":
            out.update(neighbours(out.pop("toward_low"), out.pop("toward_high")))
        return out

    now = advance("first", now)
    now = advance("plain", now)
    one = advance("keep", now)
    saved["field"] = one["field"]
    now = advance("last", one)
    saved.update(change=now["change"], seg_change=now["seg_change"])
    now = advance("after", now)
    saved["omega"] = now["omega"]
    now = advance("plain", now)
    two = advance("keep", now)
    saved["field"] = two["field"]
    sums = advance("final", two)
    cells, segments = call(
        finish,
        [CELLS, ((2, 128), F32)],
        [sums["arrived"], saved["omega"], one["field"], two["field"], one["state"], two["state"]],
        name="finish",
    )
    return cells.reshape(3, NZ, CX, CY), segments.reshape(256)


def solution(mesh):
    grid = P(None, None, "gx", "gy")
    pairs = P(AXES, None, None)
    flat = P(AXES)
    return jax.shard_map(
        on_device,
        mesh=mesh,
        in_specs=(grid, grid, grid, grid, pairs, pairs, pairs, flat, flat, flat),
        out_specs=(grid, flat),
        check_vma=False,
    )
```

```python
import functools

import jax
import jax.numpy as jnp
from jax import lax
from jax.experimental import pallas as pl
from jax.experimental.pallas import tpu as pltpu
from jax.sharding import PartitionSpec as P

F32 = jnp.float32
BF16 = jnp.bfloat16
AXES = ("gx", "gy")
NZ, CX, CY = 20, 8, 128
ROWS = NZ * CX
STEP = 16
CHUNKS = ROWS // STEP
PEERS = 128
CAP = 8


def lanes(shape):
    return lax.broadcasted_iota(jnp.int32, shape, 1)


def subs(shape):
    return lax.broadcasted_iota(jnp.int32, shape, 0)


def split3(x):
    high = x.astype(BF16)
    rest = x - high.astype(F32)
    mid = rest.astype(BF16)
    low = (rest - mid.astype(F32)).astype(BF16)
    return high, mid, low


def pick_rows(onehot, x):
    high, mid, low = split3(x)

    def dot(part):
        return lax.dot_general(onehot, part, (((1,), (0,)), ((), ())), preferred_element_type=F32)

    return (dot(low) + dot(mid)) + dot(high)


def is_slot(lane):
    return (lane & 63) >= 60


def slot_values(rows_of, start, first):
    lane = lanes((PEERS, CY))
    number = (lane & 3) + jnp.where(lane >= 64, 4, 0)
    picked = pick_rows(rows_of, first)
    window = jnp.take_along_axis(picked, (start + number) & (CY - 1), axis=1)
    return jnp.where(is_slot(lane), window, 0.0)


def into_cells(rows_to, start, flows):
    number = (lanes((PEERS, CY)) - start) & (CY - 1)
    place = jnp.where(number < 4, number + 60, jnp.where(number < CAP, number + 120, 0))
    return pick_rows(rows_to, jnp.take_along_axis(flows, place, axis=1))


def segment_values(state, index):
    low = index & 127
    first = jnp.take_along_axis(jnp.broadcast_to(state[0:1], (8, 128)), low, axis=1)
    second = jnp.take_along_axis(jnp.broadcast_to(state[1:2], (8, 128)), low, axis=1)
    return jnp.where(index >= 128, second, first)


def into_segments(values, index, table):
    parts = [part.astype(F32) for part in split3(values)]
    sub = subs((16, 128))
    upper = (index >= 128).astype(jnp.int32)
    tiles = []
    for k in range(CAP):
        row = [jnp.broadcast_to(part[k : k + 1], (16, 128)) for part in parts]
        mine = jnp.broadcast_to(upper[k : k + 1], (16, 128)) == (sub & 1)
        tile = jnp.where(sub < 2, row[0], jnp.where(sub < 4, row[1], row[2]))
        tiles.append(jnp.where(mine & (sub < 6), tile, 0.0).astype(BF16))
    left = jnp.concatenate(tiles, axis=1)
    out = lax.dot_general(left, table, (((1,), (1,)), ((), ())), preferred_element_type=F32)[:8]
    total = (pltpu.roll(out, 4, 0) + pltpu.roll(out, 6, 0)) + out
    return jnp.where(subs((8, 128)) < 2, total, 0.0)


def previous(state):
    moved = pltpu.roll(state, 1, 1)
    return jnp.where(lanes((8, 128)) == 0, pltpu.roll(moved, 1, 0), moved)


def following(state):
    moved = pltpu.roll(state, 127, 1)
    return jnp.where(lanes((8, 128)) == 127, pltpu.roll(moved, 7, 0), moved)


def to_columns(values):
    gap = jnp.zeros((60, 128), F32)
    return jnp.concatenate([gap, values[0:4], gap, values[4:8]], axis=0).T


def to_rows(columns):
    turned = columns.T
    return jnp.concatenate([turned[60:64], turned[124:128]], axis=0)


def block(n):
    return pl.ds(n, PEERS, stride=4)


def chunk(t):
    return pl.ds(t * STEP, STEP)


def me():
    return lax.axis_index("gx") * 16 + lax.axis_index("gy")


def peer_rows(shift):
    return pl.ds(4 * ((me() + shift) & (PEERS - 1)), 4)


def tile_to_rows(tile, pad):
    pad[0:8] = tile
    pad[8:16] = pltpu.roll(tile, 64, 1)
    even = pad[pl.ds(0, 4, stride=2), :]
    odd = pad[pl.ds(9, 4, stride=2), :]
    return jnp.where(lanes((4, 128)) < 64, even, odd)


def rows_to_tile(four, pad):
    pad[0:4] = four
    pad[8:16] = pltpu.roll(pad[0:8], 64, 1)
    low, high = pad[0:4], pad[8:12]
    pad[pl.ds(0, 4, stride=2), :] = low
    pad[pl.ds(1, 4, stride=2), :] = high
    return pad[0:8]


def mix(matrix, rows, vector):
    entry = [matrix[n, rows, :].astype(F32) for n in range(9)]
    x, y, z = vector
    return [entry[3 * n] * x + entry[3 * n + 1] * y + entry[3 * n + 2] * z for n in range(3)]


def solve(diag, rows, vector):
    a, b, c, d, e, f, g, h, i = [diag[n, rows, :].astype(F32) for n in range(9)]
    x, y, z = vector
    p, q, s = e * i - f * h, f * g - d * i, d * h - e * g
    scale = 1.0 / (a * p + b * q + c * s)
    return [
        (p * x + (c * h - b * i) * y + (b * f - c * e) * z) * scale,
        (q * x + (a * i - c * g) * y + (c * d - a * f) * z) * scale,
        (s * x + (b * g - a * h) * y + (a * e - b * d) * z) * scale,
    ]


def borders(values, mobility, trans, weighted, along, t):
    rows = chunk(t)
    tx = trans[0, rows, :].astype(F32)
    for n, value in enumerate(mix(mobility, rows, values)):
        weighted[n, rows, :] = value
        along[pl.ds(n * ROWS + t * STEP, STEP), :] = tx * value


def send_borders(trans, weighted, along, toward_low, toward_high, message, pad):
    toward_low[...] = along[pl.ds(0, 3 * NZ, stride=CX), :]
    toward_high[...] = along[pl.ds(CX - 1, 3 * NZ, stride=CX), :]
    small = lanes((8, 128))
    high = jnp.zeros((8, 128), F32)
    low = jnp.zeros((8, 128), F32)
    for t in range(CHUNKS):
        ty = trans[1, chunk(t), :].astype(F32)
        for n in range(3):
            py = ty * weighted[n, chunk(t), :]
            for half in range(2):
                j = n * NZ + 2 * t + half
                moved = pltpu.roll(py[8 * half : 8 * half + 8], j + 1, 1)
                high = jnp.where(small == j, moved, high)
                low = jnp.where(small == j + 1, moved, low)
    low = pltpu.roll(low, 127, 1)
    mine = is_slot(lanes((4, 128)))
    for shift, tile in ((1, high), (-1, low)):
        rows = peer_rows(shift)
        packed = tile_to_rows(tile, pad)
        message[rows, :] = jnp.where(mine, message[rows, :], packed)


def interior(weighted, trans, near):
    lane = lanes((STEP, 128))
    sub = subs((STEP, 128)) & 7
    zero = jnp.zeros((8, 128), F32)
    up = [trans[2, chunk(t), :].astype(F32) for t in range(CHUNKS)]
    for t in range(CHUNKS):
        rows = chunk(t)
        tx, ty = [trans[n, rows, :].astype(F32) for n in range(2)]
        tz = up[t]
        for n in range(3):
            value = weighted[n, rows, :]
            px, py = tx * value, ty * value
            nx = jnp.where(sub == 0, 0.0, pltpu.roll(px, 1, 0)) + jnp.where(
                sub == 7, 0.0, pltpu.roll(px, STEP - 1, 0)
            )
            ny = jnp.where(lane == 0, 0.0, pltpu.roll(py, 1, 1)) + jnp.where(
                lane == 127, 0.0, pltpu.roll(py, 127, 1)
            )
            pz = tz * value
            below = zero
            above = zero
            if t:
                below = up[t - 1][8:16] * weighted[n, pl.ds(t * STEP - 8, 8), :]
            if t + 1 < CHUNKS:
                above = up[t + 1][0:8] * weighted[n, pl.ds(t * STEP + STEP, 8), :]
            nz = jnp.concatenate([below + pz[8:16], pz[0:8] + above], axis=0)
            near[n, rows, :] = tx * nx + ty * ny + tz * nz


def cell_setup(rhs_in, diag_in, mobility_in, trans_in, cells_in, pi_in,
               rows_of, rows_to, start, weight, slots,
               weighted, toward_low, toward_high, message, along, pad, forward,
               rhs, diag, mobility, trans, cells, pi, sems):
    pairs = ((rhs_in, rhs), (diag_in, diag), (cells_in, cells), (pi_in, pi),
             (mobility_in, mobility), (trans_in, trans))
    copies = [pltpu.make_async_copy(a, b, sems.at[n]) for n, (a, b) in enumerate(pairs)]
    for copy in copies:
        copy.start()
    for copy in copies:
        copy.wait()
    for t in range(CHUNKS):
        rows = chunk(t)
        values = solve(diag, rows, [rhs[n, rows, :] for n in range(3)])
        forward[rows, :] = values[0]
        borders(values, mobility, trans, weighted, along, t)
    base = cells[0:1, :]
    row = lax.shift_right_logical(base, 7)
    live = pi[...]
    gap = jnp.zeros((44, 128), F32)
    info = jnp.concatenate(
        [jnp.broadcast_to(row.astype(F32), (8, 128)),
         jnp.broadcast_to((base & 127).astype(F32), (8, 128)),
         gap, live[0:4], gap, jnp.zeros((16, 128), F32), live[4:8]],
        axis=0,
    ).T
    rows_to[...] = (subs((ROWS, PEERS)) == jnp.broadcast_to(row, (ROWS, PEERS))).astype(F32).astype(BF16)
    row_column = jnp.broadcast_to(info[:, 0:1], (PEERS, ROWS)).astype(jnp.int32)
    rows_of[...] = (lanes((PEERS, ROWS)) == row_column).astype(F32).astype(BF16)
    begin = jnp.broadcast_to(info[:, 8:9], (PEERS, 128)).astype(jnp.int32)
    start[...] = begin
    weights = jnp.where(is_slot(lanes((PEERS, 128))), info, 0.0)
    weight[...] = weights
    values = slot_values(rows_of[...], begin, forward[...])
    slots[...] = values
    message[block(0), :] = values
    message[block(1), :] = weights
    message[block(2), :] = jnp.zeros((PEERS, 128), F32)
    message[block(3), :] = jnp.zeros((PEERS, 128), F32)
    send_borders(trans, weighted, along, toward_low, toward_high, message, pad)


def well_tables(index, parent, trans, rhs, table, fixed):
    low = index[...] & 127
    for k in range(CAP):
        hit = subs((128, 128)) == jnp.broadcast_to(low[k : k + 1], (128, 128))
        table[:, 128 * k : 128 * (k + 1)] = hit.astype(F32).astype(BF16)
    zeros = jnp.zeros((6, 128), F32)
    linked = jnp.concatenate([(parent[...] >= 0).astype(F32), zeros], axis=0)
    across = jnp.concatenate([trans[...], zeros], axis=0)
    fixed[0] = linked
    fixed[1] = across
    fixed[2] = jnp.concatenate([rhs[...], zeros], axis=0)
    fixed[3] = across + following(linked * across)


def well_setup(arrived, index, table, fixed, message, weight, state, at_slots, diagonal):
    pi = to_rows(arrived[block(1), :])
    weight[...] = pi
    number = index[...]
    total = fixed[3] + into_segments(pi, number, table[...])
    total = jnp.where(subs((8, 128)) < 2, total, 1.0)
    diagonal[...] = total
    now = fixed[2] / total
    state[...] = now
    values = segment_values(now, number)
    at_slots[...] = values
    message[...] = to_columns(values)


def ratio(sums, place):
    total = jnp.sum(sums, axis=0, keepdims=True)
    lane = lanes((1, 128))
    numer = jnp.sum(jnp.where(lane == place, total, 0.0), axis=1, keepdims=True)
    denom = jnp.sum(jnp.where(lane == place + 1, total, 0.0), axis=1, keepdims=True)
    return numer / denom


def spread_pair(two):
    return jnp.concatenate(
        [jnp.broadcast_to(two[h : h + 1], (8, 128)) for h in range(2)], axis=0
    )


STEADY = ("rhs", "diag", "mobility", "trans", "rows_of", "rows_to", "start", "weight",
          "own_weight", "table", "index", "fixed", "diagonal")
MOVING = ("arrived", "near", "from_low", "from_high", "slots", "at_slots", "state")
NEXT = ("weighted", "toward_low", "toward_high", "message", "slots", "at_slots", "state")
MORE_IN = {
    "first": ("pressures",), "plain": (), "keep": (), "last": ("field",), "after": (),
    "final": ("field", "change", "seg_change", "omega"),
}
MORE_OUT = {
    "first": (), "plain": (), "keep": ("field",), "last": ("change", "seg_change"),
    "after": ("omega",), "final": (),
}


def results_of(kind):
    return ("message",) if kind == "final" else NEXT + MORE_OUT[kind]


def sweep(kind, *refs):
    take = iter(refs)
    now = {name: next(take) for name in MOVING}
    fixed = {name: next(take) for name in STEADY}
    extra = {name: next(take) for name in MORE_IN[kind]}
    out = {name: next(take) for name in results_of(kind)}
    along, pad, forward = take
    weighted = out.get("weighted")
    final = kind == "final"
    gx, gy = lax.axis_index("gx"), lax.axis_index("gy")

    arrived = now["arrived"]
    pressures = extra["pressures"][...] if kind == "first" else arrived[block(1), :]
    pull = fixed["weight"][...] * (now["slots"][...] - pressures)
    perforated = into_cells(fixed["rows_to"][...], fixed["start"][...], pull)

    side_low = rows_to_tile(arrived[peer_rows(-1), :], pad)
    side_high = rows_to_tile(arrived[peer_rows(1), :], pad)
    side_low = jnp.where(gy == 0, 0.0, side_low)
    side_high = jnp.where(gy == lax.axis_size("gy") - 1, 0.0, side_high)
    open_low, open_high = gx > 0, gx < lax.axis_size("gx") - 1

    state = now["state"][...]
    linked, across, source = [fixed["fixed"][n] for n in range(3)]
    push = fixed["own_weight"][...] * (to_rows(arrived[block(0), :]) - now["at_slots"][...])
    number = fixed["index"][...]
    inflow = into_segments(push, number, fixed["table"][...])
    flux = across * (state - linked * previous(state))
    seg_res = source - flux + following(linked * flux) + inflow

    lane = lanes((STEP, 128))
    sub = subs((STEP, 128)) & 7
    numer = jnp.zeros((STEP, 128), F32)
    denom = jnp.zeros((STEP, 128), F32)
    if final:
        omega = extra["omega"][0:1, 0:1]
    for t in range(CHUNKS):
        rows = chunk(t)
        tx, ty = [fixed["trans"][n, rows, :].astype(F32) for n in range(2)]
        terms = []
        for n in range(3):
            j = n * NZ + 2 * t
            low = jnp.where(open_low, now["from_low"][j : j + 2, :], 0.0)
            high = jnp.where(open_high, now["from_high"][j : j + 2, :], 0.0)
            nx = jnp.where(sub == 0, spread_pair(low), jnp.where(sub == 7, spread_pair(high), 0.0))
            before = [pltpu.roll(side_low, (128 - j - h) % 128, 1) for h in range(2)]
            behind = [pltpu.roll(side_high, 127 - j - h, 1) for h in range(2)]
            ny = jnp.where(
                lane == 0, jnp.concatenate(before, axis=0),
                jnp.where(lane == 127, jnp.concatenate(behind, axis=0), 0.0),
            )
            share = fixed["mobility"][3 * n, rows, :].astype(F32)
            value = now["near"][n, rows, :] + tx * nx + ty * ny
            terms.append(value - share * perforated[t * STEP : (t + 1) * STEP])
        if kind in ("last", "final"):
            own = mix(fixed["diag"], rows, [extra["field"][n, rows, :] for n in range(3)])
            for n in range(3):
                change = own[n] - terms[n]
                before = fixed["rhs"][n, rows, :]
                if final:
                    kept = extra["change"][n, rows, :]
                    before = before - omega * kept
                    change = kept + omega * (change - 2.0 * kept)
                else:
                    out["change"][n, rows, :] = change
                numer += before * change
                denom += change * change
        if not final:
            total = [fixed["rhs"][n, rows, :] + terms[n] for n in range(3)]
            values = solve(fixed["diag"], rows, total)
            forward[rows, :] = values[0]
            if kind == "keep":
                for n in range(3):
                    out["field"][n, rows, :] = values[n]
            borders(values, fixed["mobility"], fixed["trans"], weighted, along, t)

    if kind in ("last", "final"):
        before = source
        change = source - seg_res
        if final:
            kept = extra["seg_change"][...]
            before = source - omega * kept
            change = kept + omega * (change - 2.0 * kept)
        else:
            out["seg_change"][...] = change
        above = jnp.sum(numer, keepdims=True) + jnp.sum(before * change, keepdims=True)
        below = jnp.sum(denom, keepdims=True) + jnp.sum(change * change, keepdims=True)
        place = lanes((PEERS, 128))
        sums = jnp.where(place == 60, above, jnp.where(place == 61, below, 0.0))
        if final:
            out["message"][...] = sums
            return
    else:
        sums = jnp.zeros((PEERS, 128), F32)
    message = out["message"]
    advanced = state + seg_res / fixed["diagonal"][...]
    out["state"][...] = advanced
    values = segment_values(advanced, number)
    out["at_slots"][...] = values
    cells = slot_values(fixed["rows_of"][...], fixed["start"][...], forward[...])
    out["slots"][...] = cells
    message[block(0), :] = cells
    message[block(1), :] = to_columns(values)
    message[block(2), :] = sums
    message[block(3), :] = jnp.zeros((PEERS, 128), F32)
    if kind == "after":
        out["omega"][...] = jnp.broadcast_to(ratio(arrived[block(2), :], 60), (8, 128))
    send_borders(
        fixed["trans"], weighted, along, out["toward_low"], out["toward_high"], message, pad
    )


def finish(arrived, omega, field_one, field_two, state_one, state_two, cells, segments):
    first = omega[0:1, 0:1]
    second = ratio(arrived[...], 60)

    def blend(one, two):
        kept = first * one
        return kept + second * (one + first * (two - one) - kept)

    for n in range(3):
        for t in range(CHUNKS):
            rows = chunk(t)
            cells[n, rows, :] = blend(field_one[n, rows, :], field_two[n, rows, :])
    segments[...] = blend(state_one[0:2], state_two[0:2])


CELLS = ((3, ROWS, 128), F32)
PAIRS = ((PEERS, 128), F32)
MESSAGE = ((4 * PEERS, 128), F32)
TILE = ((8, 128), F32)
EDGE = ((3 * NZ, 128), F32)
SHAPES = {
    "weighted": CELLS, "toward_low": EDGE, "toward_high": EDGE, "message": MESSAGE, "slots": PAIRS,
    "at_slots": TILE, "state": TILE, "omega": TILE, "field": CELLS, "change": CELLS,
    "seg_change": TILE,
}
SCRATCH = (
    pltpu.VMEM((3 * ROWS, 128), F32),
    pltpu.VMEM((16, 128), F32),
    pltpu.VMEM((ROWS, 128), F32),
)


def call(body, outs, args, scratch=(), name=None, space=pltpu.VMEM, grant=24 * 1024 * 1024):
    moved = sum(a.size * a.dtype.itemsize for a in args)
    return pl.pallas_call(
        body,
        out_shape=[jax.ShapeDtypeStruct(*out) for out in outs],
        in_specs=[pl.BlockSpec(memory_space=space)] * len(args),
        out_specs=[pl.BlockSpec(memory_space=pltpu.VMEM)] * len(outs),
        scratch_shapes=list(scratch),
        compiler_params=pltpu.CompilerParams(vmem_limit_bytes=grant),
        cost_estimate=pl.CostEstimate(flops=4_000_000, bytes_accessed=moved, transcendentals=0),
        name=name,
    )(*args)


def exchange(message):
    return lax.all_to_all(message, AXES, split_axis=0, concat_axis=0, tiled=True)


def neighbours(toward_low, toward_high):
    count = lax.axis_size("gx")
    up = [(i, (i + 1) % count) for i in range(count)]
    down = [(b, a) for a, b in up]
    return {
        "from_low": lax.ppermute(toward_high, "gx", up),
        "from_high": lax.ppermute(toward_low, "gx", down),
    }


def on_device(
    rhs, diag_block, mobility, trans, perf_cell, perf_pi, perf_seg, seg_parent, seg_trans, seg_rhs
):
    rhs = rhs.reshape(3, ROWS, 128)
    diag = diag_block.reshape(9, ROWS, 128)
    mobility = mobility.reshape(9, ROWS, 128)
    trans = trans.reshape(3, ROWS, 128)
    index = perf_seg[0]

    fixed = {"rhs": rhs, "diag": diag, "mobility": mobility, "trans": trans, "index": index}
    inputs = [rhs, diag, mobility, trans, perf_cell[0], perf_pi[0]]
    (rows_of, rows_to, start, weight, slots, weighted, toward_low, toward_high, message) = call(
        cell_setup,
        [((PEERS, ROWS), BF16), ((ROWS, PEERS), BF16),
         ((PEERS, 128), jnp.int32), PAIRS, PAIRS, CELLS, EDGE, EDGE, MESSAGE],
        inputs,
        SCRATCH + tuple(pltpu.VMEM(a.shape, a.dtype) for a in inputs)
        + (pltpu.SemaphoreType.DMA((6,)),),
        name="cell_setup",
        space=pltpu.HBM,
        grant=64 * 1024 * 1024 - 256 * 1024,
    )
    arrived = exchange(message)

    def inside(weighted):
        return call(interior, [CELLS], [weighted, trans], name="interior")[0]

    table, constants = call(
        well_tables,
        [((128, CAP * 128), BF16), ((4, 8, 128), F32)],
        [index, seg_parent.reshape(2, 128), seg_trans.reshape(2, 128), seg_rhs.reshape(2, 128)],
        name="well_tables",
    )
    fixed.update(rows_of=rows_of, rows_to=rows_to, start=start, weight=weight)
    now = {"arrived": arrived, "near": inside(weighted), "slots": slots}
    now.update(neighbours(toward_low, toward_high))
    message, own_weight, state, at_slots, diagonal = call(
        well_setup,
        [PAIRS, TILE, TILE, TILE, TILE],
        [arrived, index, table, constants],
        name="well_setup",
    )
    fixed.update(own_weight=own_weight, table=table, fixed=constants, diagonal=diagonal)
    now.update(at_slots=at_slots, state=state)
    saved = {"pressures": exchange(message)}

    def advance(kind, now):
        args = [now[name] for name in MOVING]
        args += [fixed[name] for name in STEADY]
        args += [saved[name] for name in MORE_IN[kind]]
        names = results_of(kind)
        out = call(
            functools.partial(sweep, kind),
            [PAIRS if kind == "final" else SHAPES[name] for name in names],
            args,
            SCRATCH,
            name="sweep_" + kind,
        )
        out = dict(zip(names, out))
        out["arrived"] = exchange(out.pop("message"))
        if kind != "final":
            out.update(neighbours(out.pop("toward_low"), out.pop("toward_high")))
            out["near"] = inside(out.pop("weighted"))
        return out

    now = advance("first", now)
    now = advance("plain", now)
    one = advance("keep", now)
    saved["field"] = one["field"]
    now = advance("last", one)
    saved.update(change=now["change"], seg_change=now["seg_change"])
    now = advance("after", now)
    saved["omega"] = now["omega"]
    now = advance("plain", now)
    two = advance("keep", now)
    saved["field"] = two["field"]
    sums = advance("final", two)
    cells, segments = call(
        finish,
        [CELLS, ((2, 128), F32)],
        [sums["arrived"], saved["omega"], one["field"], two["field"], one["state"], two["state"]],
        name="finish",
    )
    return cells.reshape(3, NZ, CX, CY), segments.reshape(256)


def solution(mesh):
    grid = P(None, None, "gx", "gy")
    pairs = P(AXES, None, None)
    flat = P(AXES)
    return jax.shard_map(
        on_device,
        mesh=mesh,
        in_specs=(grid, grid, grid, grid, pairs, pairs, pairs, flat, flat, flat),
        out_specs=(grid, flat),
        check_vma=False,
    )
```

```python
import functools

import jax
import jax.numpy as jnp
from jax import lax
from jax.experimental import pallas as pl
from jax.experimental.pallas import tpu as pltpu
from jax.sharding import PartitionSpec as P

F32 = jnp.float32
BF16 = jnp.bfloat16
AXES = ("gx", "gy")
NZ, CX, CY = 20, 8, 128
ROWS = NZ * CX
STEP = 16
CHUNKS = ROWS // STEP
PEERS = 128
CAP = 8


def lanes(shape):
    return lax.broadcasted_iota(jnp.int32, shape, 1)


def subs(shape):
    return lax.broadcasted_iota(jnp.int32, shape, 0)


def split3(x):
    high = x.astype(BF16)
    rest = x - high.astype(F32)
    mid = rest.astype(BF16)
    low = (rest - mid.astype(F32)).astype(BF16)
    return high, mid, low


def pick_rows(onehot, x):
    high, mid, low = split3(x)

    def dot(part):
        return lax.dot_general(onehot, part, (((1,), (0,)), ((), ())), preferred_element_type=F32)

    return (dot(low) + dot(mid)) + dot(high)


def is_slot(lane):
    return (lane & 63) >= 60


def slot_values(rows_of, start, first):
    lane = lanes((PEERS, CY))
    number = (lane & 3) + jnp.where(lane >= 64, 4, 0)
    picked = pick_rows(rows_of, first)
    window = jnp.take_along_axis(picked, (start + number) & (CY - 1), axis=1)
    return jnp.where(is_slot(lane), window, 0.0)


def into_cells(rows_to, start, flows):
    number = (lanes((PEERS, CY)) - start) & (CY - 1)
    place = jnp.where(number < 4, number + 60, jnp.where(number < CAP, number + 120, 0))
    return pick_rows(rows_to, jnp.take_along_axis(flows, place, axis=1))


def segment_values(state, index):
    low = index & 127
    first = jnp.take_along_axis(jnp.broadcast_to(state[0:1], (8, 128)), low, axis=1)
    second = jnp.take_along_axis(jnp.broadcast_to(state[1:2], (8, 128)), low, axis=1)
    return jnp.where(index >= 128, second, first)


def into_segments(values, index, table):
    parts = [part.astype(F32) for part in split3(values)]
    sub = subs((16, 128))
    upper = (index >= 128).astype(jnp.int32)
    tiles = []
    for k in range(CAP):
        row = [jnp.broadcast_to(part[k : k + 1], (16, 128)) for part in parts]
        mine = jnp.broadcast_to(upper[k : k + 1], (16, 128)) == (sub & 1)
        tile = jnp.where(sub < 2, row[0], jnp.where(sub < 4, row[1], row[2]))
        tiles.append(jnp.where(mine & (sub < 6), tile, 0.0).astype(BF16))
    left = jnp.concatenate(tiles, axis=1)
    out = lax.dot_general(left, table, (((1,), (1,)), ((), ())), preferred_element_type=F32)[:8]
    total = (pltpu.roll(out, 4, 0) + pltpu.roll(out, 6, 0)) + out
    return jnp.where(subs((8, 128)) < 2, total, 0.0)


def previous(state):
    moved = pltpu.roll(state, 1, 1)
    return jnp.where(lanes((8, 128)) == 0, pltpu.roll(moved, 1, 0), moved)


def following(state):
    moved = pltpu.roll(state, 127, 1)
    return jnp.where(lanes((8, 128)) == 127, pltpu.roll(moved, 7, 0), moved)


def to_columns(values):
    gap = jnp.zeros((60, 128), F32)
    return jnp.concatenate([gap, values[0:4], gap, values[4:8]], axis=0).T


def to_rows(columns):
    turned = columns.T
    return jnp.concatenate([turned[60:64], turned[124:128]], axis=0)


def block(n):
    return pl.ds(n, PEERS, stride=4)


def halves(x):
    high = x.astype(BF16).astype(F32)
    return high, x - high


def chunk(t):
    return pl.ds(t * STEP, STEP)


def me():
    return lax.axis_index("gx") * 16 + lax.axis_index("gy")


def peer_rows(shift):
    return pl.ds(4 * ((me() + shift) & (PEERS - 1)), 4)


def tile_to_rows(tile, pad):
    pad[0:8] = tile
    pad[8:16] = pltpu.roll(tile, 64, 1)
    even = pad[pl.ds(0, 4, stride=2), :]
    odd = pad[pl.ds(9, 4, stride=2), :]
    return jnp.where(lanes((4, 128)) < 64, even, odd)


def rows_to_tile(four, pad):
    pad[0:4] = four
    pad[8:16] = pltpu.roll(pad[0:8], 64, 1)
    low, high = pad[0:4], pad[8:12]
    pad[pl.ds(0, 4, stride=2), :] = low
    pad[pl.ds(1, 4, stride=2), :] = high
    return pad[0:8]


def mix(matrix, rows, vector):
    entry = [matrix[n, rows, :].astype(F32) for n in range(9)]
    x, y, z = vector
    return [entry[3 * n] * x + entry[3 * n + 1] * y + entry[3 * n + 2] * z for n in range(3)]


def solve(diag, rows, vector):
    a, b, c, d, e, f, g, h, i = [diag[n, rows, :].astype(F32) for n in range(9)]
    x, y, z = vector
    p, q, s = e * i - f * h, f * g - d * i, d * h - e * g
    scale = 1.0 / (a * p + b * q + c * s)
    return [
        (p * x + (c * h - b * i) * y + (b * f - c * e) * z) * scale,
        (q * x + (a * i - c * g) * y + (c * d - a * f) * z) * scale,
        (s * x + (b * g - a * h) * y + (a * e - b * d) * z) * scale,
    ]


def borders(values, mobility, trans, weighted, along, t):
    rows = chunk(t)
    tx = trans[0, rows, :].astype(F32)
    for n, value in enumerate(mix(mobility, rows, values)):
        weighted[n, rows, :] = value
        along[pl.ds(n * ROWS + t * STEP, STEP), :] = tx * value


def send_borders(trans, weighted, along, toward_low, toward_high, message, pad):
    toward_low[...] = along[pl.ds(0, 3 * NZ, stride=CX), :]
    toward_high[...] = along[pl.ds(CX - 1, 3 * NZ, stride=CX), :]
    small = lanes((8, 128))
    high = jnp.zeros((8, 128), F32)
    low = jnp.zeros((8, 128), F32)
    for t in range(CHUNKS):
        ty = trans[1, chunk(t), :].astype(F32)
        for n in range(3):
            py = ty * weighted[n, chunk(t), :]
            for half in range(2):
                j = n * NZ + 2 * t + half
                moved = pltpu.roll(py[8 * half : 8 * half + 8], j + 1, 1)
                high = jnp.where(small == j, moved, high)
                low = jnp.where(small == j + 1, moved, low)
    low = pltpu.roll(low, 127, 1)
    mine = is_slot(lanes((4, 128)))
    for shift, tile in ((1, high), (-1, low)):
        rows = peer_rows(shift)
        packed = tile_to_rows(tile, pad)
        message[rows, :] = jnp.where(mine, message[rows, :], packed)


def interior(weighted, trans, near):
    lane = lanes((STEP, 128))
    sub = subs((STEP, 128)) & 7
    zero = jnp.zeros((8, 128), F32)
    up = [trans[2, chunk(t), :].astype(F32) for t in range(CHUNKS)]
    for t in range(CHUNKS):
        rows = chunk(t)
        tx, ty = [trans[n, rows, :].astype(F32) for n in range(2)]
        tz = up[t]
        for n in range(3):
            value = weighted[n, rows, :]
            px, py = tx * value, ty * value
            nx = jnp.where(sub == 0, 0.0, pltpu.roll(px, 1, 0)) + jnp.where(
                sub == 7, 0.0, pltpu.roll(px, STEP - 1, 0)
            )
            ny = jnp.where(lane == 0, 0.0, pltpu.roll(py, 1, 1)) + jnp.where(
                lane == 127, 0.0, pltpu.roll(py, 127, 1)
            )
            pz = tz * value
            below = zero
            above = zero
            if t:
                below = up[t - 1][8:16] * weighted[n, pl.ds(t * STEP - 8, 8), :]
            if t + 1 < CHUNKS:
                above = up[t + 1][0:8] * weighted[n, pl.ds(t * STEP + STEP, 8), :]
            nz = jnp.concatenate([below + pz[8:16], pz[0:8] + above], axis=0)
            near[n, rows, :] = tx * nx + ty * ny + tz * nz


def cell_setup(rhs_in, diag_in, mobility_in, trans_in, cells_in, pi_in,
               rows_of, rows_to, start, weight, slots,
               weighted, toward_low, toward_high, message, along, pad, forward,
               rhs, diag, mobility, trans, cells, pi, sems):
    pairs = ((rhs_in, rhs), (diag_in, diag), (cells_in, cells), (pi_in, pi),
             (mobility_in, mobility), (trans_in, trans))
    copies = [pltpu.make_async_copy(a, b, sems.at[n]) for n, (a, b) in enumerate(pairs)]
    for copy in copies:
        copy.start()
    for copy in copies:
        copy.wait()
    for t in range(CHUNKS):
        rows = chunk(t)
        values = solve(diag, rows, [rhs[n, rows, :] for n in range(3)])
        forward[rows, :] = values[0]
        borders(values, mobility, trans, weighted, along, t)
    base = cells[0:1, :]
    row = lax.shift_right_logical(base, 7)
    live = pi[...]
    gap = jnp.zeros((44, 128), F32)
    info = jnp.concatenate(
        [jnp.broadcast_to(row.astype(F32), (8, 128)),
         jnp.broadcast_to((base & 127).astype(F32), (8, 128)),
         gap, live[0:4], gap, jnp.zeros((16, 128), F32), live[4:8]],
        axis=0,
    ).T
    rows_to[...] = (subs((ROWS, PEERS)) == jnp.broadcast_to(row, (ROWS, PEERS))).astype(F32).astype(BF16)
    row_column = jnp.broadcast_to(info[:, 0:1], (PEERS, ROWS)).astype(jnp.int32)
    rows_of[...] = (lanes((PEERS, ROWS)) == row_column).astype(F32).astype(BF16)
    begin = jnp.broadcast_to(info[:, 8:9], (PEERS, 128)).astype(jnp.int32)
    start[...] = begin
    weights = jnp.where(is_slot(lanes((PEERS, 128))), info, 0.0)
    weight[...] = weights
    values = slot_values(rows_of[...], begin, forward[...])
    slots[...] = values
    message[block(0), :] = values
    message[block(1), :] = weights
    message[block(2), :] = jnp.zeros((PEERS, 128), F32)
    message[block(3), :] = jnp.zeros((PEERS, 128), F32)
    send_borders(trans, weighted, along, toward_low, toward_high, message, pad)


def well_tables(index, parent, trans, rhs, table, fixed):
    low = index[...] & 127
    for k in range(CAP):
        hit = subs((128, 128)) == jnp.broadcast_to(low[k : k + 1], (128, 128))
        table[:, 128 * k : 128 * (k + 1)] = hit.astype(F32).astype(BF16)
    zeros = jnp.zeros((6, 128), F32)
    linked = jnp.concatenate([(parent[...] >= 0).astype(F32), zeros], axis=0)
    across = jnp.concatenate([trans[...], zeros], axis=0)
    fixed[0] = linked
    fixed[1] = across
    fixed[2] = jnp.concatenate([rhs[...], zeros], axis=0)
    fixed[3] = across + following(linked * across)


def well_setup(arrived, index, table, fixed, message, weight, state, at_slots, diagonal):
    pi = to_rows(arrived[block(1), :])
    weight[...] = pi
    number = index[...]
    total = fixed[3] + into_segments(pi, number, table[...])
    total = jnp.where(subs((8, 128)) < 2, total, 1.0)
    diagonal[...] = total
    now = fixed[2] / total
    state[...] = now
    values = segment_values(now, number)
    at_slots[...] = values
    message[...] = to_columns(values)


def ratio(sums, place):
    total = jnp.sum(sums, axis=0, keepdims=True)
    lane = lanes((1, 128))
    numer = jnp.sum(jnp.where(lane == place, total, 0.0), axis=1, keepdims=True)
    denom = jnp.sum(jnp.where(lane == place + 1, total, 0.0), axis=1, keepdims=True)
    return numer / denom


def spread_pair(two):
    return jnp.concatenate(
        [jnp.broadcast_to(two[h : h + 1], (8, 128)) for h in range(2)], axis=0
    )


STEADY = ("rhs", "diag", "mobility", "trans", "rows_of", "rows_to", "start", "weight",
          "own_weight", "table", "index", "fixed", "diagonal")
MOVING = ("arrived", "near", "from_low", "from_high", "slots", "at_slots", "state")
NEXT = ("weighted", "toward_low", "toward_high", "message", "slots", "at_slots", "state")
MORE_IN = {
    "first": ("pressures",), "plain": (), "keep": (), "last": ("field",), "after": (),
    "final": ("field", "change", "seg_change", "omega"),
}
NARROW = ("first", "plain", "keep", "after")
MORE_OUT = {
    "first": (), "plain": (), "keep": ("field",), "last": ("change", "seg_change"),
    "after": ("omega",), "final": (),
}


def results_of(kind):
    return ("message",) if kind == "final" else NEXT + MORE_OUT[kind]


def sweep(kind, *refs):
    take = iter(refs)
    now = {name: next(take) for name in MOVING}
    fixed = {name: next(take) for name in STEADY}
    extra = {name: next(take) for name in MORE_IN[kind]}
    out = {name: next(take) for name in results_of(kind)}
    along, pad, forward, wide = take
    narrow = kind in NARROW
    weighted = out.get("weighted")
    final = kind == "final"
    gx, gy = lax.axis_index("gx"), lax.axis_index("gy")

    arrived = now["arrived"]
    if arrived.dtype == BF16:
        wide[...] = arrived[...].astype(F32)
        arrived = wide
        pressures = arrived[block(1), :] + arrived[block(3), :]
        heads = arrived[block(0), :] + arrived[block(2), :]
    else:
        pressures = extra["pressures"][...] if kind == "first" else arrived[block(1), :]
        heads = arrived[block(0), :]
    pull = fixed["weight"][...] * (now["slots"][...] - pressures)
    perforated = into_cells(fixed["rows_to"][...], fixed["start"][...], pull)

    side_low = rows_to_tile(arrived[peer_rows(-1), :], pad)
    side_high = rows_to_tile(arrived[peer_rows(1), :], pad)
    side_low = jnp.where(gy == 0, 0.0, side_low)
    side_high = jnp.where(gy == lax.axis_size("gy") - 1, 0.0, side_high)
    open_low, open_high = gx > 0, gx < lax.axis_size("gx") - 1

    state = now["state"][...]
    linked, across, source = [fixed["fixed"][n] for n in range(3)]
    push = fixed["own_weight"][...] * (to_rows(heads) - now["at_slots"][...])
    number = fixed["index"][...]
    inflow = into_segments(push, number, fixed["table"][...])
    flux = across * (state - linked * previous(state))
    seg_res = source - flux + following(linked * flux) + inflow

    lane = lanes((STEP, 128))
    sub = subs((STEP, 128)) & 7
    numer = jnp.zeros((STEP, 128), F32)
    denom = jnp.zeros((STEP, 128), F32)
    if final:
        omega = extra["omega"][0:1, 0:1]
    for t in range(CHUNKS):
        rows = chunk(t)
        tx, ty = [fixed["trans"][n, rows, :].astype(F32) for n in range(2)]
        terms = []
        for n in range(3):
            j = n * NZ + 2 * t
            low = jnp.where(open_low, now["from_low"][j : j + 2, :], 0.0)
            high = jnp.where(open_high, now["from_high"][j : j + 2, :], 0.0)
            nx = jnp.where(sub == 0, spread_pair(low), jnp.where(sub == 7, spread_pair(high), 0.0))
            before = [pltpu.roll(side_low, (128 - j - h) % 128, 1) for h in range(2)]
            behind = [pltpu.roll(side_high, 127 - j - h, 1) for h in range(2)]
            ny = jnp.where(
                lane == 0, jnp.concatenate(before, axis=0),
                jnp.where(lane == 127, jnp.concatenate(behind, axis=0), 0.0),
            )
            share = fixed["mobility"][3 * n, rows, :].astype(F32)
            value = now["near"][n, rows, :] + tx * nx + ty * ny
            terms.append(value - share * perforated[t * STEP : (t + 1) * STEP])
        if kind in ("last", "final"):
            own = mix(fixed["diag"], rows, [extra["field"][n, rows, :] for n in range(3)])
            for n in range(3):
                change = own[n] - terms[n]
                before = fixed["rhs"][n, rows, :]
                if final:
                    kept = extra["change"][n, rows, :]
                    before = before - omega * kept
                    change = kept + omega * (change - 2.0 * kept)
                else:
                    out["change"][n, rows, :] = change
                numer += before * change
                denom += change * change
        if not final:
            total = [fixed["rhs"][n, rows, :] + terms[n] for n in range(3)]
            values = solve(fixed["diag"], rows, total)
            forward[rows, :] = values[0]
            if kind == "keep":
                for n in range(3):
                    out["field"][n, rows, :] = values[n]
            borders(values, fixed["mobility"], fixed["trans"], weighted, along, t)

    if kind in ("last", "final"):
        before = source
        change = source - seg_res
        if final:
            kept = extra["seg_change"][...]
            before = source - omega * kept
            change = kept + omega * (change - 2.0 * kept)
        else:
            out["seg_change"][...] = change
        above = jnp.sum(numer, keepdims=True) + jnp.sum(before * change, keepdims=True)
        below = jnp.sum(denom, keepdims=True) + jnp.sum(change * change, keepdims=True)
        place = lanes((PEERS, 128))
        sums = jnp.where(place == 60, above, jnp.where(place == 61, below, 0.0))
        if final:
            out["message"][...] = sums
            return
    if kind == "after":
        out["omega"][...] = jnp.broadcast_to(ratio(arrived[block(2), :], 60), (8, 128))
    message = wide if narrow else out["message"]
    advanced = state + seg_res / fixed["diagonal"][...]
    out["state"][...] = advanced
    values = segment_values(advanced, number)
    out["at_slots"][...] = values
    cells = slot_values(fixed["rows_of"][...], fixed["start"][...], forward[...])
    out["slots"][...] = cells
    columns = to_columns(values)
    if narrow:
        message[block(0), :], message[block(2), :] = halves(cells)
        message[block(1), :], message[block(3), :] = halves(columns)
    else:
        message[block(0), :] = cells
        message[block(1), :] = columns
        message[block(2), :] = sums
        message[block(3), :] = jnp.zeros((PEERS, 128), F32)
    send_borders(
        fixed["trans"], weighted, along, out["toward_low"], out["toward_high"], message, pad
    )
    if narrow:
        out["message"][...] = message[...].astype(BF16)


def finish(arrived, omega, field_one, field_two, state_one, state_two, cells, segments):
    first = omega[0:1, 0:1]
    second = ratio(arrived[...], 60)

    def blend(one, two):
        kept = first * one
        return kept + second * (one + first * (two - one) - kept)

    for n in range(3):
        for t in range(CHUNKS):
            rows = chunk(t)
            cells[n, rows, :] = blend(field_one[n, rows, :], field_two[n, rows, :])
    segments[...] = blend(state_one[0:2], state_two[0:2])


CELLS = ((3, ROWS, 128), F32)
PAIRS = ((PEERS, 128), F32)
MESSAGE = ((4 * PEERS, 128), F32)
TILE = ((8, 128), F32)
EDGE = ((3 * NZ, 128), F32)
SHAPES = {
    "weighted": CELLS, "toward_low": EDGE, "toward_high": EDGE, "message": MESSAGE, "slots": PAIRS,
    "at_slots": TILE, "state": TILE, "omega": TILE, "field": CELLS, "change": CELLS,
    "seg_change": TILE,
}


def shape_of(kind, name):
    if name != "message":
        return SHAPES[name]
    if kind == "final":
        return PAIRS
    return (MESSAGE[0], BF16) if kind in NARROW else MESSAGE


SCRATCH = (
    pltpu.VMEM((3 * ROWS, 128), F32),
    pltpu.VMEM((16, 128), F32),
    pltpu.VMEM((ROWS, 128), F32),
)


def call(body, outs, args, scratch=(), name=None, space=pltpu.VMEM, grant=24 * 1024 * 1024):
    moved = sum(a.size * a.dtype.itemsize for a in args)
    return pl.pallas_call(
        body,
        out_shape=[jax.ShapeDtypeStruct(*out) for out in outs],
        in_specs=[pl.BlockSpec(memory_space=space)] * len(args),
        out_specs=[pl.BlockSpec(memory_space=pltpu.VMEM)] * len(outs),
        scratch_shapes=list(scratch),
        compiler_params=pltpu.CompilerParams(vmem_limit_bytes=grant),
        cost_estimate=pl.CostEstimate(flops=4_000_000, bytes_accessed=moved, transcendentals=0),
        name=name,
    )(*args)


def exchange(message):
    return lax.all_to_all(message, AXES, split_axis=0, concat_axis=0, tiled=True)


def neighbours(toward_low, toward_high):
    count = lax.axis_size("gx")
    up = [(i, (i + 1) % count) for i in range(count)]
    down = [(b, a) for a, b in up]
    return {
        "from_low": lax.ppermute(toward_high, "gx", up),
        "from_high": lax.ppermute(toward_low, "gx", down),
    }


def on_device(
    rhs, diag_block, mobility, trans, perf_cell, perf_pi, perf_seg, seg_parent, seg_trans, seg_rhs
):
    rhs = rhs.reshape(3, ROWS, 128)
    diag = diag_block.reshape(9, ROWS, 128)
    mobility = mobility.reshape(9, ROWS, 128)
    trans = trans.reshape(3, ROWS, 128)
    index = perf_seg[0]

    fixed = {"rhs": rhs, "diag": diag, "mobility": mobility, "trans": trans, "index": index}
    inputs = [rhs, diag, mobility, trans, perf_cell[0], perf_pi[0]]
    (rows_of, rows_to, start, weight, slots, weighted, toward_low, toward_high, message) = call(
        cell_setup,
        [((PEERS, ROWS), BF16), ((ROWS, PEERS), BF16),
         ((PEERS, 128), jnp.int32), PAIRS, PAIRS, CELLS, EDGE, EDGE, MESSAGE],
        inputs,
        SCRATCH + tuple(pltpu.VMEM(a.shape, a.dtype) for a in inputs)
        + (pltpu.SemaphoreType.DMA((6,)),),
        name="cell_setup",
        space=pltpu.HBM,
        grant=64 * 1024 * 1024 - 256 * 1024,
    )
    arrived = exchange(message)

    def inside(weighted):
        return call(interior, [CELLS], [weighted, trans], name="interior")[0]

    table, constants = call(
        well_tables,
        [((128, CAP * 128), BF16), ((4, 8, 128), F32)],
        [index, seg_parent.reshape(2, 128), seg_trans.reshape(2, 128), seg_rhs.reshape(2, 128)],
        name="well_tables",
    )
    fixed.update(rows_of=rows_of, rows_to=rows_to, start=start, weight=weight)
    now = {"arrived": arrived, "near": inside(weighted), "slots": slots}
    now.update(neighbours(toward_low, toward_high))
    message, own_weight, state, at_slots, diagonal = call(
        well_setup,
        [PAIRS, TILE, TILE, TILE, TILE],
        [arrived, index, table, constants],
        name="well_setup",
    )
    fixed.update(own_weight=own_weight, table=table, fixed=constants, diagonal=diagonal)
    now.update(at_slots=at_slots, state=state)
    saved = {"pressures": exchange(message)}

    def advance(kind, now):
        args = [now[name] for name in MOVING]
        args += [fixed[name] for name in STEADY]
        args += [saved[name] for name in MORE_IN[kind]]
        names = results_of(kind)
        out = call(
            functools.partial(sweep, kind),
            [shape_of(kind, name) for name in names],
            args,
            SCRATCH + (pltpu.VMEM(*MESSAGE),),
            name="sweep_" + kind,
        )
        out = dict(zip(names, out))
        out["arrived"] = exchange(out.pop("message"))
        if kind != "final":
            out.update(neighbours(out.pop("toward_low"), out.pop("toward_high")))
            out["near"] = inside(out.pop("weighted"))
        return out

    now = advance("first", now)
    now = advance("plain", now)
    one = advance("keep", now)
    saved["field"] = one["field"]
    now = advance("last", one)
    saved.update(change=now["change"], seg_change=now["seg_change"])
    now = advance("after", now)
    saved["omega"] = now["omega"]
    now = advance("plain", now)
    two = advance("keep", now)
    saved["field"] = two["field"]
    sums = advance("final", two)
    cells, segments = call(
        finish,
        [CELLS, ((2, 128), F32)],
        [sums["arrived"], saved["omega"], one["field"], two["field"], one["state"], two["state"]],
        name="finish",
    )
    return cells.reshape(3, NZ, CX, CY), segments.reshape(256)


def solution(mesh):
    grid = P(None, None, "gx", "gy")
    pairs = P(AXES, None, None)
    flat = P(AXES)
    return jax.shard_map(
        on_device,
        mesh=mesh,
        in_specs=(grid, grid, grid, grid, pairs, pairs, pairs, flat, flat, flat),
        out_specs=(grid, flat),
        check_vma=False,
    )
```

```python
import functools

import jax
import jax.numpy as jnp
from jax import lax
from jax.experimental import pallas as pl
from jax.experimental.pallas import tpu as pltpu
from jax.sharding import PartitionSpec as P

F32 = jnp.float32
BF16 = jnp.bfloat16
AXES = ("gx", "gy")
NZ, CX, CY = 20, 8, 128
ROWS = NZ * CX
STEP = 16
CHUNKS = ROWS // STEP
PEERS = 128
CAP = 8


def lanes(shape):
    return lax.broadcasted_iota(jnp.int32, shape, 1)


def subs(shape):
    return lax.broadcasted_iota(jnp.int32, shape, 0)


def split3(x):
    high = x.astype(BF16)
    rest = x - high.astype(F32)
    mid = rest.astype(BF16)
    low = (rest - mid.astype(F32)).astype(BF16)
    return high, mid, low


def pick_rows(onehot, x):
    high, mid, low = split3(x)

    def dot(part):
        return lax.dot_general(onehot, part, (((1,), (0,)), ((), ())), preferred_element_type=F32)

    return (dot(low) + dot(mid)) + dot(high)


def is_slot(lane):
    return (lane & 63) >= 60


def slot_values(rows_of, start, first):
    lane = lanes((PEERS, CY))
    number = (lane & 3) + jnp.where(lane >= 64, 4, 0)
    picked = pick_rows(rows_of, first)
    window = jnp.take_along_axis(picked, (start + number) & (CY - 1), axis=1)
    return jnp.where(is_slot(lane), window, 0.0)


def into_cells(rows_to, start, flows):
    number = (lanes((PEERS, CY)) - start) & (CY - 1)
    place = jnp.where(number < 4, number + 60, jnp.where(number < CAP, number + 120, 0))
    return pick_rows(rows_to, jnp.take_along_axis(flows, place, axis=1))


def segment_values(state, index):
    low = index & 127
    first = jnp.take_along_axis(jnp.broadcast_to(state[0:1], (8, 128)), low, axis=1)
    second = jnp.take_along_axis(jnp.broadcast_to(state[1:2], (8, 128)), low, axis=1)
    return jnp.where(index >= 128, second, first)


def into_segments(values, index, table):
    parts = [part.astype(F32) for part in split3(values)]
    sub = subs((16, 128))
    upper = (index >= 128).astype(jnp.int32)
    tiles = []
    for k in range(CAP):
        row = [jnp.broadcast_to(part[k : k + 1], (16, 128)) for part in parts]
        mine = jnp.broadcast_to(upper[k : k + 1], (16, 128)) == (sub & 1)
        tile = jnp.where(sub < 2, row[0], jnp.where(sub < 4, row[1], row[2]))
        tiles.append(jnp.where(mine & (sub < 6), tile, 0.0).astype(BF16))
    left = jnp.concatenate(tiles, axis=1)
    out = lax.dot_general(left, table, (((1,), (1,)), ((), ())), preferred_element_type=F32)[:8]
    total = (pltpu.roll(out, 4, 0) + pltpu.roll(out, 6, 0)) + out
    return jnp.where(subs((8, 128)) < 2, total, 0.0)


def previous(state):
    moved = pltpu.roll(state, 1, 1)
    return jnp.where(lanes((8, 128)) == 0, pltpu.roll(moved, 1, 0), moved)


def following(state):
    moved = pltpu.roll(state, 127, 1)
    return jnp.where(lanes((8, 128)) == 127, pltpu.roll(moved, 7, 0), moved)


def to_columns(values):
    gap = jnp.zeros((60, 128), F32)
    return jnp.concatenate([gap, values[0:4], gap, values[4:8]], axis=0).T


def to_rows(columns):
    turned = columns.T
    return jnp.concatenate([turned[60:64], turned[124:128]], axis=0)


def block(n):
    return pl.ds(n, PEERS, stride=4)


def halves(x):
    high = x.astype(BF16).astype(F32)
    return high, x - high


def chunk(t):
    return pl.ds(t * STEP, STEP)


def me():
    return lax.axis_index("gx") * 16 + lax.axis_index("gy")


def peer_rows(shift):
    return pl.ds(4 * ((me() + shift) & (PEERS - 1)), 4)


def tile_to_rows(tile, pad):
    pad[0:8] = tile
    pad[8:16] = pltpu.roll(tile, 64, 1)
    even = pad[pl.ds(0, 4, stride=2), :]
    odd = pad[pl.ds(9, 4, stride=2), :]
    return jnp.where(lanes((4, 128)) < 64, even, odd)


def rows_to_tile(four, pad):
    pad[0:4] = four
    pad[8:16] = pltpu.roll(pad[0:8], 64, 1)
    low, high = pad[0:4], pad[8:12]
    pad[pl.ds(0, 4, stride=2), :] = low
    pad[pl.ds(1, 4, stride=2), :] = high
    return pad[0:8]


def mix(matrix, rows, vector):
    entry = [matrix[n, rows, :].astype(F32) for n in range(9)]
    x, y, z = vector
    return [entry[3 * n] * x + entry[3 * n + 1] * y + entry[3 * n + 2] * z for n in range(3)]


def solve(diag, rows, vector):
    a, b, c, d, e, f, g, h, i = [diag[n, rows, :].astype(F32) for n in range(9)]
    x, y, z = vector
    p, q, s = e * i - f * h, f * g - d * i, d * h - e * g
    scale = 1.0 / (a * p + b * q + c * s)
    return [
        (p * x + (c * h - b * i) * y + (b * f - c * e) * z) * scale,
        (q * x + (a * i - c * g) * y + (c * d - a * f) * z) * scale,
        (s * x + (b * g - a * h) * y + (a * e - b * d) * z) * scale,
    ]


def borders(values, mobility, trans, weighted, along, t):
    rows = chunk(t)
    tx = trans[0, rows, :].astype(F32)
    for n, value in enumerate(mix(mobility, rows, values)):
        weighted[n, rows, :] = value
        along[pl.ds(n * ROWS + t * STEP, STEP), :] = tx * value


def send_borders(trans, weighted, along, toward_low, toward_high, message, pad):
    toward_low[...] = along[pl.ds(0, 3 * NZ, stride=CX), :]
    toward_high[...] = along[pl.ds(CX - 1, 3 * NZ, stride=CX), :]
    small = lanes((8, 128))
    high = jnp.zeros((8, 128), F32)
    low = jnp.zeros((8, 128), F32)
    for t in range(CHUNKS):
        ty = trans[1, chunk(t), :].astype(F32)
        for n in range(3):
            py = ty * weighted[n, chunk(t), :]
            for half in range(2):
                j = n * NZ + 2 * t + half
                moved = pltpu.roll(py[8 * half : 8 * half + 8], j + 1, 1)
                high = jnp.where(small == j, moved, high)
                low = jnp.where(small == j + 1, moved, low)
    low = pltpu.roll(low, 127, 1)
    mine = is_slot(lanes((4, 128)))
    for shift, tile in ((1, high), (-1, low)):
        rows = peer_rows(shift)
        packed = tile_to_rows(tile, pad)
        message[rows, :] = jnp.where(mine, message[rows, :], packed)


def interior(weighted, trans, near):
    lane = lanes((STEP, 128))
    sub = subs((STEP, 128)) & 7
    zero = jnp.zeros((8, 128), F32)
    up = [trans[2, chunk(t), :].astype(F32) for t in range(CHUNKS)]
    for t in range(CHUNKS):
        rows = chunk(t)
        tx, ty = [trans[n, rows, :].astype(F32) for n in range(2)]
        tz = up[t]
        for n in range(3):
            value = weighted[n, rows, :]
            px, py = tx * value, ty * value
            nx = jnp.where(sub == 0, 0.0, pltpu.roll(px, 1, 0)) + jnp.where(
                sub == 7, 0.0, pltpu.roll(px, STEP - 1, 0)
            )
            ny = jnp.where(lane == 0, 0.0, pltpu.roll(py, 1, 1)) + jnp.where(
                lane == 127, 0.0, pltpu.roll(py, 127, 1)
            )
            pz = tz * value
            below = zero
            above = zero
            if t:
                below = up[t - 1][8:16] * weighted[n, pl.ds(t * STEP - 8, 8), :]
            if t + 1 < CHUNKS:
                above = up[t + 1][0:8] * weighted[n, pl.ds(t * STEP + STEP, 8), :]
            nz = jnp.concatenate([below + pz[8:16], pz[0:8] + above], axis=0)
            near[n, rows, :] = tx * nx + ty * ny + tz * nz


def cell_setup(rhs_in, diag_in, mobility_in, trans_in, cells_in, pi_in,
               rows_of, rows_to, start, weight, slots,
               weighted, toward_low, toward_high, message, along, pad, forward, wide,
               rhs, diag, mobility, trans, cells, pi, sems):
    pairs = ((cells_in, cells), (pi_in, pi), (rhs_in, rhs), (diag_in, diag),
             (mobility_in, mobility), (trans_in, trans))
    copies = [pltpu.make_async_copy(a, b, sems.at[n]) for n, (a, b) in enumerate(pairs)]
    for copy in copies:
        copy.start()
    for copy in copies[:2]:
        copy.wait()
    base = cells[0:1, :]
    row = lax.shift_right_logical(base, 7)
    live = pi[...]
    gap = jnp.zeros((44, 128), F32)
    info = jnp.concatenate(
        [jnp.broadcast_to(row.astype(F32), (8, 128)),
         jnp.broadcast_to((base & 127).astype(F32), (8, 128)),
         gap, live[0:4], gap, jnp.zeros((16, 128), F32), live[4:8]],
        axis=0,
    ).T
    rows_to[...] = (subs((ROWS, PEERS)) == jnp.broadcast_to(row, (ROWS, PEERS))).astype(F32).astype(BF16)
    row_column = jnp.broadcast_to(info[:, 0:1], (PEERS, ROWS)).astype(jnp.int32)
    rows_of[...] = (lanes((PEERS, ROWS)) == row_column).astype(F32).astype(BF16)
    begin = jnp.broadcast_to(info[:, 8:9], (PEERS, 128)).astype(jnp.int32)
    start[...] = begin
    weights = jnp.where(is_slot(lanes((PEERS, 128))), info, 0.0)
    weight[...] = weights
    wide[block(1), :], wide[block(3), :] = halves(weights)
    for copy in copies[2:4]:
        copy.wait()
    for t in range(CHUNKS):
        rows = chunk(t)
        values = solve(diag, rows, [rhs[n, rows, :] for n in range(3)])
        forward[rows, :] = values[0]
        for n in range(3):
            weighted[n, rows, :] = values[n]
    values = slot_values(rows_of[...], begin, forward[...])
    slots[...] = values
    wide[block(0), :], wide[block(2), :] = halves(values)
    for copy in copies[4:]:
        copy.wait()
    for t in range(CHUNKS):
        values = [weighted[n, chunk(t), :] for n in range(3)]
        borders(values, mobility, trans, weighted, along, t)
    send_borders(trans, weighted, along, toward_low, toward_high, wide, pad)
    message[...] = wide[...].astype(BF16)


def well_tables(index, parent, trans, rhs, table, fixed):
    low = index[...] & 127
    for k in range(CAP):
        hit = subs((128, 128)) == jnp.broadcast_to(low[k : k + 1], (128, 128))
        table[:, 128 * k : 128 * (k + 1)] = hit.astype(F32).astype(BF16)
    zeros = jnp.zeros((6, 128), F32)
    linked = jnp.concatenate([(parent[...] >= 0).astype(F32), zeros], axis=0)
    across = jnp.concatenate([trans[...], zeros], axis=0)
    fixed[0] = linked
    fixed[1] = across
    fixed[2] = jnp.concatenate([rhs[...], zeros], axis=0)
    fixed[3] = across + following(linked * across)


def well_setup(arrived, index, table, fixed, message, weight, state, at_slots, diagonal, wide):
    wide[...] = arrived[...].astype(F32)
    pi = to_rows(wide[block(1), :] + wide[block(3), :])
    weight[...] = pi
    number = index[...]
    total = fixed[3] + into_segments(pi, number, table[...])
    total = jnp.where(subs((8, 128)) < 2, total, 1.0)
    diagonal[...] = total
    now = fixed[2] / total
    state[...] = now
    values = segment_values(now, number)
    at_slots[...] = values
    message[...] = to_columns(values)


def ratio(sums, place):
    total = jnp.sum(sums, axis=0, keepdims=True)
    lane = lanes((1, 128))
    numer = jnp.sum(jnp.where(lane == place, total, 0.0), axis=1, keepdims=True)
    denom = jnp.sum(jnp.where(lane == place + 1, total, 0.0), axis=1, keepdims=True)
    return numer / denom


def spread_pair(two):
    return jnp.concatenate(
        [jnp.broadcast_to(two[h : h + 1], (8, 128)) for h in range(2)], axis=0
    )


STEADY = ("rhs", "diag", "mobility", "trans", "rows_of", "rows_to", "start", "weight",
          "own_weight", "table", "index", "fixed", "diagonal")
MOVING = ("arrived", "near", "from_low", "from_high", "slots", "at_slots", "state")
NEXT = ("weighted", "toward_low", "toward_high", "message", "slots", "at_slots", "state")
MORE_IN = {
    "first": ("pressures",), "plain": (), "keep": (), "last": ("field",), "after": (),
    "final": ("field", "change", "seg_change", "omega"),
}
NARROW = ("first", "plain", "keep", "after")
MORE_OUT = {
    "first": (), "plain": (), "keep": ("field",), "last": ("change", "seg_change"),
    "after": ("omega",), "final": (),
}


def results_of(kind):
    return ("message",) if kind == "final" else NEXT + MORE_OUT[kind]


def sweep(kind, *refs):
    take = iter(refs)
    now = {name: next(take) for name in MOVING}
    fixed = {name: next(take) for name in STEADY}
    extra = {name: next(take) for name in MORE_IN[kind]}
    out = {name: next(take) for name in results_of(kind)}
    along, pad, forward, wide = take
    narrow = kind in NARROW
    weighted = out.get("weighted")
    final = kind == "final"
    gx, gy = lax.axis_index("gx"), lax.axis_index("gy")

    arrived = now["arrived"]
    if arrived.dtype == BF16:
        wide[...] = arrived[...].astype(F32)
        arrived = wide
        heads = arrived[block(0), :] + arrived[block(2), :]
        if kind == "first":
            pressures = extra["pressures"][...]
        else:
            pressures = arrived[block(1), :] + arrived[block(3), :]
    else:
        heads, pressures = arrived[block(0), :], arrived[block(1), :]
    pull = fixed["weight"][...] * (now["slots"][...] - pressures)
    perforated = into_cells(fixed["rows_to"][...], fixed["start"][...], pull)

    side_low = rows_to_tile(arrived[peer_rows(-1), :], pad)
    side_high = rows_to_tile(arrived[peer_rows(1), :], pad)
    side_low = jnp.where(gy == 0, 0.0, side_low)
    side_high = jnp.where(gy == lax.axis_size("gy") - 1, 0.0, side_high)
    small = lanes((8, 128))
    ahead = pltpu.roll(side_high, 127, 1)
    sides = [jnp.where((small & 1) == odd, side_low, ahead) for odd in range(2)]
    open_low, open_high = gx > 0, gx < lax.axis_size("gx") - 1

    state = now["state"][...]
    linked, across, source = [fixed["fixed"][n] for n in range(3)]
    push = fixed["own_weight"][...] * (to_rows(heads) - now["at_slots"][...])
    number = fixed["index"][...]
    inflow = into_segments(push, number, fixed["table"][...])
    flux = across * (state - linked * previous(state))
    seg_res = source - flux + following(linked * flux) + inflow

    lane = lanes((STEP, 128))
    sub = subs((STEP, 128)) & 7
    numer = jnp.zeros((STEP, 128), F32)
    denom = jnp.zeros((STEP, 128), F32)
    if final:
        omega = extra["omega"][0:1, 0:1]
    for t in range(CHUNKS):
        rows = chunk(t)
        tx, ty = [fixed["trans"][n, rows, :].astype(F32) for n in range(2)]
        tx = jnp.where(
            sub == 0, jnp.where(open_low, tx, 0.0),
            jnp.where((sub == 7) & open_high, tx, 0.0),
        )
        ty = jnp.where((lane == 0) | (lane == 127), ty, 0.0)
        terms = []
        for n in range(3):
            j = n * NZ + 2 * t
            low, high = now["from_low"][j : j + 2, :], now["from_high"][j : j + 2, :]
            nx = jnp.where(sub == 0, spread_pair(low), spread_pair(high))
            ny = jnp.concatenate(
                [pltpu.roll(sides[(j + h) & 1], (128 - j - h) % 128, 1) for h in range(2)], axis=0
            )
            share = fixed["mobility"][3 * n, rows, :].astype(F32)
            value = now["near"][n, rows, :] + tx * nx + ty * ny
            terms.append(value - share * perforated[t * STEP : (t + 1) * STEP])
        if kind in ("last", "final"):
            own = mix(fixed["diag"], rows, [extra["field"][n, rows, :] for n in range(3)])
            for n in range(3):
                change = own[n] - terms[n]
                before = fixed["rhs"][n, rows, :]
                if final:
                    kept = extra["change"][n, rows, :]
                    before = before - omega * kept
                    change = kept + omega * (change - 2.0 * kept)
                else:
                    out["change"][n, rows, :] = change
                numer += before * change
                denom += change * change
        if not final:
            total = [fixed["rhs"][n, rows, :] + terms[n] for n in range(3)]
            values = solve(fixed["diag"], rows, total)
            forward[rows, :] = values[0]
            if kind == "keep":
                for n in range(3):
                    out["field"][n, rows, :] = values[n]
            borders(values, fixed["mobility"], fixed["trans"], weighted, along, t)

    if kind in ("last", "final"):
        before = source
        change = source - seg_res
        if final:
            kept = extra["seg_change"][...]
            before = source - omega * kept
            change = kept + omega * (change - 2.0 * kept)
        else:
            out["seg_change"][...] = change
        above = jnp.sum(numer, keepdims=True) + jnp.sum(before * change, keepdims=True)
        below = jnp.sum(denom, keepdims=True) + jnp.sum(change * change, keepdims=True)
        place = lanes((PEERS, 128))
        sums = jnp.where(place == 60, above, jnp.where(place == 61, below, 0.0))
        if final:
            out["message"][...] = sums
            return
    if kind == "after":
        out["omega"][...] = jnp.broadcast_to(ratio(arrived[block(2), :], 60), (8, 128))
    message = wide if narrow else out["message"]
    advanced = state + seg_res / fixed["diagonal"][...]
    out["state"][...] = advanced
    values = segment_values(advanced, number)
    out["at_slots"][...] = values
    cells = slot_values(fixed["rows_of"][...], fixed["start"][...], forward[...])
    out["slots"][...] = cells
    columns = to_columns(values)
    if narrow:
        message[block(0), :], message[block(2), :] = halves(cells)
        message[block(1), :], message[block(3), :] = halves(columns)
    else:
        message[block(0), :] = cells
        message[block(1), :] = columns
        message[block(2), :] = sums
        message[block(3), :] = jnp.zeros((PEERS, 128), F32)
    send_borders(
        fixed["trans"], weighted, along, out["toward_low"], out["toward_high"], message, pad
    )
    if narrow:
        out["message"][...] = message[...].astype(BF16)


def finish(arrived, omega, field_one, field_two, state_one, state_two, cells, segments):
    first = omega[0:1, 0:1]
    second = ratio(arrived[...], 60)

    def blend(one, two):
        kept = first * one
        return kept + second * (one + first * (two - one) - kept)

    for n in range(3):
        for t in range(CHUNKS):
            rows = chunk(t)
            cells[n, rows, :] = blend(field_one[n, rows, :], field_two[n, rows, :])
    segments[...] = blend(state_one[0:2], state_two[0:2])


CELLS = ((3, ROWS, 128), F32)
PAIRS = ((PEERS, 128), F32)
MESSAGE = ((4 * PEERS, 128), F32)
TILE = ((8, 128), F32)
EDGE = ((3 * NZ, 128), F32)
SHAPES = {
    "weighted": CELLS, "toward_low": EDGE, "toward_high": EDGE, "message": MESSAGE, "slots": PAIRS,
    "at_slots": TILE, "state": TILE, "omega": TILE, "field": CELLS, "change": CELLS,
    "seg_change": TILE,
}


def shape_of(kind, name):
    if name != "message":
        return SHAPES[name]
    if kind == "final":
        return PAIRS
    return (MESSAGE[0], BF16) if kind in NARROW else MESSAGE


SCRATCH = (
    pltpu.VMEM((3 * ROWS, 128), F32),
    pltpu.VMEM((16, 128), F32),
    pltpu.VMEM((ROWS, 128), F32),
)


def call(body, outs, args, scratch=(), name=None, space=pltpu.VMEM, grant=24 * 1024 * 1024):
    moved = sum(a.size * a.dtype.itemsize for a in args)
    return pl.pallas_call(
        body,
        out_shape=[jax.ShapeDtypeStruct(*out) for out in outs],
        in_specs=[pl.BlockSpec(memory_space=space)] * len(args),
        out_specs=[pl.BlockSpec(memory_space=pltpu.VMEM)] * len(outs),
        scratch_shapes=list(scratch),
        compiler_params=pltpu.CompilerParams(vmem_limit_bytes=grant),
        cost_estimate=pl.CostEstimate(flops=4_000_000, bytes_accessed=moved, transcendentals=0),
        name=name,
    )(*args)


def exchange(message):
    return lax.all_to_all(message, AXES, split_axis=0, concat_axis=0, tiled=True)


def neighbours(toward_low, toward_high):
    count = lax.axis_size("gx")
    up = [(i, (i + 1) % count) for i in range(count)]
    down = [(b, a) for a, b in up]
    return {
        "from_low": lax.ppermute(toward_high, "gx", up),
        "from_high": lax.ppermute(toward_low, "gx", down),
    }


def on_device(
    rhs, diag_block, mobility, trans, perf_cell, perf_pi, perf_seg, seg_parent, seg_trans, seg_rhs
):
    rhs = rhs.reshape(3, ROWS, 128)
    diag = diag_block.reshape(9, ROWS, 128)
    mobility = mobility.reshape(9, ROWS, 128)
    trans = trans.reshape(3, ROWS, 128)
    index = perf_seg[0]

    fixed = {"rhs": rhs, "diag": diag, "mobility": mobility, "trans": trans, "index": index}
    inputs = [rhs, diag, mobility, trans, perf_cell[0], perf_pi[0]]
    packed = (MESSAGE[0], BF16)
    (rows_of, rows_to, start, weight, slots, weighted, toward_low, toward_high, message) = call(
        cell_setup,
        [((PEERS, ROWS), BF16), ((ROWS, PEERS), BF16),
         ((PEERS, 128), jnp.int32), PAIRS, PAIRS, CELLS, EDGE, EDGE, packed],
        inputs,
        SCRATCH + (pltpu.VMEM(*MESSAGE),) + tuple(pltpu.VMEM(a.shape, a.dtype) for a in inputs)
        + (pltpu.SemaphoreType.DMA((6,)),),
        name="cell_setup",
        space=pltpu.HBM,
        grant=64 * 1024 * 1024 - 256 * 1024,
    )
    arrived = exchange(message)

    def inside(weighted):
        return call(interior, [CELLS], [weighted, trans], name="interior")[0]

    table, constants = call(
        well_tables,
        [((128, CAP * 128), BF16), ((4, 8, 128), F32)],
        [index, seg_parent.reshape(2, 128), seg_trans.reshape(2, 128), seg_rhs.reshape(2, 128)],
        name="well_tables",
    )
    fixed.update(rows_of=rows_of, rows_to=rows_to, start=start, weight=weight)
    now = {"arrived": arrived, "near": inside(weighted), "slots": slots}
    now.update(neighbours(toward_low, toward_high))
    message, own_weight, state, at_slots, diagonal = call(
        well_setup,
        [PAIRS, TILE, TILE, TILE, TILE],
        [arrived, index, table, constants],
        [pltpu.VMEM(*MESSAGE)],
        name="well_setup",
    )
    fixed.update(own_weight=own_weight, table=table, fixed=constants, diagonal=diagonal)
    now.update(at_slots=at_slots, state=state)
    saved = {"pressures": exchange(message)}

    def advance(kind, now):
        args = [now[name] for name in MOVING]
        args += [fixed[name] for name in STEADY]
        args += [saved[name] for name in MORE_IN[kind]]
        names = results_of(kind)
        out = call(
            functools.partial(sweep, kind),
            [shape_of(kind, name) for name in names],
            args,
            SCRATCH + (pltpu.VMEM(*MESSAGE),),
            name="sweep_" + kind,
        )
        out = dict(zip(names, out))
        out["arrived"] = exchange(out.pop("message"))
        if kind != "final":
            out.update(neighbours(out.pop("toward_low"), out.pop("toward_high")))
            out["near"] = inside(out.pop("weighted"))
        return out

    now = advance("first", now)
    now = advance("plain", now)
    one = advance("keep", now)
    saved["field"] = one["field"]
    now = advance("last", one)
    saved.update(change=now["change"], seg_change=now["seg_change"])
    now = advance("after", now)
    saved["omega"] = now["omega"]
    now = advance("plain", now)
    two = advance("keep", now)
    saved["field"] = two["field"]
    sums = advance("final", two)
    cells, segments = call(
        finish,
        [CELLS, ((2, 128), F32)],
        [sums["arrived"], saved["omega"], one["field"], two["field"], one["state"], two["state"]],
        name="finish",
    )
    return cells.reshape(3, NZ, CX, CY), segments.reshape(256)


def solution(mesh):
    grid = P(None, None, "gx", "gy")
    pairs = P(AXES, None, None)
    flat = P(AXES)
    return jax.shard_map(
        on_device,
        mesh=mesh,
        in_specs=(grid, grid, grid, grid, pairs, pairs, pairs, flat, flat, flat),
        out_specs=(grid, flat),
        check_vma=False,
    )
```

```python
import functools

import jax
import jax.numpy as jnp
from jax import lax
from jax.experimental import pallas as pl
from jax.experimental.pallas import tpu as pltpu
from jax.sharding import PartitionSpec as P

F32 = jnp.float32
BF16 = jnp.bfloat16
AXES = ("gx", "gy")
NZ, CX, CY = 20, 8, 128
ROWS = NZ * CX
STEP = 16
CHUNKS = ROWS // STEP
PEERS = 128
CAP = 8


def lanes(shape):
    return lax.broadcasted_iota(jnp.int32, shape, 1)


def subs(shape):
    return lax.broadcasted_iota(jnp.int32, shape, 0)


def split3(x):
    high = x.astype(BF16)
    rest = x - high.astype(F32)
    mid = rest.astype(BF16)
    low = (rest - mid.astype(F32)).astype(BF16)
    return high, mid, low


def pick_rows(onehot, x):
    high, mid, low = split3(x)

    def dot(part):
        return lax.dot_general(onehot, part, (((1,), (0,)), ((), ())), preferred_element_type=F32)

    return (dot(low) + dot(mid)) + dot(high)


def is_slot(lane):
    return (lane & 63) >= 60


def slot_values(rows_of, start, first):
    lane = lanes((PEERS, CY))
    number = (lane & 3) + jnp.where(lane >= 64, 4, 0)
    picked = pick_rows(rows_of, first)
    window = jnp.take_along_axis(picked, (start + number) & (CY - 1), axis=1)
    return jnp.where(is_slot(lane), window, 0.0)


def into_cells(rows_to, start, flows):
    number = (lanes((PEERS, CY)) - start) & (CY - 1)
    place = jnp.where(number < 4, number + 60, jnp.where(number < CAP, number + 120, 0))
    return pick_rows(rows_to, jnp.take_along_axis(flows, place, axis=1))


def segment_values(state, index):
    low = index & 127
    first = jnp.take_along_axis(jnp.broadcast_to(state[0:1], (8, 128)), low, axis=1)
    second = jnp.take_along_axis(jnp.broadcast_to(state[1:2], (8, 128)), low, axis=1)
    return jnp.where(index >= 128, second, first)


def into_segments(values, index, table):
    parts = [part.astype(F32) for part in split3(values)]
    sub = subs((16, 128))
    upper = (index >= 128).astype(jnp.int32)
    tiles = []
    for k in range(CAP):
        row = [jnp.broadcast_to(part[k : k + 1], (16, 128)) for part in parts]
        mine = jnp.broadcast_to(upper[k : k + 1], (16, 128)) == (sub & 1)
        tile = jnp.where(sub < 2, row[0], jnp.where(sub < 4, row[1], row[2]))
        tiles.append(jnp.where(mine & (sub < 6), tile, 0.0).astype(BF16))
    left = jnp.concatenate(tiles, axis=1)
    out = lax.dot_general(left, table, (((1,), (1,)), ((), ())), preferred_element_type=F32)[:8]
    total = (pltpu.roll(out, 4, 0) + pltpu.roll(out, 6, 0)) + out
    return jnp.where(subs((8, 128)) < 2, total, 0.0)


def previous(state):
    moved = pltpu.roll(state, 1, 1)
    return jnp.where(lanes((8, 128)) == 0, pltpu.roll(moved, 1, 0), moved)


def following(state):
    moved = pltpu.roll(state, 127, 1)
    return jnp.where(lanes((8, 128)) == 127, pltpu.roll(moved, 7, 0), moved)


def to_columns(values):
    gap = jnp.zeros((60, 128), F32)
    return jnp.concatenate([gap, values[0:4], gap, values[4:8]], axis=0).T


def to_rows(columns):
    turned = columns.T
    return jnp.concatenate([turned[60:64], turned[124:128]], axis=0)


def field(n):
    return pl.ds(n, PEERS, stride=8)


def block(n):
    return pl.ds(n, PEERS, stride=4)


def halves(x):
    high = x.astype(BF16).astype(F32)
    return high, x - high


def chunk(t):
    return pl.ds(t * STEP, STEP)


def me():
    return lax.axis_index("gx") * 16 + lax.axis_index("gy")


def peer_rows(shift, pitch=4):
    return pl.ds(pitch * ((me() + shift) & (PEERS - 1)), 4)


def tile_to_rows(tile, pad):
    pad[0:8] = tile
    pad[8:16] = pltpu.roll(tile, 64, 1)
    even = pad[pl.ds(0, 4, stride=2), :]
    odd = pad[pl.ds(9, 4, stride=2), :]
    return jnp.where(lanes((4, 128)) < 64, even, odd)


def rows_to_tile(four, pad):
    pad[0:4] = four
    pad[8:16] = pltpu.roll(pad[0:8], 64, 1)
    low, high = pad[0:4], pad[8:12]
    pad[pl.ds(0, 4, stride=2), :] = low
    pad[pl.ds(1, 4, stride=2), :] = high
    return pad[0:8]


def mix(matrix, rows, vector):
    entry = [matrix[n, rows, :].astype(F32) for n in range(9)]
    x, y, z = vector
    return [entry[3 * n] * x + entry[3 * n + 1] * y + entry[3 * n + 2] * z for n in range(3)]


def solve(diag, rows, vector):
    a, b, c, d, e, f, g, h, i = [diag[n, rows, :].astype(F32) for n in range(9)]
    x, y, z = vector
    p, q, s = e * i - f * h, f * g - d * i, d * h - e * g
    scale = 1.0 / (a * p + b * q + c * s)
    return [
        (p * x + (c * h - b * i) * y + (b * f - c * e) * z) * scale,
        (q * x + (a * i - c * g) * y + (c * d - a * f) * z) * scale,
        (s * x + (b * g - a * h) * y + (a * e - b * d) * z) * scale,
    ]


def borders(values, mobility, trans, weighted, along, t):
    rows = chunk(t)
    tx = trans[0, rows, :].astype(F32)
    for n, value in enumerate(mix(mobility, rows, values)):
        weighted[n, rows, :] = value
        along[pl.ds(n * ROWS + t * STEP, STEP), :] = tx * value


def send_borders(trans, weighted, along, toward_low, toward_high, message, pad, pitch=4):
    toward_low[...] = along[pl.ds(0, 3 * NZ, stride=CX), :]
    toward_high[...] = along[pl.ds(CX - 1, 3 * NZ, stride=CX), :]
    small = lanes((8, 128))
    high = jnp.zeros((8, 128), F32)
    low = jnp.zeros((8, 128), F32)
    for t in range(CHUNKS):
        ty = trans[1, chunk(t), :].astype(F32)
        for n in range(3):
            py = ty * weighted[n, chunk(t), :]
            for half in range(2):
                j = n * NZ + 2 * t + half
                moved = pltpu.roll(py[8 * half : 8 * half + 8], j + 1, 1)
                high = jnp.where(small == j, moved, high)
                low = jnp.where(small == j + 1, moved, low)
    low = pltpu.roll(low, 127, 1)
    mine = is_slot(lanes((4, 128)))
    for shift, tile in ((1, high), (-1, low)):
        rows = peer_rows(shift, pitch)
        packed = tile_to_rows(tile, pad)
        message[rows, :] = jnp.where(mine, message[rows, :], packed)


def interior(weighted, trans, near):
    lane = lanes((STEP, 128))
    sub = subs((STEP, 128)) & 7
    zero = jnp.zeros((8, 128), F32)
    up = [trans[2, chunk(t), :].astype(F32) for t in range(CHUNKS)]
    for t in range(CHUNKS):
        rows = chunk(t)
        tx, ty = [trans[n, rows, :].astype(F32) for n in range(2)]
        tz = up[t]
        for n in range(3):
            value = weighted[n, rows, :]
            px, py = tx * value, ty * value
            nx = jnp.where(sub == 0, 0.0, pltpu.roll(px, 1, 0)) + jnp.where(
                sub == 7, 0.0, pltpu.roll(px, STEP - 1, 0)
            )
            ny = jnp.where(lane == 0, 0.0, pltpu.roll(py, 1, 1)) + jnp.where(
                lane == 127, 0.0, pltpu.roll(py, 127, 1)
            )
            pz = tz * value
            below = zero
            above = zero
            if t:
                below = up[t - 1][8:16] * weighted[n, pl.ds(t * STEP - 8, 8), :]
            if t + 1 < CHUNKS:
                above = up[t + 1][0:8] * weighted[n, pl.ds(t * STEP + STEP, 8), :]
            nz = jnp.concatenate([below + pz[8:16], pz[0:8] + above], axis=0)
            near[n, rows, :] = tx * nx + ty * ny + tz * nz


def cell_setup(rhs_in, diag_in, mobility_in, trans_in, cells_in, pi_in, index_in, parent_in,
               across_in, source_in,
               rows_of, rows_to, start, weight, slots, fixed,
               weighted, toward_low, toward_high, message, along, pad, forward, own,
               rhs, diag, mobility, trans, cells, pi, index, parent, across, source, sems):
    pairs = ((cells_in, cells), (pi_in, pi), (index_in, index), (parent_in, parent),
             (across_in, across), (source_in, source), (rhs_in, rhs), (diag_in, diag),
             (mobility_in, mobility), (trans_in, trans))
    copies = [pltpu.make_async_copy(a, b, sems.at[n]) for n, (a, b) in enumerate(pairs)]
    for copy in copies:
        copy.start()
    for copy in copies[:6]:
        copy.wait()
    zeros = jnp.zeros((6, 128), F32)
    linked = jnp.concatenate([(parent[...] >= 0).astype(F32), zeros], axis=0)
    moving = jnp.concatenate([across[...], zeros], axis=0)
    given = jnp.concatenate([source[...], zeros], axis=0)
    partial = moving + following(linked * moving)
    fixed[0] = linked
    fixed[1] = moving
    fixed[2] = given
    fixed[3] = partial
    number = index[...]
    own[field(1), :], own[field(3), :] = halves(to_columns(segment_values(given, number)))
    own[field(4), :], own[field(5), :] = halves(to_columns(segment_values(partial, number)))
    own[field(6), :] = jnp.zeros((PEERS, 128), F32)
    own[field(7), :] = jnp.zeros((PEERS, 128), F32)
    base = cells[0:1, :]
    row = lax.shift_right_logical(base, 7)
    live = pi[...]
    gap = jnp.zeros((44, 128), F32)
    info = jnp.concatenate(
        [jnp.broadcast_to(row.astype(F32), (8, 128)),
         jnp.broadcast_to((base & 127).astype(F32), (8, 128)),
         gap, live[0:4], gap, jnp.zeros((16, 128), F32), live[4:8]],
        axis=0,
    ).T
    rows_to[...] = (subs((ROWS, PEERS)) == jnp.broadcast_to(row, (ROWS, PEERS))).astype(F32).astype(BF16)
    row_column = jnp.broadcast_to(info[:, 0:1], (PEERS, ROWS)).astype(jnp.int32)
    rows_of[...] = (lanes((PEERS, ROWS)) == row_column).astype(F32).astype(BF16)
    begin = jnp.broadcast_to(info[:, 8:9], (PEERS, 128)).astype(jnp.int32)
    start[...] = begin
    weights = jnp.where(is_slot(lanes((PEERS, 128))), info, 0.0)
    weight[...] = weights
    high, low = halves(live)
    common = jnp.concatenate([low, number.astype(F32)], axis=0).astype(BF16)
    for d in range(PEERS):
        message[pl.ds(32 * d + 16, 16), :] = common
    for copy in copies[6:8]:
        copy.wait()
    for t in range(CHUNKS):
        rows = chunk(t)
        values = solve(diag, rows, [rhs[n, rows, :] for n in range(3)])
        forward[rows, :] = values[0]
        for n in range(3):
            weighted[n, rows, :] = values[n]
    values = slot_values(rows_of[...], begin, forward[...])
    slots[...] = values
    own[field(0), :], own[field(2), :] = halves(values)
    for copy in copies[8:]:
        copy.wait()
    for t in range(CHUNKS):
        values = [weighted[n, chunk(t), :] for n in range(3)]
        borders(values, mobility, trans, weighted, along, t)
    send_borders(trans, weighted, along, toward_low, toward_high, own, pad, 8)
    for d in range(PEERS):
        both = jnp.concatenate([own[pl.ds(8 * d, 8), :], high], axis=0)
        message[pl.ds(32 * d, 16), :] = both.astype(BF16)


def well_tables(index, table):
    low = index[...] & 127
    for k in range(CAP):
        hit = subs((128, 128)) == jnp.broadcast_to(low[k : k + 1], (128, 128))
        table[:, 128 * k : 128 * (k + 1)] = hit.astype(F32).astype(BF16)


def well_setup(arrived, index, table, fixed, message, weight, state, at_slots, diagonal,
               wide, turned):
    wide[...] = arrived[...].astype(F32)

    def part(n):
        return wide[pl.ds(n, PEERS, stride=32), :]

    lane = lanes((PEERS, 128))
    mine = lane == me()
    for k in range(CAP):
        turned[k] = (part(8 + k) + part(16 + k)).T
    total = part(4) + part(5)
    for k in range(CAP):
        target = jnp.sum(jnp.where(mine, part(24 + k), 0.0), axis=1, keepdims=True)
        target = jnp.broadcast_to(target, (PEERS, 128))
        found = jnp.zeros((PEERS, 128), F32)
        for m in range(CAP):
            found += jnp.where(part(24 + m) == target, turned[m], 0.0)
        place = 60 + k if k < 4 else 120 + k
        total += jnp.where(lane == place, jnp.sum(found, axis=1, keepdims=True), 0.0)
    slot = is_slot(lane)
    pressures = (part(1) + part(3)) / jnp.where(slot, total, 1.0)
    message[block(0), :] = jnp.where(slot, part(0) + part(2), part(0))
    message[block(1), :] = jnp.where(slot, pressures, part(1))
    message[block(2), :] = part(2)
    message[block(3), :] = part(3)
    pi = jnp.concatenate([turned[k, pl.ds(me(), 1), :] for k in range(CAP)], axis=0)
    weight[...] = pi
    number = index[...]
    total = fixed[3] + into_segments(pi, number, table[...])
    total = jnp.where(subs((8, 128)) < 2, total, 1.0)
    diagonal[...] = total
    now = fixed[2] / total
    state[...] = now
    at_slots[...] = segment_values(now, number)


def ratio(sums, place):
    total = jnp.sum(sums, axis=0, keepdims=True)
    lane = lanes((1, 128))
    numer = jnp.sum(jnp.where(lane == place, total, 0.0), axis=1, keepdims=True)
    denom = jnp.sum(jnp.where(lane == place + 1, total, 0.0), axis=1, keepdims=True)
    return numer / denom


def spread_pair(two):
    return jnp.concatenate(
        [jnp.broadcast_to(two[h : h + 1], (8, 128)) for h in range(2)], axis=0
    )


STEADY = ("rhs", "diag", "mobility", "trans", "rows_of", "rows_to", "start", "weight",
          "own_weight", "table", "index", "fixed", "diagonal")
MOVING = ("arrived", "near", "from_low", "from_high", "slots", "at_slots", "state")
NEXT = ("weighted", "toward_low", "toward_high", "message", "slots", "at_slots", "state")
MORE_IN = {
    "plain": (), "keep": (), "last": ("field",), "after": (),
    "final": ("field", "change", "seg_change", "omega"),
}
NARROW = ("plain", "keep", "after")
MORE_OUT = {
    "plain": (), "keep": ("field",), "last": ("change", "seg_change"),
    "after": ("omega",), "final": (),
}


def results_of(kind):
    return ("message",) if kind == "final" else NEXT + MORE_OUT[kind]


def sweep(kind, *refs):
    take = iter(refs)
    now = {name: next(take) for name in MOVING}
    fixed = {name: next(take) for name in STEADY}
    extra = {name: next(take) for name in MORE_IN[kind]}
    out = {name: next(take) for name in results_of(kind)}
    along, pad, forward, wide = take
    narrow = kind in NARROW
    weighted = out.get("weighted")
    final = kind == "final"
    gx, gy = lax.axis_index("gx"), lax.axis_index("gy")

    arrived = now["arrived"]
    if arrived.dtype == BF16:
        wide[...] = arrived[...].astype(F32)
        arrived = wide
        heads = arrived[block(0), :] + arrived[block(2), :]
        pressures = arrived[block(1), :] + arrived[block(3), :]
    else:
        heads, pressures = arrived[block(0), :], arrived[block(1), :]
    pull = fixed["weight"][...] * (now["slots"][...] - pressures)
    perforated = into_cells(fixed["rows_to"][...], fixed["start"][...], pull)

    side_low = rows_to_tile(arrived[peer_rows(-1), :], pad)
    side_high = rows_to_tile(arrived[peer_rows(1), :], pad)
    side_low = jnp.where(gy == 0, 0.0, side_low)
    side_high = jnp.where(gy == lax.axis_size("gy") - 1, 0.0, side_high)
    small = lanes((8, 128))
    ahead = pltpu.roll(side_high, 127, 1)
    sides = [jnp.where((small & 1) == odd, side_low, ahead) for odd in range(2)]
    open_low, open_high = gx > 0, gx < lax.axis_size("gx") - 1

    state = now["state"][...]
    linked, across, source = [fixed["fixed"][n] for n in range(3)]
    push = fixed["own_weight"][...] * (to_rows(heads) - now["at_slots"][...])
    number = fixed["index"][...]
    inflow = into_segments(push, number, fixed["table"][...])
    flux = across * (state - linked * previous(state))
    seg_res = source - flux + following(linked * flux) + inflow

    lane = lanes((STEP, 128))
    sub = subs((STEP, 128)) & 7
    numer = jnp.zeros((STEP, 128), F32)
    denom = jnp.zeros((STEP, 128), F32)
    if final:
        omega = extra["omega"][0:1, 0:1]
    for t in range(CHUNKS):
        rows = chunk(t)
        tx, ty = [fixed["trans"][n, rows, :].astype(F32) for n in range(2)]
        tx = jnp.where(
            sub == 0, jnp.where(open_low, tx, 0.0),
            jnp.where((sub == 7) & open_high, tx, 0.0),
        )
        ty = jnp.where((lane == 0) | (lane == 127), ty, 0.0)
        terms = []
        for n in range(3):
            j = n * NZ + 2 * t
            low, high = now["from_low"][j : j + 2, :], now["from_high"][j : j + 2, :]
            nx = jnp.where(sub == 0, spread_pair(low), spread_pair(high))
            ny = jnp.concatenate(
                [pltpu.roll(sides[(j + h) & 1], (128 - j - h) % 128, 1) for h in range(2)], axis=0
            )
            share = fixed["mobility"][3 * n, rows, :].astype(F32)
            value = now["near"][n, rows, :] + tx * nx + ty * ny
            terms.append(value - share * perforated[t * STEP : (t + 1) * STEP])
        if kind in ("last", "final"):
            own = mix(fixed["diag"], rows, [extra["field"][n, rows, :] for n in range(3)])
            for n in range(3):
                change = own[n] - terms[n]
                before = fixed["rhs"][n, rows, :]
                if final:
                    kept = extra["change"][n, rows, :]
                    before = before - omega * kept
                    change = kept + omega * (change - 2.0 * kept)
                else:
                    out["change"][n, rows, :] = change
                numer += before * change
                denom += change * change
        if not final:
            total = [fixed["rhs"][n, rows, :] + terms[n] for n in range(3)]
            values = solve(fixed["diag"], rows, total)
            forward[rows, :] = values[0]
            if kind == "keep":
                for n in range(3):
                    out["field"][n, rows, :] = values[n]
            borders(values, fixed["mobility"], fixed["trans"], weighted, along, t)

    if kind in ("last", "final"):
        before = source
        change = source - seg_res
        if final:
            kept = extra["seg_change"][...]
            before = source - omega * kept
            change = kept + omega * (change - 2.0 * kept)
        else:
            out["seg_change"][...] = change
        above = jnp.sum(numer, keepdims=True) + jnp.sum(before * change, keepdims=True)
        below = jnp.sum(denom, keepdims=True) + jnp.sum(change * change, keepdims=True)
        place = lanes((PEERS, 128))
        sums = jnp.where(place == 60, above, jnp.where(place == 61, below, 0.0))
        if final:
            out["message"][...] = sums
            return
    if kind == "after":
        out["omega"][...] = jnp.broadcast_to(ratio(arrived[block(2), :], 60), (8, 128))
    message = wide if narrow else out["message"]
    advanced = state + seg_res / fixed["diagonal"][...]
    out["state"][...] = advanced
    values = segment_values(advanced, number)
    out["at_slots"][...] = values
    cells = slot_values(fixed["rows_of"][...], fixed["start"][...], forward[...])
    out["slots"][...] = cells
    columns = to_columns(values)
    if narrow:
        message[block(0), :], message[block(2), :] = halves(cells)
        message[block(1), :], message[block(3), :] = halves(columns)
    else:
        message[block(0), :] = cells
        message[block(1), :] = columns
        message[block(2), :] = sums
        message[block(3), :] = jnp.zeros((PEERS, 128), F32)
    send_borders(
        fixed["trans"], weighted, along, out["toward_low"], out["toward_high"], message, pad
    )
    if narrow:
        out["message"][...] = message[...].astype(BF16)


def finish(arrived, omega, field_one, field_two, state_one, state_two, cells, segments):
    first = omega[0:1, 0:1]
    second = ratio(arrived[...], 60)

    def blend(one, two):
        kept = first * one
        return kept + second * (one + first * (two - one) - kept)

    for n in range(3):
        for t in range(CHUNKS):
            rows = chunk(t)
            cells[n, rows, :] = blend(field_one[n, rows, :], field_two[n, rows, :])
    segments[...] = blend(state_one[0:2], state_two[0:2])


CELLS = ((3, ROWS, 128), F32)
PAIRS = ((PEERS, 128), F32)
MESSAGE = ((4 * PEERS, 128), F32)
TILE = ((8, 128), F32)
EDGE = ((3 * NZ, 128), F32)
SHAPES = {
    "weighted": CELLS, "toward_low": EDGE, "toward_high": EDGE, "message": MESSAGE, "slots": PAIRS,
    "at_slots": TILE, "state": TILE, "omega": TILE, "field": CELLS, "change": CELLS,
    "seg_change": TILE,
}


def shape_of(kind, name):
    if name != "message":
        return SHAPES[name]
    if kind == "final":
        return PAIRS
    return (MESSAGE[0], BF16) if kind in NARROW else MESSAGE


SCRATCH = (
    pltpu.VMEM((3 * ROWS, 128), F32),
    pltpu.VMEM((16, 128), F32),
    pltpu.VMEM((ROWS, 128), F32),
)


def call(body, outs, args, scratch=(), name=None, space=pltpu.VMEM, grant=24 * 1024 * 1024):
    moved = sum(a.size * a.dtype.itemsize for a in args)
    return pl.pallas_call(
        body,
        out_shape=[jax.ShapeDtypeStruct(*out) for out in outs],
        in_specs=[pl.BlockSpec(memory_space=space)] * len(args),
        out_specs=[pl.BlockSpec(memory_space=pltpu.VMEM)] * len(outs),
        scratch_shapes=list(scratch),
        compiler_params=pltpu.CompilerParams(vmem_limit_bytes=grant),
        cost_estimate=pl.CostEstimate(flops=4_000_000, bytes_accessed=moved, transcendentals=0),
        name=name,
    )(*args)


def exchange(message):
    return lax.all_to_all(message, AXES, split_axis=0, concat_axis=0, tiled=True)


def neighbours(toward_low, toward_high):
    count = lax.axis_size("gx")
    up = [(i, (i + 1) % count) for i in range(count)]
    down = [(b, a) for a, b in up]
    return {
        "from_low": lax.ppermute(toward_high, "gx", up),
        "from_high": lax.ppermute(toward_low, "gx", down),
    }


def on_device(
    rhs, diag_block, mobility, trans, perf_cell, perf_pi, perf_seg, seg_parent, seg_trans, seg_rhs
):
    rhs = rhs.reshape(3, ROWS, 128)
    diag = diag_block.reshape(9, ROWS, 128)
    mobility = mobility.reshape(9, ROWS, 128)
    trans = trans.reshape(3, ROWS, 128)
    index = perf_seg[0]

    fixed = {"rhs": rhs, "diag": diag, "mobility": mobility, "trans": trans, "index": index}
    inputs = [rhs, diag, mobility, trans, perf_cell[0], perf_pi[0], index]
    inputs += [a.reshape(2, 128) for a in (seg_parent, seg_trans, seg_rhs)]
    (rows_of, rows_to, start, weight, slots, constants, weighted, toward_low, toward_high,
     message) = call(
        cell_setup,
        [((PEERS, ROWS), BF16), ((ROWS, PEERS), BF16),
         ((PEERS, 128), jnp.int32), PAIRS, PAIRS, ((4, 8, 128), F32), CELLS, EDGE, EDGE,
         ((32 * PEERS, 128), BF16)],
        inputs,
        SCRATCH + (pltpu.VMEM((8 * PEERS, 128), F32),)
        + tuple(pltpu.VMEM(a.shape, a.dtype) for a in inputs) + (pltpu.SemaphoreType.DMA((10,)),),
        name="cell_setup",
        space=pltpu.HBM,
        grant=64 * 1024 * 1024 - 256 * 1024,
    )
    arrived = exchange(message)

    def inside(weighted):
        return call(interior, [CELLS], [weighted, trans], name="interior")[0]

    (table,) = call(well_tables, [((128, CAP * 128), BF16)], [index], name="well_tables")
    fixed.update(rows_of=rows_of, rows_to=rows_to, start=start, weight=weight)
    now = {"near": inside(weighted), "slots": slots}
    now.update(neighbours(toward_low, toward_high))
    now["arrived"], own_weight, state, at_slots, diagonal = call(
        well_setup,
        [MESSAGE, TILE, TILE, TILE, TILE],
        [arrived, index, table, constants],
        [pltpu.VMEM((32 * PEERS, 128), F32), pltpu.VMEM((CAP, PEERS, 128), F32)],
        name="well_setup",
    )
    fixed.update(own_weight=own_weight, table=table, fixed=constants, diagonal=diagonal)
    now.update(at_slots=at_slots, state=state)
    saved = {}

    def advance(kind, now):
        args = [now[name] for name in MOVING]
        args += [fixed[name] for name in STEADY]
        args += [saved[name] for name in MORE_IN[kind]]
        names = results_of(kind)
        out = call(
            functools.partial(sweep, kind),
            [shape_of(kind, name) for name in names],
            args,
            SCRATCH + (pltpu.VMEM(*MESSAGE),),
            name="sweep_" + kind,
        )
        out = dict(zip(names, out))
        out["arrived"] = exchange(out.pop("message"))
        if kind != "final":
            out.update(neighbours(out.pop("toward_low"), out.pop("toward_high")))
            out["near"] = inside(out.pop("weighted"))
        return out

    now = advance("plain", now)
    now = advance("plain", now)
    one = advance("keep", now)
    saved["field"] = one["field"]
    now = advance("last", one)
    saved.update(change=now["change"], seg_change=now["seg_change"])
    now = advance("after", now)
    saved["omega"] = now["omega"]
    now = advance("plain", now)
    two = advance("keep", now)
    saved["field"] = two["field"]
    sums = advance("final", two)
    cells, segments = call(
        finish,
        [CELLS, ((2, 128), F32)],
        [sums["arrived"], saved["omega"], one["field"], two["field"], one["state"], two["state"]],
        name="finish",
    )
    return cells.reshape(3, NZ, CX, CY), segments.reshape(256)


def solution(mesh):
    grid = P(None, None, "gx", "gy")
    pairs = P(AXES, None, None)
    flat = P(AXES)
    return jax.shard_map(
        on_device,
        mesh=mesh,
        in_specs=(grid, grid, grid, grid, pairs, pairs, pairs, flat, flat, flat),
        out_specs=(grid, flat),
        check_vma=False,
    )
```

```python
import functools

import jax
import jax.numpy as jnp
from jax import lax
from jax.experimental import pallas as pl
from jax.experimental.pallas import tpu as pltpu
from jax.sharding import PartitionSpec as P

F32 = jnp.float32
BF16 = jnp.bfloat16
AXES = ("gx", "gy")
NZ, CX, CY = 20, 8, 128
ROWS = NZ * CX
STEP = 16
CHUNKS = ROWS // STEP
PEERS = 128
CAP = 8


def lanes(shape):
    return lax.broadcasted_iota(jnp.int32, shape, 1)


def subs(shape):
    return lax.broadcasted_iota(jnp.int32, shape, 0)


def split3(x):
    high = x.astype(BF16)
    rest = x - high.astype(F32)
    mid = rest.astype(BF16)
    low = (rest - mid.astype(F32)).astype(BF16)
    return high, mid, low


def pick_rows(onehot, x):
    high, mid, low = split3(x)

    def dot(part):
        return lax.dot_general(onehot, part, (((1,), (0,)), ((), ())), preferred_element_type=F32)

    return (dot(low) + dot(mid)) + dot(high)


def is_slot(lane):
    return (lane & 63) >= 60


def slot_values(rows_of, start, first):
    lane = lanes((PEERS, CY))
    number = (lane & 3) + jnp.where(lane >= 64, 4, 0)
    picked = pick_rows(rows_of, first)
    window = jnp.take_along_axis(picked, (start + number) & (CY - 1), axis=1)
    return jnp.where(is_slot(lane), window, 0.0)


def into_cells(rows_to, start, flows):
    number = (lanes((PEERS, CY)) - start) & (CY - 1)
    place = jnp.where(number < 4, number + 60, jnp.where(number < CAP, number + 120, 0))
    return pick_rows(rows_to, jnp.take_along_axis(flows, place, axis=1))


def segment_values(state, index):
    low = index & 127
    first = jnp.take_along_axis(jnp.broadcast_to(state[0:1], (8, 128)), low, axis=1)
    second = jnp.take_along_axis(jnp.broadcast_to(state[1:2], (8, 128)), low, axis=1)
    return jnp.where(index >= 128, second, first)


def into_segments(values, index, table):
    parts = [part.astype(F32) for part in split3(values)]
    sub = subs((16, 128))
    upper = (index >= 128).astype(jnp.int32)
    tiles = []
    for k in range(CAP):
        row = [jnp.broadcast_to(part[k : k + 1], (16, 128)) for part in parts]
        mine = jnp.broadcast_to(upper[k : k + 1], (16, 128)) == (sub & 1)
        tile = jnp.where(sub < 2, row[0], jnp.where(sub < 4, row[1], row[2]))
        tiles.append(jnp.where(mine & (sub < 6), tile, 0.0).astype(BF16))
    left = jnp.concatenate(tiles, axis=1)
    out = lax.dot_general(left, table, (((1,), (1,)), ((), ())), preferred_element_type=F32)[:8]
    total = (pltpu.roll(out, 4, 0) + pltpu.roll(out, 6, 0)) + out
    return jnp.where(subs((8, 128)) < 2, total, 0.0)


def previous(state):
    moved = pltpu.roll(state, 1, 1)
    return jnp.where(lanes((8, 128)) == 0, pltpu.roll(moved, 1, 0), moved)


def following(state):
    moved = pltpu.roll(state, 127, 1)
    return jnp.where(lanes((8, 128)) == 127, pltpu.roll(moved, 7, 0), moved)


def to_columns(values):
    gap = jnp.zeros((60, 128), F32)
    return jnp.concatenate([gap, values[0:4], gap, values[4:8]], axis=0).T


def to_rows(columns):
    turned = columns.T
    return jnp.concatenate([turned[60:64], turned[124:128]], axis=0)


def field(n):
    return pl.ds(n, PEERS, stride=8)


def block(n):
    return pl.ds(n, PEERS, stride=4)


def halves(x):
    high = x.astype(BF16).astype(F32)
    return high, x - high


def chunk(t):
    return pl.ds(t * STEP, STEP)


def me():
    return lax.axis_index("gx") * 16 + lax.axis_index("gy")


def peer_rows(shift, pitch=4):
    return pl.ds(pitch * ((me() + shift) & (PEERS - 1)), 4)


def tile_to_rows(tile, pad):
    pad[0:8] = tile
    pad[8:16] = pltpu.roll(tile, 64, 1)
    even = pad[pl.ds(0, 4, stride=2), :]
    odd = pad[pl.ds(9, 4, stride=2), :]
    return jnp.where(lanes((4, 128)) < 64, even, odd)


def rows_to_tile(four, pad):
    pad[0:4] = four
    pad[8:16] = pltpu.roll(pad[0:8], 64, 1)
    low, high = pad[0:4], pad[8:12]
    pad[pl.ds(0, 4, stride=2), :] = low
    pad[pl.ds(1, 4, stride=2), :] = high
    return pad[0:8]


def mix(matrix, rows, vector):
    entry = [matrix[n, rows, :].astype(F32) for n in range(9)]
    x, y, z = vector
    return [entry[3 * n] * x + entry[3 * n + 1] * y + entry[3 * n + 2] * z for n in range(3)]


def solve(diag, rows, vector):
    a, b, c, d, e, f, g, h, i = [diag[n, rows, :].astype(F32) for n in range(9)]
    x, y, z = vector
    p, q, s = e * i - f * h, f * g - d * i, d * h - e * g
    scale = 1.0 / (a * p + b * q + c * s)
    return [
        (p * x + (c * h - b * i) * y + (b * f - c * e) * z) * scale,
        (q * x + (a * i - c * g) * y + (c * d - a * f) * z) * scale,
        (s * x + (b * g - a * h) * y + (a * e - b * d) * z) * scale,
    ]


def borders(values, mobility, trans, weighted, along, t):
    rows = chunk(t)
    tx = trans[0, rows, :].astype(F32)
    for n, value in enumerate(mix(mobility, rows, values)):
        weighted[n, rows, :] = value
        along[pl.ds(n * ROWS + t * STEP, STEP), :] = tx * value


def send_borders(trans, weighted, along, toward_low, toward_high, message, pad, pitch=4):
    toward_low[...] = along[pl.ds(0, 3 * NZ, stride=CX), :]
    toward_high[...] = along[pl.ds(CX - 1, 3 * NZ, stride=CX), :]
    small = lanes((8, 128))
    high = jnp.zeros((8, 128), F32)
    low = jnp.zeros((8, 128), F32)
    for t in range(CHUNKS):
        ty = trans[1, chunk(t), :].astype(F32)
        for n in range(3):
            py = ty * weighted[n, chunk(t), :]
            for half in range(2):
                j = n * NZ + 2 * t + half
                moved = pltpu.roll(py[8 * half : 8 * half + 8], j + 1, 1)
                high = jnp.where(small == j, moved, high)
                low = jnp.where(small == j + 1, moved, low)
    low = pltpu.roll(low, 127, 1)
    mine = is_slot(lanes((4, 128)))
    for shift, tile in ((1, high), (-1, low)):
        rows = peer_rows(shift, pitch)
        packed = tile_to_rows(tile, pad)
        message[rows, :] = jnp.where(mine, message[rows, :], packed)


def interior(weighted, trans, near):
    lane = lanes((STEP, 128))
    sub = subs((STEP, 128)) & 7
    zero = jnp.zeros((8, 128), F32)
    up = [trans[2, chunk(t), :].astype(F32) for t in range(CHUNKS)]
    for t in range(CHUNKS):
        rows = chunk(t)
        tx, ty = [trans[n, rows, :].astype(F32) for n in range(2)]
        tz = up[t]
        for n in range(3):
            value = weighted[n, rows, :]
            px, py = tx * value, ty * value
            nx = jnp.where(sub == 0, 0.0, pltpu.roll(px, 1, 0)) + jnp.where(
                sub == 7, 0.0, pltpu.roll(px, STEP - 1, 0)
            )
            ny = jnp.where(lane == 0, 0.0, pltpu.roll(py, 1, 1)) + jnp.where(
                lane == 127, 0.0, pltpu.roll(py, 127, 1)
            )
            pz = tz * value
            below = zero
            above = zero
            if t:
                below = up[t - 1][8:16] * weighted[n, pl.ds(t * STEP - 8, 8), :]
            if t + 1 < CHUNKS:
                above = up[t + 1][0:8] * weighted[n, pl.ds(t * STEP + STEP, 8), :]
            nz = jnp.concatenate([below + pz[8:16], pz[0:8] + above], axis=0)
            near[n, rows, :] = tx * nx + ty * ny + tz * nz


def cell_setup(rhs_in, diag_in, mobility_in, trans_in, cells_in, pi_in, index_in, parent_in,
               across_in, source_in,
               rows_of, rows_to, start, weight, slots, fixed,
               weighted, toward_low, toward_high, message, along, pad, forward, own,
               rhs, diag, mobility, trans, cells, pi, index, parent, across, source, sems):
    pairs = ((cells_in, cells), (pi_in, pi), (index_in, index), (parent_in, parent),
             (across_in, across), (source_in, source), (rhs_in, rhs), (diag_in, diag),
             (mobility_in, mobility), (trans_in, trans))
    copies = [pltpu.make_async_copy(a, b, sems.at[n]) for n, (a, b) in enumerate(pairs)]
    for copy in copies:
        copy.start()
    for copy in copies[:6]:
        copy.wait()
    zeros = jnp.zeros((6, 128), F32)
    linked = jnp.concatenate([(parent[...] >= 0).astype(F32), zeros], axis=0)
    moving = jnp.concatenate([across[...], zeros], axis=0)
    given = jnp.concatenate([source[...], zeros], axis=0)
    partial = moving + following(linked * moving)
    fixed[0] = linked
    fixed[1] = moving
    fixed[2] = given
    fixed[3] = partial
    number = index[...]
    own[field(1), :], own[field(3), :] = halves(to_columns(segment_values(given, number)))
    own[field(4), :], own[field(5), :] = halves(to_columns(segment_values(partial, number)))
    own[field(7), :] = jnp.zeros((PEERS, 128), F32)
    base = cells[0:1, :]
    row = lax.shift_right_logical(base, 7)
    live = pi[...]
    gap = jnp.zeros((44, 128), F32)
    info = jnp.concatenate(
        [jnp.broadcast_to(row.astype(F32), (8, 128)),
         jnp.broadcast_to((base & 127).astype(F32), (8, 128)),
         gap, live[0:4], gap, jnp.zeros((16, 128), F32), live[4:8]],
        axis=0,
    ).T
    rows_to[...] = (subs((ROWS, PEERS)) == jnp.broadcast_to(row, (ROWS, PEERS))).astype(F32).astype(BF16)
    row_column = jnp.broadcast_to(info[:, 0:1], (PEERS, ROWS)).astype(jnp.int32)
    rows_of[...] = (lanes((PEERS, ROWS)) == row_column).astype(F32).astype(BF16)
    begin = jnp.broadcast_to(info[:, 8:9], (PEERS, 128)).astype(jnp.int32)
    start[...] = begin
    weights = jnp.where(is_slot(lanes((PEERS, 128))), info, 0.0)
    weight[...] = weights
    own[field(6), :] = halves(weights)[1]
    high = halves(live)[0]
    order = number.astype(F32)
    common = jnp.concatenate([high, order], axis=0).astype(BF16)
    for d in range(0, PEERS, 2):
        message[pl.ds(24 * d + 32, 16), :] = common
    for copy in copies[6:8]:
        copy.wait()
    for t in range(CHUNKS):
        rows = chunk(t)
        values = solve(diag, rows, [rhs[n, rows, :] for n in range(3)])
        forward[rows, :] = values[0]
        for n in range(3):
            weighted[n, rows, :] = values[n]
    values = slot_values(rows_of[...], begin, forward[...])
    slots[...] = values
    own[field(0), :], own[field(2), :] = halves(values)
    for copy in copies[8:]:
        copy.wait()
    for t in range(CHUNKS):
        values = [weighted[n, chunk(t), :] for n in range(3)]
        borders(values, mobility, trans, weighted, along, t)
    send_borders(trans, weighted, along, toward_low, toward_high, own, pad, 8)
    for d in range(0, PEERS, 2):
        two = [own[pl.ds(8 * d, 8), :], high, order, own[pl.ds(8 * d + 8, 8), :]]
        message[pl.ds(24 * d, 32), :] = jnp.concatenate(two, axis=0).astype(BF16)


def well_tables(index, table):
    low = index[...] & 127
    for k in range(CAP):
        hit = subs((128, 128)) == jnp.broadcast_to(low[k : k + 1], (128, 128))
        table[:, 128 * k : 128 * (k + 1)] = hit.astype(F32).astype(BF16)


def well_setup(arrived, index, table, fixed, message, weight, state, at_slots, diagonal,
               wide, turned):
    wide[...] = arrived[...].astype(F32)

    def part(n):
        return wide[pl.ds(n, PEERS, stride=24), :]

    lane = lanes((PEERS, 128))
    mine = lane == me()
    for k in range(CAP):
        turned[k] = part(8 + k).T
    total = part(4) + part(5)
    for k in range(CAP):
        target = jnp.sum(jnp.where(mine, part(16 + k), 0.0), axis=1, keepdims=True)
        target = jnp.broadcast_to(target, (PEERS, 128))
        found = jnp.zeros((PEERS, 128), F32)
        for m in range(CAP):
            found += jnp.where(part(16 + m) == target, turned[m], 0.0)
        place = 60 + k if k < 4 else 120 + k
        total += jnp.where(lane == place, jnp.sum(found, axis=1, keepdims=True), 0.0)
    slot = is_slot(lane)
    pressures = (part(1) + part(3)) / jnp.where(slot, total, 1.0)
    message[block(0), :] = jnp.where(slot, part(0) + part(2), part(0))
    message[block(1), :] = jnp.where(slot, pressures, part(1))
    message[block(2), :] = part(2)
    message[block(3), :] = part(3)
    pi = jnp.concatenate([turned[k, pl.ds(me(), 1), :] for k in range(CAP)], axis=0)
    pi += to_rows(part(6))
    weight[...] = pi
    number = index[...]
    total = fixed[3] + into_segments(pi, number, table[...])
    total = jnp.where(subs((8, 128)) < 2, total, 1.0)
    diagonal[...] = total
    now = fixed[2] / total
    state[...] = now
    at_slots[...] = segment_values(now, number)


def ratio(sums, place):
    total = jnp.sum(sums, axis=0, keepdims=True)
    lane = lanes((1, 128))
    numer = jnp.sum(jnp.where(lane == place, total, 0.0), axis=1, keepdims=True)
    denom = jnp.sum(jnp.where(lane == place + 1, total, 0.0), axis=1, keepdims=True)
    return numer / denom


def spread_pair(two):
    return jnp.concatenate(
        [jnp.broadcast_to(two[h : h + 1], (8, 128)) for h in range(2)], axis=0
    )


STEADY = ("rhs", "diag", "mobility", "trans", "rows_of", "rows_to", "start", "weight",
          "own_weight", "table", "index", "fixed", "diagonal")
MOVING = ("arrived", "near", "from_low", "from_high", "slots", "at_slots", "state")
NEXT = ("weighted", "toward_low", "toward_high", "message", "slots", "at_slots", "state")
MORE_IN = {
    "plain": (), "keep": (), "last": ("field",), "after": (),
    "final": ("field", "change", "seg_change", "omega"),
}
NARROW = ("plain", "keep", "after")
MORE_OUT = {
    "plain": (), "keep": ("field",), "last": ("change", "seg_change"),
    "after": ("omega",), "final": (),
}


def results_of(kind):
    return ("message",) if kind == "final" else NEXT + MORE_OUT[kind]


def sweep(kind, *refs):
    take = iter(refs)
    now = {name: next(take) for name in MOVING}
    fixed = {name: next(take) for name in STEADY}
    extra = {name: next(take) for name in MORE_IN[kind]}
    out = {name: next(take) for name in results_of(kind)}
    along, pad, forward, wide = take
    narrow = kind in NARROW
    weighted = out.get("weighted")
    final = kind == "final"
    gx, gy = lax.axis_index("gx"), lax.axis_index("gy")

    arrived = now["arrived"]
    if arrived.dtype == BF16:
        wide[...] = arrived[...].astype(F32)
        arrived = wide
        heads = arrived[block(0), :] + arrived[block(2), :]
        pressures = arrived[block(1), :] + arrived[block(3), :]
    else:
        heads, pressures = arrived[block(0), :], arrived[block(1), :]
    pull = fixed["weight"][...] * (now["slots"][...] - pressures)
    perforated = into_cells(fixed["rows_to"][...], fixed["start"][...], pull)

    side_low = rows_to_tile(arrived[peer_rows(-1), :], pad)
    side_high = rows_to_tile(arrived[peer_rows(1), :], pad)
    side_low = jnp.where(gy == 0, 0.0, side_low)
    side_high = jnp.where(gy == lax.axis_size("gy") - 1, 0.0, side_high)
    small = lanes((8, 128))
    ahead = pltpu.roll(side_high, 127, 1)
    sides = [jnp.where((small & 1) == odd, side_low, ahead) for odd in range(2)]
    open_low, open_high = gx > 0, gx < lax.axis_size("gx") - 1

    state = now["state"][...]
    linked, across, source = [fixed["fixed"][n] for n in range(3)]
    push = fixed["own_weight"][...] * (to_rows(heads) - now["at_slots"][...])
    number = fixed["index"][...]
    inflow = into_segments(push, number, fixed["table"][...])
    flux = across * (state - linked * previous(state))
    seg_res = source - flux + following(linked * flux) + inflow

    lane = lanes((STEP, 128))
    sub = subs((STEP, 128)) & 7
    numer = jnp.zeros((STEP, 128), F32)
    denom = jnp.zeros((STEP, 128), F32)
    if final:
        omega = extra["omega"][0:1, 0:1]
    for t in range(CHUNKS):
        rows = chunk(t)
        tx, ty = [fixed["trans"][n, rows, :].astype(F32) for n in range(2)]
        tx = jnp.where(
            sub == 0, jnp.where(open_low, tx, 0.0),
            jnp.where((sub == 7) & open_high, tx, 0.0),
        )
        ty = jnp.where((lane == 0) | (lane == 127), ty, 0.0)
        terms = []
        for n in range(3):
            j = n * NZ + 2 * t
            low, high = now["from_low"][j : j + 2, :], now["from_high"][j : j + 2, :]
            nx = jnp.where(sub == 0, spread_pair(low), spread_pair(high))
            ny = jnp.concatenate(
                [pltpu.roll(sides[(j + h) & 1], (128 - j - h) % 128, 1) for h in range(2)], axis=0
            )
            share = fixed["mobility"][3 * n, rows, :].astype(F32)
            value = now["near"][n, rows, :] + tx * nx + ty * ny
            terms.append(value - share * perforated[t * STEP : (t + 1) * STEP])
        if kind in ("last", "final"):
            own = mix(fixed["diag"], rows, [extra["field"][n, rows, :] for n in range(3)])
            for n in range(3):
                change = own[n] - terms[n]
                before = fixed["rhs"][n, rows, :]
                if final:
                    kept = extra["change"][n, rows, :]
                    before = before - omega * kept
                    change = kept + omega * (change - 2.0 * kept)
                else:
                    out["change"][n, rows, :] = change
                numer += before * change
                denom += change * change
        if not final:
            total = [fixed["rhs"][n, rows, :] + terms[n] for n in range(3)]
            values = solve(fixed["diag"], rows, total)
            forward[rows, :] = values[0]
            if kind == "keep":
                for n in range(3):
                    out["field"][n, rows, :] = values[n]
            borders(values, fixed["mobility"], fixed["trans"], weighted, along, t)

    if kind in ("last", "final"):
        before = source
        change = source - seg_res
        if final:
            kept = extra["seg_change"][...]
            before = source - omega * kept
            change = kept + omega * (change - 2.0 * kept)
        else:
            out["seg_change"][...] = change
        above = jnp.sum(numer, keepdims=True) + jnp.sum(before * change, keepdims=True)
        below = jnp.sum(denom, keepdims=True) + jnp.sum(change * change, keepdims=True)
        place = lanes((PEERS, 128))
        sums = jnp.where(place == 60, above, jnp.where(place == 61, below, 0.0))
        if final:
            out["message"][...] = sums
            return
    if kind == "after":
        out["omega"][...] = jnp.broadcast_to(ratio(arrived[block(2), :], 60), (8, 128))
    message = wide if narrow else out["message"]
    advanced = state + seg_res / fixed["diagonal"][...]
    out["state"][...] = advanced
    values = segment_values(advanced, number)
    out["at_slots"][...] = values
    cells = slot_values(fixed["rows_of"][...], fixed["start"][...], forward[...])
    out["slots"][...] = cells
    columns = to_columns(values)
    if narrow:
        message[block(0), :], message[block(2), :] = halves(cells)
        message[block(1), :], message[block(3), :] = halves(columns)
    else:
        message[block(0), :] = cells
        message[block(1), :] = columns
        message[block(2), :] = sums
        message[block(3), :] = jnp.zeros((PEERS, 128), F32)
    send_borders(
        fixed["trans"], weighted, along, out["toward_low"], out["toward_high"], message, pad
    )
    if narrow:
        out["message"][...] = message[...].astype(BF16)


def finish(arrived, omega, field_one, field_two, state_one, state_two, cells, segments):
    first = omega[0:1, 0:1]
    second = ratio(arrived[...], 60)

    def blend(one, two):
        kept = first * one
        return kept + second * (one + first * (two - one) - kept)

    for n in range(3):
        for t in range(CHUNKS):
            rows = chunk(t)
            cells[n, rows, :] = blend(field_one[n, rows, :], field_two[n, rows, :])
    segments[...] = blend(state_one[0:2], state_two[0:2])


CELLS = ((3, ROWS, 128), F32)
PAIRS = ((PEERS, 128), F32)
MESSAGE = ((4 * PEERS, 128), F32)
TILE = ((8, 128), F32)
EDGE = ((3 * NZ, 128), F32)
SHAPES = {
    "weighted": CELLS, "toward_low": EDGE, "toward_high": EDGE, "message": MESSAGE, "slots": PAIRS,
    "at_slots": TILE, "state": TILE, "omega": TILE, "field": CELLS, "change": CELLS,
    "seg_change": TILE,
}


def shape_of(kind, name):
    if name != "message":
        return SHAPES[name]
    if kind == "final":
        return PAIRS
    return (MESSAGE[0], BF16) if kind in NARROW else MESSAGE


SCRATCH = (
    pltpu.VMEM((3 * ROWS, 128), F32),
    pltpu.VMEM((16, 128), F32),
    pltpu.VMEM((ROWS, 128), F32),
)


def call(body, outs, args, scratch=(), name=None, space=pltpu.VMEM, grant=24 * 1024 * 1024):
    moved = sum(a.size * a.dtype.itemsize for a in args)
    return pl.pallas_call(
        body,
        out_shape=[jax.ShapeDtypeStruct(*out) for out in outs],
        in_specs=[pl.BlockSpec(memory_space=space)] * len(args),
        out_specs=[pl.BlockSpec(memory_space=pltpu.VMEM)] * len(outs),
        scratch_shapes=list(scratch),
        compiler_params=pltpu.CompilerParams(vmem_limit_bytes=grant),
        cost_estimate=pl.CostEstimate(flops=4_000_000, bytes_accessed=moved, transcendentals=0),
        name=name,
    )(*args)


def exchange(message):
    return lax.all_to_all(message, AXES, split_axis=0, concat_axis=0, tiled=True)


def neighbours(toward_low, toward_high):
    count = lax.axis_size("gx")
    up = [(i, (i + 1) % count) for i in range(count)]
    down = [(b, a) for a, b in up]
    return {
        "from_low": lax.ppermute(toward_high, "gx", up),
        "from_high": lax.ppermute(toward_low, "gx", down),
    }


def on_device(
    rhs, diag_block, mobility, trans, perf_cell, perf_pi, perf_seg, seg_parent, seg_trans, seg_rhs
):
    rhs = rhs.reshape(3, ROWS, 128)
    diag = diag_block.reshape(9, ROWS, 128)
    mobility = mobility.reshape(9, ROWS, 128)
    trans = trans.reshape(3, ROWS, 128)
    index = perf_seg[0]

    fixed = {"rhs": rhs, "diag": diag, "mobility": mobility, "trans": trans, "index": index}
    inputs = [rhs, diag, mobility, trans, perf_cell[0], perf_pi[0], index]
    inputs += [a.reshape(2, 128) for a in (seg_parent, seg_trans, seg_rhs)]
    (rows_of, rows_to, start, weight, slots, constants, weighted, toward_low, toward_high,
     message) = call(
        cell_setup,
        [((PEERS, ROWS), BF16), ((ROWS, PEERS), BF16),
         ((PEERS, 128), jnp.int32), PAIRS, PAIRS, ((4, 8, 128), F32), CELLS, EDGE, EDGE,
         ((24 * PEERS, 128), BF16)],
        inputs,
        SCRATCH + (pltpu.VMEM((8 * PEERS, 128), F32),)
        + tuple(pltpu.VMEM(a.shape, a.dtype) for a in inputs) + (pltpu.SemaphoreType.DMA((10,)),),
        name="cell_setup",
        space=pltpu.HBM,
        grant=64 * 1024 * 1024 - 256 * 1024,
    )
    arrived = exchange(message)

    def inside(weighted):
        return call(interior, [CELLS], [weighted, trans], name="interior")[0]

    (table,) = call(well_tables, [((128, CAP * 128), BF16)], [index], name="well_tables")
    fixed.update(rows_of=rows_of, rows_to=rows_to, start=start, weight=weight)
    now = {"near": inside(weighted), "slots": slots}
    now.update(neighbours(toward_low, toward_high))
    now["arrived"], own_weight, state, at_slots, diagonal = call(
        well_setup,
        [MESSAGE, TILE, TILE, TILE, TILE],
        [arrived, index, table, constants],
        [pltpu.VMEM((24 * PEERS, 128), F32), pltpu.VMEM((CAP, PEERS, 128), F32)],
        name="well_setup",
    )
    fixed.update(own_weight=own_weight, table=table, fixed=constants, diagonal=diagonal)
    now.update(at_slots=at_slots, state=state)
    saved = {}

    def advance(kind, now):
        args = [now[name] for name in MOVING]
        args += [fixed[name] for name in STEADY]
        args += [saved[name] for name in MORE_IN[kind]]
        names = results_of(kind)
        out = call(
            functools.partial(sweep, kind),
            [shape_of(kind, name) for name in names],
            args,
            SCRATCH + (pltpu.VMEM(*MESSAGE),),
            name="sweep_" + kind,
        )
        out = dict(zip(names, out))
        out["arrived"] = exchange(out.pop("message"))
        if kind != "final":
            out.update(neighbours(out.pop("toward_low"), out.pop("toward_high")))
            out["near"] = inside(out.pop("weighted"))
        return out

    now = advance("plain", now)
    now = advance("plain", now)
    one = advance("keep", now)
    saved["field"] = one["field"]
    now = advance("last", one)
    saved.update(change=now["change"], seg_change=now["seg_change"])
    now = advance("after", now)
    saved["omega"] = now["omega"]
    now = advance("plain", now)
    two = advance("keep", now)
    saved["field"] = two["field"]
    sums = advance("final", two)
    cells, segments = call(
        finish,
        [CELLS, ((2, 128), F32)],
        [sums["arrived"], saved["omega"], one["field"], two["field"], one["state"], two["state"]],
        name="finish",
    )
    return cells.reshape(3, NZ, CX, CY), segments.reshape(256)


def solution(mesh):
    grid = P(None, None, "gx", "gy")
    pairs = P(AXES, None, None)
    flat = P(AXES)
    return jax.shard_map(
        on_device,
        mesh=mesh,
        in_specs=(grid, grid, grid, grid, pairs, pairs, pairs, flat, flat, flat),
        out_specs=(grid, flat),
        check_vma=False,
    )
```

```python
import functools

import jax
import jax.numpy as jnp
from jax import lax
from jax.experimental import pallas as pl
from jax.experimental.pallas import tpu as pltpu
from jax.sharding import PartitionSpec as P

F32 = jnp.float32
BF16 = jnp.bfloat16
AXES = ("gx", "gy")
NZ, CX, CY = 20, 8, 128
ROWS = NZ * CX
STEP = 16
CHUNKS = ROWS // STEP
PEERS = 128
CAP = 8


def lanes(shape):
    return lax.broadcasted_iota(jnp.int32, shape, 1)


def subs(shape):
    return lax.broadcasted_iota(jnp.int32, shape, 0)


def halves(x):
    high = x.astype(BF16).astype(F32)
    return high, x - high


def pick_rows(onehot, x):
    def dot(part):
        return lax.dot_general(
            onehot, part.astype(BF16), (((1,), (0,)), ((), ())), preferred_element_type=F32
        )

    high, low = halves(x)
    return dot(low) + dot(high)


def is_slot(lane):
    return (lane & 63) >= 60


def slot_values(rows_of, start, first):
    lane = lanes((PEERS, CY))
    number = (lane & 3) + jnp.where(lane >= 64, 4, 0)
    picked = pick_rows(rows_of, first)
    window = jnp.take_along_axis(picked, (start + number) & (CY - 1), axis=1)
    return jnp.where(is_slot(lane), window, 0.0)


def into_cells(rows_to, start, flows):
    number = (lanes((PEERS, CY)) - start) & (CY - 1)
    place = jnp.where(number < 4, number + 60, jnp.where(number < CAP, number + 120, 0))
    return pick_rows(rows_to, jnp.take_along_axis(flows, place, axis=1))


def segment_values(state, index):
    low = index & 127
    first = jnp.take_along_axis(jnp.broadcast_to(state[0:1], (8, 128)), low, axis=1)
    second = jnp.take_along_axis(jnp.broadcast_to(state[1:2], (8, 128)), low, axis=1)
    return jnp.where(index >= 128, second, first)


def into_segments(values, index, table):
    parts = halves(values)
    sub = subs((16, 128))
    upper = (index >= 128).astype(jnp.int32)
    tiles = []
    for k in range(CAP):
        row = [jnp.broadcast_to(part[k : k + 1], (16, 128)) for part in parts]
        mine = jnp.broadcast_to(upper[k : k + 1], (16, 128)) == (sub & 1)
        tile = jnp.where(sub < 2, row[0], row[1])
        tiles.append(jnp.where(mine & (sub < 4), tile, 0.0).astype(BF16))
    left = jnp.concatenate(tiles, axis=1)
    out = lax.dot_general(left, table, (((1,), (1,)), ((), ())), preferred_element_type=F32)[:8]
    return jnp.where(subs((8, 128)) < 2, pltpu.roll(out, 6, 0) + out, 0.0)


def previous(state):
    moved = pltpu.roll(state, 1, 1)
    return jnp.where(lanes((8, 128)) == 0, pltpu.roll(moved, 1, 0), moved)


def following(state):
    moved = pltpu.roll(state, 127, 1)
    return jnp.where(lanes((8, 128)) == 127, pltpu.roll(moved, 7, 0), moved)


def to_columns(values):
    gap = jnp.zeros((60, 128), F32)
    return jnp.concatenate([gap, values[0:4], gap, values[4:8]], axis=0).T


def to_rows(columns):
    turned = columns.T
    return jnp.concatenate([turned[60:64], turned[124:128]], axis=0)


def field(n):
    return pl.ds(n, PEERS, stride=8)


def block(n):
    return pl.ds(n, PEERS, stride=4)


def chunk(t):
    return pl.ds(t * STEP, STEP)


def me():
    return lax.axis_index("gx") * 16 + lax.axis_index("gy")


def peer_rows(shift, pitch=4):
    return pl.ds(pitch * ((me() + shift) & (PEERS - 1)), 4)


def tile_to_rows(tile, pad):
    pad[0:8] = tile
    pad[8:16] = pltpu.roll(tile, 64, 1)
    even = pad[pl.ds(0, 4, stride=2), :]
    odd = pad[pl.ds(9, 4, stride=2), :]
    return jnp.where(lanes((4, 128)) < 64, even, odd)


def rows_to_tile(four, pad):
    pad[0:4] = four
    pad[8:16] = pltpu.roll(pad[0:8], 64, 1)
    low, high = pad[0:4], pad[8:12]
    pad[pl.ds(0, 4, stride=2), :] = low
    pad[pl.ds(1, 4, stride=2), :] = high
    return pad[0:8]


def mix(matrix, rows, vector):
    entry = [matrix[n, rows, :].astype(F32) for n in range(9)]
    x, y, z = vector
    return [entry[3 * n] * x + entry[3 * n + 1] * y + entry[3 * n + 2] * z for n in range(3)]


def solve(diag, rows, vector, scale=None):
    a, b, c, d, e, f, g, h, i = [diag[n, rows, :].astype(F32) for n in range(9)]
    x, y, z = vector
    p, q, s = e * i - f * h, f * g - d * i, d * h - e * g
    if scale is None:
        scale = 1.0 / (a * p + b * q + c * s)
    return [
        (p * x + (c * h - b * i) * y + (b * f - c * e) * z) * scale,
        (q * x + (a * i - c * g) * y + (c * d - a * f) * z) * scale,
        (s * x + (b * g - a * h) * y + (a * e - b * d) * z) * scale,
    ], scale


def borders(values, mobility, trans, weighted, along, t):
    rows = chunk(t)
    tx = trans[0, rows, :].astype(F32)
    for n, value in enumerate(mix(mobility, rows, values)):
        weighted[n, rows, :] = value
        along[pl.ds(n * ROWS + t * STEP, STEP), :] = tx * value


def send_borders(trans, weighted, along, toward_low, toward_high, message, pad, pitch=4):
    toward_low[...] = along[pl.ds(0, 3 * NZ, stride=CX), :]
    toward_high[...] = along[pl.ds(CX - 1, 3 * NZ, stride=CX), :]
    small = lanes((8, 128))
    high = jnp.zeros((8, 128), F32)
    low = jnp.zeros((8, 128), F32)
    for t in range(CHUNKS):
        ty = trans[1, chunk(t), :].astype(F32)
        for n in range(3):
            py = ty * weighted[n, chunk(t), :]
            for half in range(2):
                j = n * NZ + 2 * t + half
                moved = pltpu.roll(py[8 * half : 8 * half + 8], j + 1, 1)
                high = jnp.where(small == j, moved, high)
                low = jnp.where(small == j + 1, moved, low)
    low = pltpu.roll(low, 127, 1)
    mine = is_slot(lanes((4, 128)))
    for shift, tile in ((1, high), (-1, low)):
        rows = peer_rows(shift, pitch)
        packed = tile_to_rows(tile, pad)
        message[rows, :] = jnp.where(mine, message[rows, :], packed)


def interior(weighted, trans, near):
    lane = lanes((STEP, 128))
    sub = subs((STEP, 128)) & 7
    zero = jnp.zeros((8, 128), F32)
    up = [trans[2, chunk(t), :].astype(F32) for t in range(CHUNKS)]
    for t in range(CHUNKS):
        rows = chunk(t)
        tx, ty = [trans[n, rows, :].astype(F32) for n in range(2)]
        tz = up[t]
        for n in range(3):
            value = weighted[n, rows, :]
            px, py = tx * value, ty * value
            nx = jnp.where(sub == 0, 0.0, pltpu.roll(px, 1, 0)) + jnp.where(
                sub == 7, 0.0, pltpu.roll(px, STEP - 1, 0)
            )
            ny = jnp.where(lane == 0, 0.0, pltpu.roll(py, 1, 1)) + jnp.where(
                lane == 127, 0.0, pltpu.roll(py, 127, 1)
            )
            pz = tz * value
            below = zero
            above = zero
            if t:
                below = up[t - 1][8:16] * weighted[n, pl.ds(t * STEP - 8, 8), :]
            if t + 1 < CHUNKS:
                above = up[t + 1][0:8] * weighted[n, pl.ds(t * STEP + STEP, 8), :]
            nz = jnp.concatenate([below + pz[8:16], pz[0:8] + above], axis=0)
            near[n, rows, :] = tx * nx + ty * ny + tz * nz


def cell_setup(rhs_in, diag_in, mobility_in, trans_in, cells_in, pi_in, index_in, parent_in,
               across_in, source_in,
               rows_of, rows_to, start, weight, slots, fixed, scale,
               weighted, toward_low, toward_high, message, along, pad, forward, own,
               rhs, diag, mobility, trans, cells, pi, index, parent, across, source, sems):
    pairs = ((cells_in, cells), (pi_in, pi), (index_in, index), (parent_in, parent),
             (across_in, across), (source_in, source), (rhs_in, rhs), (diag_in, diag),
             (mobility_in, mobility), (trans_in, trans))
    copies = [pltpu.make_async_copy(a, b, sems.at[n]) for n, (a, b) in enumerate(pairs)]
    for copy in copies:
        copy.start()
    for copy in copies[:6]:
        copy.wait()
    zeros = jnp.zeros((6, 128), F32)
    linked = jnp.concatenate([(parent[...] >= 0).astype(F32), zeros], axis=0)
    moving = jnp.concatenate([across[...], zeros], axis=0)
    given = jnp.concatenate([source[...], zeros], axis=0)
    partial = moving + following(linked * moving)
    fixed[0] = linked
    fixed[1] = moving
    fixed[2] = given
    fixed[3] = partial
    number = index[...]
    own[field(1), :], own[field(3), :] = halves(to_columns(segment_values(given, number)))
    own[field(4), :], own[field(5), :] = halves(to_columns(segment_values(partial, number)))
    own[field(7), :] = jnp.zeros((PEERS, 128), F32)
    base = cells[0:1, :]
    row = lax.shift_right_logical(base, 7)
    live = pi[...]
    gap = jnp.zeros((44, 128), F32)
    info = jnp.concatenate(
        [jnp.broadcast_to(row.astype(F32), (8, 128)),
         jnp.broadcast_to((base & 127).astype(F32), (8, 128)),
         gap, live[0:4], gap, jnp.zeros((16, 128), F32), live[4:8]],
        axis=0,
    ).T
    rows_to[...] = (subs((ROWS, PEERS)) == jnp.broadcast_to(row, (ROWS, PEERS))).astype(F32).astype(BF16)
    row_column = jnp.broadcast_to(info[:, 0:1], (PEERS, ROWS)).astype(jnp.int32)
    rows_of[...] = (lanes((PEERS, ROWS)) == row_column).astype(F32).astype(BF16)
    begin = jnp.broadcast_to(info[:, 8:9], (PEERS, 128)).astype(jnp.int32)
    start[...] = begin
    weights = jnp.where(is_slot(lanes((PEERS, 128))), info, 0.0)
    weight[...] = weights
    own[field(6), :] = halves(weights)[1]
    high = halves(live)[0]
    order = number.astype(F32)
    common = jnp.concatenate([high, order], axis=0).astype(BF16)
    for d in range(0, PEERS, 2):
        message[pl.ds(24 * d + 32, 16), :] = common
    for copy in copies[6:8]:
        copy.wait()
    for t in range(CHUNKS):
        rows = chunk(t)
        values, scale[rows, :] = solve(diag, rows, [rhs[n, rows, :] for n in range(3)])
        forward[rows, :] = values[0]
        for n in range(3):
            weighted[n, rows, :] = values[n]
    values = slot_values(rows_of[...], begin, forward[...])
    slots[...] = values
    own[field(0), :], own[field(2), :] = halves(values)
    for copy in copies[8:]:
        copy.wait()
    for t in range(CHUNKS):
        values = [weighted[n, chunk(t), :] for n in range(3)]
        borders(values, mobility, trans, weighted, along, t)
    send_borders(trans, weighted, along, toward_low, toward_high, own, pad, 8)
    for d in range(0, PEERS, 2):
        two = [own[pl.ds(8 * d, 8), :], high, order, own[pl.ds(8 * d + 8, 8), :]]
        message[pl.ds(24 * d, 32), :] = jnp.concatenate(two, axis=0).astype(BF16)


def well_tables(index, table):
    low = index[...] & 127
    for k in range(CAP):
        hit = subs((128, 128)) == jnp.broadcast_to(low[k : k + 1], (128, 128))
        table[:, 128 * k : 128 * (k + 1)] = hit.astype(F32).astype(BF16)


def well_setup(arrived, index, table, fixed, message, weight, state, at_slots, diagonal,
               wide, turned):
    wide[...] = arrived[...].astype(F32)

    def part(n):
        return wide[pl.ds(n, PEERS, stride=24), :]

    lane = lanes((PEERS, 128))
    mine = lane == me()
    for k in range(CAP):
        turned[k] = part(8 + k).T
    total = part(4) + part(5)
    for k in range(CAP):
        target = jnp.sum(jnp.where(mine, part(16 + k), 0.0), axis=1, keepdims=True)
        target = jnp.broadcast_to(target, (PEERS, 128))
        found = jnp.zeros((PEERS, 128), F32)
        for m in range(CAP):
            found += jnp.where(part(16 + m) == target, turned[m], 0.0)
        place = 60 + k if k < 4 else 120 + k
        total += jnp.where(lane == place, jnp.sum(found, axis=1, keepdims=True), 0.0)
    slot = is_slot(lane)
    pressures = (part(1) + part(3)) / jnp.where(slot, total, 1.0)
    message[block(0), :] = jnp.where(slot, part(0) + part(2), part(0))
    message[block(1), :] = jnp.where(slot, pressures, part(1))
    message[block(2), :] = part(2)
    message[block(3), :] = part(3)
    pi = jnp.concatenate([turned[k, pl.ds(me(), 1), :] for k in range(CAP)], axis=0)
    pi += to_rows(part(6))
    weight[...] = pi
    number = index[...]
    total = fixed[3] + into_segments(pi, number, table[...])
    total = jnp.where(subs((8, 128)) < 2, total, 1.0)
    diagonal[...] = total
    now = fixed[2] / total
    state[...] = now
    at_slots[...] = segment_values(now, number)


def ratio(sums, place):
    total = jnp.sum(sums, axis=0, keepdims=True)
    lane = lanes((1, 128))
    numer = jnp.sum(jnp.where(lane == place, total, 0.0), axis=1, keepdims=True)
    denom = jnp.sum(jnp.where(lane == place + 1, total, 0.0), axis=1, keepdims=True)
    return numer / denom


def spread_pair(two):
    return jnp.concatenate(
        [jnp.broadcast_to(two[h : h + 1], (8, 128)) for h in range(2)], axis=0
    )


STEADY = ("rhs", "diag", "mobility", "trans", "rows_of", "rows_to", "start", "weight",
          "own_weight", "table", "index", "fixed", "diagonal", "scale")
MOVING = ("arrived", "near", "from_low", "from_high", "slots", "at_slots", "state")
NEXT = ("weighted", "toward_low", "toward_high", "message", "slots", "at_slots", "state")
MORE_IN = {
    "plain": (), "keep": (), "last": ("field",), "after": (),
    "final": ("field", "change", "seg_change", "omega"),
}
NARROW = ("plain", "keep", "after")
MORE_OUT = {
    "plain": (), "keep": ("field",), "last": ("change", "seg_change"),
    "after": ("omega",), "final": (),
}


def results_of(kind):
    return ("message",) if kind == "final" else NEXT + MORE_OUT[kind]


def sweep(kind, *refs):
    take = iter(refs)
    now = {name: next(take) for name in MOVING}
    fixed = {name: next(take) for name in STEADY}
    extra = {name: next(take) for name in MORE_IN[kind]}
    out = {name: next(take) for name in results_of(kind)}
    along, pad, forward, wide = take
    narrow = kind in NARROW
    weighted = out.get("weighted")
    final = kind == "final"
    gx, gy = lax.axis_index("gx"), lax.axis_index("gy")

    arrived = now["arrived"]
    if arrived.dtype == BF16:
        wide[...] = arrived[...].astype(F32)
        arrived = wide
        heads = arrived[block(0), :] + arrived[block(2), :]
        pressures = arrived[block(1), :] + arrived[block(3), :]
    else:
        heads, pressures = arrived[block(0), :], arrived[block(1), :]
    pull = fixed["weight"][...] * (now["slots"][...] - pressures)
    perforated = into_cells(fixed["rows_to"][...], fixed["start"][...], pull)

    side_low = rows_to_tile(arrived[peer_rows(-1), :], pad)
    side_high = rows_to_tile(arrived[peer_rows(1), :], pad)
    side_low = jnp.where(gy == 0, 0.0, side_low)
    side_high = jnp.where(gy == lax.axis_size("gy") - 1, 0.0, side_high)
    small = lanes((8, 128))
    ahead = pltpu.roll(side_high, 127, 1)
    sides = [jnp.where((small & 1) == odd, side_low, ahead) for odd in range(2)]
    open_low, open_high = gx > 0, gx < lax.axis_size("gx") - 1

    state = now["state"][...]
    linked, across, source = [fixed["fixed"][n] for n in range(3)]
    push = fixed["own_weight"][...] * (to_rows(heads) - now["at_slots"][...])
    number = fixed["index"][...]
    inflow = into_segments(push, number, fixed["table"][...])
    flux = across * (state - linked * previous(state))
    seg_res = source - flux + following(linked * flux) + inflow

    lane = lanes((STEP, 128))
    sub = subs((STEP, 128)) & 7
    numer = jnp.zeros((STEP, 128), F32)
    denom = jnp.zeros((STEP, 128), F32)
    if final:
        omega = extra["omega"][0:1, 0:1]
    for t in range(CHUNKS):
        rows = chunk(t)
        tx, ty = [fixed["trans"][n, rows, :].astype(F32) for n in range(2)]
        tx = jnp.where(
            sub == 0, jnp.where(open_low, tx, 0.0),
            jnp.where((sub == 7) & open_high, tx, 0.0),
        )
        ty = jnp.where((lane == 0) | (lane == 127), ty, 0.0)
        terms = []
        for n in range(3):
            j = n * NZ + 2 * t
            low, high = now["from_low"][j : j + 2, :], now["from_high"][j : j + 2, :]
            nx = jnp.where(sub == 0, spread_pair(low), spread_pair(high))
            ny = jnp.concatenate(
                [pltpu.roll(sides[(j + h) & 1], (128 - j - h) % 128, 1) for h in range(2)], axis=0
            )
            share = fixed["mobility"][3 * n, rows, :].astype(F32)
            value = now["near"][n, rows, :] + tx * nx + ty * ny
            terms.append(value - share * perforated[t * STEP : (t + 1) * STEP])
        if kind in ("last", "final"):
            own = mix(fixed["diag"], rows, [extra["field"][n, rows, :] for n in range(3)])
            for n in range(3):
                change = own[n] - terms[n]
                before = fixed["rhs"][n, rows, :]
                if final:
                    kept = extra["change"][n, rows, :]
                    before = before - omega * kept
                    change = kept + omega * (change - 2.0 * kept)
                else:
                    out["change"][n, rows, :] = change
                numer += before * change
                denom += change * change
        if not final:
            total = [fixed["rhs"][n, rows, :] + terms[n] for n in range(3)]
            values = solve(fixed["diag"], rows, total, fixed["scale"][rows, :])[0]
            forward[rows, :] = values[0]
            if kind == "keep":
                for n in range(3):
                    out["field"][n, rows, :] = values[n]
            borders(values, fixed["mobility"], fixed["trans"], weighted, along, t)

    if kind in ("last", "final"):
        before = source
        change = source - seg_res
        if final:
            kept = extra["seg_change"][...]
            before = source - omega * kept
            change = kept + omega * (change - 2.0 * kept)
        else:
            out["seg_change"][...] = change
        above = jnp.sum(numer, keepdims=True) + jnp.sum(before * change, keepdims=True)
        below = jnp.sum(denom, keepdims=True) + jnp.sum(change * change, keepdims=True)
        place = lanes((PEERS, 128))
        sums = jnp.where(place == 60, above, jnp.where(place == 61, below, 0.0))
        if final:
            out["message"][...] = sums
            return
    if kind == "after":
        out["omega"][...] = jnp.broadcast_to(ratio(arrived[block(2), :], 60), (8, 128))
    message = wide if narrow else out["message"]
    advanced = state + seg_res / fixed["diagonal"][...]
    out["state"][...] = advanced
    values = segment_values(advanced, number)
    out["at_slots"][...] = values
    cells = slot_values(fixed["rows_of"][...], fixed["start"][...], forward[...])
    out["slots"][...] = cells
    columns = to_columns(values)
    if narrow:
        message[block(0), :], message[block(2), :] = halves(cells)
        message[block(1), :], message[block(3), :] = halves(columns)
    else:
        message[block(0), :] = cells
        message[block(1), :] = columns
        message[block(2), :] = sums
        message[block(3), :] = jnp.zeros((PEERS, 128), F32)
    send_borders(
        fixed["trans"], weighted, along, out["toward_low"], out["toward_high"], message, pad
    )
    if narrow:
        out["message"][...] = message[...].astype(BF16)


def finish(arrived, omega, field_one, field_two, state_one, state_two, cells, segments):
    first = omega[0:1, 0:1]
    second = ratio(arrived[...], 60)

    def blend(one, two):
        kept = first * one
        return kept + second * (one + first * (two - one) - kept)

    for n in range(3):
        for t in range(CHUNKS):
            rows = chunk(t)
            cells[n, rows, :] = blend(field_one[n, rows, :], field_two[n, rows, :])
    segments[...] = blend(state_one[0:2], state_two[0:2])


CELLS = ((3, ROWS, 128), F32)
PAIRS = ((PEERS, 128), F32)
MESSAGE = ((4 * PEERS, 128), F32)
TILE = ((8, 128), F32)
EDGE = ((3 * NZ, 128), F32)
SHAPES = {
    "weighted": CELLS, "toward_low": EDGE, "toward_high": EDGE, "message": MESSAGE, "slots": PAIRS,
    "at_slots": TILE, "state": TILE, "omega": TILE, "field": CELLS, "change": CELLS,
    "seg_change": TILE,
}


def shape_of(kind, name):
    if name != "message":
        return SHAPES[name]
    if kind == "final":
        return PAIRS
    return (MESSAGE[0], BF16) if kind in NARROW else MESSAGE


SCRATCH = (
    pltpu.VMEM((3 * ROWS, 128), F32),
    pltpu.VMEM((16, 128), F32),
    pltpu.VMEM((ROWS, 128), F32),
)


def call(body, outs, args, scratch=(), name=None, space=pltpu.VMEM, grant=24 * 1024 * 1024):
    moved = sum(a.size * a.dtype.itemsize for a in args)
    return pl.pallas_call(
        body,
        out_shape=[jax.ShapeDtypeStruct(*out) for out in outs],
        in_specs=[pl.BlockSpec(memory_space=space)] * len(args),
        out_specs=[pl.BlockSpec(memory_space=pltpu.VMEM)] * len(outs),
        scratch_shapes=list(scratch),
        compiler_params=pltpu.CompilerParams(vmem_limit_bytes=grant),
        cost_estimate=pl.CostEstimate(flops=4_000_000, bytes_accessed=moved, transcendentals=0),
        name=name,
    )(*args)


def exchange(message):
    return lax.all_to_all(message, AXES, split_axis=0, concat_axis=0, tiled=True)


def neighbours(toward_low, toward_high):
    count = lax.axis_size("gx")
    up = [(i, (i + 1) % count) for i in range(count)]
    down = [(b, a) for a, b in up]
    return {
        "from_low": lax.ppermute(toward_high, "gx", up),
        "from_high": lax.ppermute(toward_low, "gx", down),
    }


def on_device(
    rhs, diag_block, mobility, trans, perf_cell, perf_pi, perf_seg, seg_parent, seg_trans, seg_rhs
):
    rhs = rhs.reshape(3, ROWS, 128)
    diag = diag_block.reshape(9, ROWS, 128)
    mobility = mobility.reshape(9, ROWS, 128)
    trans = trans.reshape(3, ROWS, 128)
    index = perf_seg[0]

    fixed = {"rhs": rhs, "diag": diag, "mobility": mobility, "trans": trans, "index": index}
    inputs = [rhs, diag, mobility, trans, perf_cell[0], perf_pi[0], index]
    inputs += [a.reshape(2, 128) for a in (seg_parent, seg_trans, seg_rhs)]
    (rows_of, rows_to, start, weight, slots, constants, scale, weighted, toward_low, toward_high,
     message) = call(
        cell_setup,
        [((PEERS, ROWS), BF16), ((ROWS, PEERS), BF16),
         ((PEERS, 128), jnp.int32), PAIRS, PAIRS, ((4, 8, 128), F32), ((ROWS, 128), F32), CELLS, EDGE, EDGE,
         ((24 * PEERS, 128), BF16)],
        inputs,
        SCRATCH + (pltpu.VMEM((8 * PEERS, 128), F32),)
        + tuple(pltpu.VMEM(a.shape, a.dtype) for a in inputs) + (pltpu.SemaphoreType.DMA((10,)),),
        name="cell_setup",
        space=pltpu.HBM,
        grant=64 * 1024 * 1024 - 256 * 1024,
    )
    arrived = exchange(message)

    def inside(weighted):
        return call(interior, [CELLS], [weighted, trans], name="interior")[0]

    (table,) = call(well_tables, [((128, CAP * 128), BF16)], [index], name="well_tables")
    fixed.update(rows_of=rows_of, rows_to=rows_to, start=start, weight=weight, scale=scale)
    now = {"near": inside(weighted), "slots": slots}
    now.update(neighbours(toward_low, toward_high))
    now["arrived"], own_weight, state, at_slots, diagonal = call(
        well_setup,
        [MESSAGE, TILE, TILE, TILE, TILE],
        [arrived, index, table, constants],
        [pltpu.VMEM((24 * PEERS, 128), F32), pltpu.VMEM((CAP, PEERS, 128), F32)],
        name="well_setup",
    )
    fixed.update(own_weight=own_weight, table=table, fixed=constants, diagonal=diagonal)
    now.update(at_slots=at_slots, state=state)
    saved = {}

    def advance(kind, now):
        args = [now[name] for name in MOVING]
        args += [fixed[name] for name in STEADY]
        args += [saved[name] for name in MORE_IN[kind]]
        names = results_of(kind)
        out = call(
            functools.partial(sweep, kind),
            [shape_of(kind, name) for name in names],
            args,
            SCRATCH + (pltpu.VMEM(*MESSAGE),),
            name="sweep_" + kind,
        )
        out = dict(zip(names, out))
        out["arrived"] = exchange(out.pop("message"))
        if kind != "final":
            out.update(neighbours(out.pop("toward_low"), out.pop("toward_high")))
            out["near"] = inside(out.pop("weighted"))
        return out

    now = advance("plain", now)
    now = advance("plain", now)
    one = advance("keep", now)
    saved["field"] = one["field"]
    now = advance("last", one)
    saved.update(change=now["change"], seg_change=now["seg_change"])
    now = advance("after", now)
    saved["omega"] = now["omega"]
    now = advance("plain", now)
    two = advance("keep", now)
    saved["field"] = two["field"]
    sums = advance("final", two)
    cells, segments = call(
        finish,
        [CELLS, ((2, 128), F32)],
        [sums["arrived"], saved["omega"], one["field"], two["field"], one["state"], two["state"]],
        name="finish",
    )
    return cells.reshape(3, NZ, CX, CY), segments.reshape(256)


def solution(mesh):
    grid = P(None, None, "gx", "gy")
    pairs = P(AXES, None, None)
    flat = P(AXES)
    return jax.shard_map(
        on_device,
        mesh=mesh,
        in_specs=(grid, grid, grid, grid, pairs, pairs, pairs, flat, flat, flat),
        out_specs=(grid, flat),
        check_vma=False,
    )
```

```python
import functools

import jax
import jax.numpy as jnp
from jax import lax
from jax.experimental import pallas as pl
from jax.experimental.pallas import tpu as pltpu
from jax.sharding import PartitionSpec as P

F32 = jnp.float32
BF16 = jnp.bfloat16
AXES = ("gx", "gy")
NZ, CX, CY = 20, 8, 128
ROWS = NZ * CX
STEP = 16
CHUNKS = ROWS // STEP
PEERS = 128
CAP = 8


def lanes(shape):
    return lax.broadcasted_iota(jnp.int32, shape, 1)


def subs(shape):
    return lax.broadcasted_iota(jnp.int32, shape, 0)


def halves(x):
    high = x.astype(BF16).astype(F32)
    return high, x - high


def pick_rows(onehot, x):
    def dot(part):
        return lax.dot_general(
            onehot, part.astype(BF16), (((1,), (0,)), ((), ())), preferred_element_type=F32
        )

    high, low = halves(x)
    return dot(low) + dot(high)


def is_slot(lane):
    return (lane & 63) >= 60


def slot_values(rows_of, start, first):
    lane = lanes((PEERS, CY))
    number = (lane & 3) + jnp.where(lane >= 64, 4, 0)
    picked = pick_rows(rows_of, first)
    window = jnp.take_along_axis(picked, (start + number) & (CY - 1), axis=1)
    return jnp.where(is_slot(lane), window, 0.0)


def into_cells(rows_to, start, flows):
    number = (lanes((PEERS, CY)) - start) & (CY - 1)
    place = jnp.where(number < 4, number + 60, jnp.where(number < CAP, number + 120, 0))
    return pick_rows(rows_to, jnp.take_along_axis(flows, place, axis=1))


def segment_values(state, index):
    low = index & 127
    first = jnp.take_along_axis(jnp.broadcast_to(state[0:1], (8, 128)), low, axis=1)
    second = jnp.take_along_axis(jnp.broadcast_to(state[1:2], (8, 128)), low, axis=1)
    return jnp.where(index >= 128, second, first)


def into_segments(values, index, table):
    parts = halves(values)
    sub = subs((16, 128))
    upper = (index >= 128).astype(jnp.int32)
    tiles = []
    for k in range(CAP):
        row = [jnp.broadcast_to(part[k : k + 1], (16, 128)) for part in parts]
        mine = jnp.broadcast_to(upper[k : k + 1], (16, 128)) == (sub & 1)
        tile = jnp.where(sub < 2, row[0], row[1])
        tiles.append(jnp.where(mine & (sub < 4), tile, 0.0).astype(BF16))
    left = jnp.concatenate(tiles, axis=1)
    out = lax.dot_general(left, table, (((1,), (1,)), ((), ())), preferred_element_type=F32)[:8]
    return jnp.where(subs((8, 128)) < 2, pltpu.roll(out, 6, 0) + out, 0.0)


def previous(state):
    moved = pltpu.roll(state, 1, 1)
    return jnp.where(lanes((8, 128)) == 0, pltpu.roll(moved, 1, 0), moved)


def following(state):
    moved = pltpu.roll(state, 127, 1)
    return jnp.where(lanes((8, 128)) == 127, pltpu.roll(moved, 7, 0), moved)


def to_columns(values):
    gap = jnp.zeros((60, 128), F32)
    return jnp.concatenate([gap, values[0:4], gap, values[4:8]], axis=0).T


def to_rows(columns):
    turned = columns.T
    return jnp.concatenate([turned[60:64], turned[124:128]], axis=0)


def field(n):
    return pl.ds(n, PEERS, stride=8)


def block(n):
    return pl.ds(n, PEERS, stride=4)


def chunk(t):
    return pl.ds(t * STEP, STEP)


def me():
    return lax.axis_index("gx") * 16 + lax.axis_index("gy")


def peer_rows(shift, pitch=4):
    return pl.ds(pitch * ((me() + shift) & (PEERS - 1)), 4)


def tile_to_rows(tile, pad):
    pad[0:8] = tile
    pad[8:16] = pltpu.roll(tile, 64, 1)
    even = pad[pl.ds(0, 4, stride=2), :]
    odd = pad[pl.ds(9, 4, stride=2), :]
    return jnp.where(lanes((4, 128)) < 64, even, odd)


def rows_to_tile(four, pad):
    pad[0:4] = four
    pad[8:16] = pltpu.roll(pad[0:8], 64, 1)
    low, high = pad[0:4], pad[8:12]
    pad[pl.ds(0, 4, stride=2), :] = low
    pad[pl.ds(1, 4, stride=2), :] = high
    return pad[0:8]


def mix(matrix, rows, vector):
    entry = [matrix[n, rows, :].astype(F32) for n in range(9)]
    x, y, z = vector
    return [entry[3 * n] * x + entry[3 * n + 1] * y + entry[3 * n + 2] * z for n in range(3)]


def solve(diag, rows, vector, scale=None):
    a, b, c, d, e, f, g, h, i = [diag[n, rows, :].astype(F32) for n in range(9)]
    x, y, z = vector
    p, q, s = e * i - f * h, f * g - d * i, d * h - e * g
    if scale is None:
        scale = 1.0 / (a * p + b * q + c * s)
    return [
        (p * x + (c * h - b * i) * y + (b * f - c * e) * z) * scale,
        (q * x + (a * i - c * g) * y + (c * d - a * f) * z) * scale,
        (s * x + (b * g - a * h) * y + (a * e - b * d) * z) * scale,
    ], scale


def borders(values, mobility, trans, weighted, along, t):
    rows = chunk(t)
    tx = trans[0, rows, :].astype(F32)
    for n, value in enumerate(mix(mobility, rows, values)):
        weighted[n, rows, :] = value
        along[pl.ds(n * ROWS + t * STEP, STEP), :] = tx * value


def send_borders(trans, weighted, along, toward_low, toward_high, message, pad, pitch=4):
    toward_low[...] = along[pl.ds(0, 3 * NZ, stride=CX), :]
    toward_high[...] = along[pl.ds(CX - 1, 3 * NZ, stride=CX), :]
    small = lanes((8, 128))
    high = jnp.zeros((8, 128), F32)
    low = jnp.zeros((8, 128), F32)
    for t in range(CHUNKS):
        ty = trans[1, chunk(t), :].astype(F32)
        for n in range(3):
            py = ty * weighted[n, chunk(t), :]
            for half in range(2):
                j = n * NZ + 2 * t + half
                moved = pltpu.roll(py[8 * half : 8 * half + 8], j + 1, 1)
                high = jnp.where(small == j, moved, high)
                low = jnp.where(small == j + 1, moved, low)
    low = pltpu.roll(low, 127, 1)
    mine = is_slot(lanes((4, 128)))
    for shift, tile in ((1, high), (-1, low)):
        rows = peer_rows(shift, pitch)
        packed = tile_to_rows(tile, pad)
        message[rows, :] = jnp.where(mine, message[rows, :], packed)


def interior(weighted, trans, near):
    lane = lanes((STEP, 128))
    sub = subs((STEP, 128)) & 7
    zero = jnp.zeros((8, 128), F32)
    up = [trans[2, chunk(t), :].astype(F32) for t in range(CHUNKS)]
    for t in range(CHUNKS):
        rows = chunk(t)
        tx, ty = [trans[n, rows, :].astype(F32) for n in range(2)]
        tz = up[t]
        for n in range(3):
            value = weighted[n, rows, :]
            px, py = tx * value, ty * value
            nx = jnp.where(sub == 0, 0.0, pltpu.roll(px, 1, 0)) + jnp.where(
                sub == 7, 0.0, pltpu.roll(px, STEP - 1, 0)
            )
            ny = jnp.where(lane == 0, 0.0, pltpu.roll(py, 1, 1)) + jnp.where(
                lane == 127, 0.0, pltpu.roll(py, 127, 1)
            )
            pz = tz * value
            below = zero
            above = zero
            if t:
                below = up[t - 1][8:16] * weighted[n, pl.ds(t * STEP - 8, 8), :]
            if t + 1 < CHUNKS:
                above = up[t + 1][0:8] * weighted[n, pl.ds(t * STEP + STEP, 8), :]
            nz = jnp.concatenate([below + pz[8:16], pz[0:8] + above], axis=0)
            near[n, rows, :] = tx * nx + ty * ny + tz * nz


def cell_setup(rhs_in, diag_in, mobility_in, trans_in, cells_in, pi_in, index_in, parent_in,
               across_in, source_in,
               rows_of, rows_to, start, weight, slots, fixed, scale,
               weighted, toward_low, toward_high, message, along, pad, forward, own,
               rhs, diag, mobility, trans, cells, pi, index, parent, across, source, sems):
    pairs = ((cells_in, cells), (pi_in, pi), (index_in, index), (parent_in, parent),
             (across_in, across), (source_in, source), (rhs_in, rhs), (diag_in, diag),
             (mobility_in, mobility), (trans_in, trans))
    copies = [pltpu.make_async_copy(a, b, sems.at[n]) for n, (a, b) in enumerate(pairs)]
    for copy in copies:
        copy.start()
    for copy in copies[:6]:
        copy.wait()
    zeros = jnp.zeros((6, 128), F32)
    linked = jnp.concatenate([(parent[...] >= 0).astype(F32), zeros], axis=0)
    moving = jnp.concatenate([across[...], zeros], axis=0)
    given = jnp.concatenate([source[...], zeros], axis=0)
    partial = moving + following(linked * moving)
    fixed[0] = linked
    fixed[1] = moving
    fixed[2] = given
    fixed[3] = partial
    number = index[...]
    own[field(1), :], own[field(3), :] = halves(to_columns(segment_values(given, number)))
    own[field(4), :], own[field(5), :] = halves(to_columns(segment_values(partial, number)))
    own[field(7), :] = jnp.zeros((PEERS, 128), F32)
    base = cells[0:1, :]
    row = lax.shift_right_logical(base, 7)
    live = pi[...]
    gap = jnp.zeros((44, 128), F32)
    info = jnp.concatenate(
        [jnp.broadcast_to(row.astype(F32), (8, 128)),
         jnp.broadcast_to((base & 127).astype(F32), (8, 128)),
         gap, live[0:4], gap, jnp.zeros((16, 128), F32), live[4:8]],
        axis=0,
    ).T
    rows_to[...] = (subs((ROWS, PEERS)) == jnp.broadcast_to(row, (ROWS, PEERS))).astype(F32).astype(BF16)
    row_column = jnp.broadcast_to(info[:, 0:1], (PEERS, ROWS)).astype(jnp.int32)
    rows_of[...] = (lanes((PEERS, ROWS)) == row_column).astype(F32).astype(BF16)
    begin = jnp.broadcast_to(info[:, 8:9], (PEERS, 128)).astype(jnp.int32)
    start[...] = begin
    weights = jnp.where(is_slot(lanes((PEERS, 128))), info, 0.0)
    weight[...] = weights
    own[field(6), :] = halves(weights)[1]
    high = halves(live)[0]
    order = number.astype(F32)
    common = jnp.concatenate([high, order], axis=0).astype(BF16)
    for d in range(0, PEERS, 2):
        message[pl.ds(24 * d + 32, 16), :] = common
    for copy in copies[6:8]:
        copy.wait()
    for t in range(CHUNKS):
        rows = chunk(t)
        values, scale[rows, :] = solve(diag, rows, [rhs[n, rows, :] for n in range(3)])
        forward[rows, :] = values[0]
        for n in range(3):
            weighted[n, rows, :] = values[n]
    values = slot_values(rows_of[...], begin, forward[...])
    slots[...] = values
    own[field(0), :], own[field(2), :] = halves(values)
    for copy in copies[8:]:
        copy.wait()
    for t in range(CHUNKS):
        values = [weighted[n, chunk(t), :] for n in range(3)]
        borders(values, mobility, trans, weighted, along, t)
    send_borders(trans, weighted, along, toward_low, toward_high, own, pad, 8)
    for d in range(0, PEERS, 2):
        two = [own[pl.ds(8 * d, 8), :], high, order, own[pl.ds(8 * d + 8, 8), :]]
        message[pl.ds(24 * d, 32), :] = jnp.concatenate(two, axis=0).astype(BF16)


def well_tables(index, table):
    low = index[...] & 127
    for k in range(CAP):
        hit = subs((128, 128)) == jnp.broadcast_to(low[k : k + 1], (128, 128))
        table[:, 128 * k : 128 * (k + 1)] = hit.astype(F32).astype(BF16)


def well_setup(arrived, index, table, fixed, message, weight, state, at_slots, diagonal,
               wide, turned):
    wide[...] = arrived[...].astype(F32)

    def part(n):
        return wide[pl.ds(n, PEERS, stride=24), :]

    lane = lanes((PEERS, 128))
    mine = lane == me()
    for k in range(CAP):
        turned[k] = part(8 + k).T
    total = part(4) + part(5)
    for k in range(CAP):
        target = jnp.sum(jnp.where(mine, part(16 + k), 0.0), axis=1, keepdims=True)
        target = jnp.broadcast_to(target, (PEERS, 128))
        found = jnp.zeros((PEERS, 128), F32)
        for m in range(CAP):
            found += jnp.where(part(16 + m) == target, turned[m], 0.0)
        place = 60 + k if k < 4 else 120 + k
        total += jnp.where(lane == place, jnp.sum(found, axis=1, keepdims=True), 0.0)
    slot = is_slot(lane)
    pressures = (part(1) + part(3)) / jnp.where(slot, total, 1.0)
    message[block(0), :] = jnp.where(slot, part(0) + part(2), part(0))
    message[block(1), :] = jnp.where(slot, pressures, part(1))
    message[block(2), :] = part(2)
    message[block(3), :] = part(3)
    pi = jnp.concatenate([turned[k, pl.ds(me(), 1), :] for k in range(CAP)], axis=0)
    pi += to_rows(part(6))
    weight[...] = pi
    number = index[...]
    total = fixed[3] + into_segments(pi, number, table[...])
    total = jnp.where(subs((8, 128)) < 2, total, 1.0)
    diagonal[...] = total
    now = fixed[2] / total
    state[...] = now
    at_slots[...] = segment_values(now, number)


def ratio(sums, place):
    total = jnp.sum(sums, axis=0, keepdims=True)
    lane = lanes((1, 128))
    numer = jnp.sum(jnp.where(lane == place, total, 0.0), axis=1, keepdims=True)
    denom = jnp.sum(jnp.where(lane == place + 1, total, 0.0), axis=1, keepdims=True)
    return numer / denom


def parts_of(x):
    high, rest = halves(x)
    return (high,) + halves(rest)


def carried(own, relayed):
    lane = lanes((8, 128))
    row = jnp.zeros((8, 128), F32)
    for n, part in enumerate(parts_of(own) + parts_of(relayed)):
        moved = pltpu.roll(part, 2 * n, 1) if n else part
        row = jnp.where((lane >> 1) == n, moved, row)
    return row[0:1]


def collected(rows):
    lane, source = lanes((PEERS, 128)), subs((PEERS, 128))

    def at(shift):
        return source == ((me() + shift) & (PEERS - 1))

    direct = (lane < 6) & ~(at(1) | at(-1))
    through = (lane >= 6) & (lane < 12) & (at(15) | at(17))
    total = jnp.sum(jnp.where(direct | through, rows, 0.0), axis=0, keepdims=True)
    odd = (lanes((1, 128)) & 1) == 1
    numer = jnp.sum(jnp.where(odd, 0.0, total), axis=1, keepdims=True)
    denom = jnp.sum(jnp.where(odd, total, 0.0), axis=1, keepdims=True)
    return numer / denom


def spread_pair(two):
    return jnp.concatenate(
        [jnp.broadcast_to(two[h : h + 1], (8, 128)) for h in range(2)], axis=0
    )


STEADY = ("rhs", "diag", "mobility", "trans", "rows_of", "rows_to", "start", "weight",
          "own_weight", "table", "index", "fixed", "diagonal", "scale")
MOVING = ("arrived", "near", "from_low", "from_high", "slots", "at_slots", "state")
NEXT = ("weighted", "toward_low", "toward_high", "message", "slots", "at_slots", "state")
MORE_IN = {
    "plain": (), "keep": (), "last": ("field",), "after": ("sums",), "omega": (),
    "final": ("field", "change", "seg_change", "omega"),
}
MORE_OUT = {
    "plain": (), "keep": ("field",), "last": ("change", "seg_change", "sums"),
    "after": (), "omega": ("omega",), "final": (),
}


def results_of(kind):
    return ("message",) if kind == "final" else NEXT + MORE_OUT[kind]


def sweep(kind, *refs):
    take = iter(refs)
    now = {name: next(take) for name in MOVING}
    fixed = {name: next(take) for name in STEADY}
    extra = {name: next(take) for name in MORE_IN[kind]}
    out = {name: next(take) for name in results_of(kind)}
    along, pad, forward, wide = take
    weighted = out.get("weighted")
    final = kind == "final"
    gx, gy = lax.axis_index("gx"), lax.axis_index("gy")

    arrived = now["arrived"]
    if arrived.dtype == BF16:
        wide[...] = arrived[...].astype(F32)
        arrived = wide
        heads = arrived[block(0), :] + arrived[block(2), :]
        pressures = arrived[block(1), :] + arrived[block(3), :]
    else:
        heads, pressures = arrived[block(0), :], arrived[block(1), :]
    pull = fixed["weight"][...] * (now["slots"][...] - pressures)
    perforated = into_cells(fixed["rows_to"][...], fixed["start"][...], pull)

    side_low = rows_to_tile(arrived[peer_rows(-1), :], pad)
    side_high = rows_to_tile(arrived[peer_rows(1), :], pad)
    side_low = jnp.where(gy == 0, 0.0, side_low)
    side_high = jnp.where(gy == lax.axis_size("gy") - 1, 0.0, side_high)
    small = lanes((8, 128))
    ahead = pltpu.roll(side_high, 127, 1)
    sides = [jnp.where((small & 1) == odd, side_low, ahead) for odd in range(2)]
    open_low, open_high = gx > 0, gx < lax.axis_size("gx") - 1

    state = now["state"][...]
    linked, across, source = [fixed["fixed"][n] for n in range(3)]
    push = fixed["own_weight"][...] * (to_rows(heads) - now["at_slots"][...])
    number = fixed["index"][...]
    inflow = into_segments(push, number, fixed["table"][...])
    flux = across * (state - linked * previous(state))
    seg_res = source - flux + following(linked * flux) + inflow

    lane = lanes((STEP, 128))
    sub = subs((STEP, 128)) & 7
    numer = jnp.zeros((STEP, 128), F32)
    denom = jnp.zeros((STEP, 128), F32)
    if final:
        omega = extra["omega"][0:1, 0:1]
    for t in range(CHUNKS):
        rows = chunk(t)
        tx, ty = [fixed["trans"][n, rows, :].astype(F32) for n in range(2)]
        tx = jnp.where(
            sub == 0, jnp.where(open_low, tx, 0.0),
            jnp.where((sub == 7) & open_high, tx, 0.0),
        )
        ty = jnp.where((lane == 0) | (lane == 127), ty, 0.0)
        terms = []
        for n in range(3):
            j = n * NZ + 2 * t
            low, high = now["from_low"][j : j + 2, :], now["from_high"][j : j + 2, :]
            nx = jnp.where(sub == 0, spread_pair(low), spread_pair(high))
            ny = jnp.concatenate(
                [pltpu.roll(sides[(j + h) & 1], (128 - j - h) % 128, 1) for h in range(2)], axis=0
            )
            share = fixed["mobility"][3 * n, rows, :].astype(F32)
            value = now["near"][n, rows, :] + tx * nx + ty * ny
            terms.append(value - share * perforated[t * STEP : (t + 1) * STEP])
        if kind in ("last", "final"):
            own = mix(fixed["diag"], rows, [extra["field"][n, rows, :] for n in range(3)])
            for n in range(3):
                change = own[n] - terms[n]
                before = fixed["rhs"][n, rows, :]
                if final:
                    kept = extra["change"][n, rows, :]
                    before = before - omega * kept
                    change = kept + omega * (change - 2.0 * kept)
                else:
                    out["change"][n, rows, :] = change
                numer += before * change
                denom += change * change
        if not final:
            total = [fixed["rhs"][n, rows, :] + terms[n] for n in range(3)]
            values = solve(fixed["diag"], rows, total, fixed["scale"][rows, :])[0]
            forward[rows, :] = values[0]
            if kind == "keep":
                for n in range(3):
                    out["field"][n, rows, :] = values[n]
            borders(values, fixed["mobility"], fixed["trans"], weighted, along, t)

    if kind in ("last", "final"):
        before = source
        change = source - seg_res
        if final:
            kept = extra["seg_change"][...]
            before = source - omega * kept
            change = kept + omega * (change - 2.0 * kept)
        else:
            out["seg_change"][...] = change
        above = jnp.sum(numer, keepdims=True) + jnp.sum(before * change, keepdims=True)
        below = jnp.sum(denom, keepdims=True) + jnp.sum(change * change, keepdims=True)
        place = lanes((PEERS, 128))
        if final:
            out["message"][...] = jnp.where(
                place == 60, above, jnp.where(place == 61, below, 0.0)
            )
            return
        sums = jnp.where(small == 0, above, jnp.where(small == 1, below, 0.0))
        out["sums"][...] = sums
        out["toward_high"][60:64, :] = sums[0:4]
    if kind == "omega":
        out["omega"][...] = jnp.broadcast_to(collected(arrived[block(0), :]), (8, 128))
    message = wide
    advanced = state + seg_res / fixed["diagonal"][...]
    out["state"][...] = advanced
    values = segment_values(advanced, number)
    out["at_slots"][...] = values
    cells = slot_values(fixed["rows_of"][...], fixed["start"][...], forward[...])
    out["slots"][...] = cells
    high, message[block(2), :] = halves(cells)
    if kind == "after":
        relayed = jnp.broadcast_to(now["from_low"][60:61, :], (8, 128))
        row = jnp.broadcast_to(carried(extra["sums"][...], relayed), (PEERS, 128))
        high = jnp.where(lanes((PEERS, 128)) < 12, row, high)
    message[block(0), :] = high
    message[block(1), :], message[block(3), :] = halves(to_columns(values))
    toward_high = out["toward_high"]
    if kind == "last":
        toward_high = toward_high.at[pl.ds(0, 3 * NZ), :]
    send_borders(fixed["trans"], weighted, along, out["toward_low"], toward_high, message, pad)
    out["message"][...] = message[...].astype(BF16)


def finish(arrived, omega, field_one, field_two, state_one, state_two, cells, segments):
    first = omega[0:1, 0:1]
    second = ratio(arrived[...], 60)

    def blend(one, two):
        kept = first * one
        return kept + second * (one + first * (two - one) - kept)

    for n in range(3):
        for t in range(CHUNKS):
            rows = chunk(t)
            cells[n, rows, :] = blend(field_one[n, rows, :], field_two[n, rows, :])
    segments[...] = blend(state_one[0:2], state_two[0:2])


CELLS = ((3, ROWS, 128), F32)
PAIRS = ((PEERS, 128), F32)
MESSAGE = ((4 * PEERS, 128), F32)
TILE = ((8, 128), F32)
EDGE = ((3 * NZ, 128), F32)
SHAPES = {
    "weighted": CELLS, "toward_low": EDGE, "toward_high": EDGE, "message": MESSAGE, "slots": PAIRS,
    "at_slots": TILE, "state": TILE, "omega": TILE, "field": CELLS, "change": CELLS,
    "seg_change": TILE, "sums": TILE,
}


def shape_of(kind, name):
    if kind == "last" and name == "toward_high":
        return ((64, 128), F32)
    if name != "message":
        return SHAPES[name]
    if kind == "final":
        return PAIRS
    return (MESSAGE[0], BF16)


SCRATCH = (
    pltpu.VMEM((3 * ROWS, 128), F32),
    pltpu.VMEM((16, 128), F32),
    pltpu.VMEM((ROWS, 128), F32),
)


def call(body, outs, args, scratch=(), name=None, space=pltpu.VMEM, grant=24 * 1024 * 1024):
    moved = sum(a.size * a.dtype.itemsize for a in args)
    return pl.pallas_call(
        body,
        out_shape=[jax.ShapeDtypeStruct(*out) for out in outs],
        in_specs=[pl.BlockSpec(memory_space=space)] * len(args),
        out_specs=[pl.BlockSpec(memory_space=pltpu.VMEM)] * len(outs),
        scratch_shapes=list(scratch),
        compiler_params=pltpu.CompilerParams(vmem_limit_bytes=grant),
        cost_estimate=pl.CostEstimate(flops=4_000_000, bytes_accessed=moved, transcendentals=0),
        name=name,
    )(*args)


def exchange(message):
    return lax.all_to_all(message, AXES, split_axis=0, concat_axis=0, tiled=True)


def neighbours(toward_low, toward_high):
    count = lax.axis_size("gx")
    up = [(i, (i + 1) % count) for i in range(count)]
    down = [(b, a) for a, b in up]
    return {
        "from_low": lax.ppermute(toward_high, "gx", up),
        "from_high": lax.ppermute(toward_low, "gx", down),
    }


def on_device(
    rhs, diag_block, mobility, trans, perf_cell, perf_pi, perf_seg, seg_parent, seg_trans, seg_rhs
):
    rhs = rhs.reshape(3, ROWS, 128)
    diag = diag_block.reshape(9, ROWS, 128)
    mobility = mobility.reshape(9, ROWS, 128)
    trans = trans.reshape(3, ROWS, 128)
    index = perf_seg[0]

    fixed = {"rhs": rhs, "diag": diag, "mobility": mobility, "trans": trans, "index": index}
    inputs = [rhs, diag, mobility, trans, perf_cell[0], perf_pi[0], index]
    inputs += [a.reshape(2, 128) for a in (seg_parent, seg_trans, seg_rhs)]
    (rows_of, rows_to, start, weight, slots, constants, scale, weighted, toward_low, toward_high,
     message) = call(
        cell_setup,
        [((PEERS, ROWS), BF16), ((ROWS, PEERS), BF16),
         ((PEERS, 128), jnp.int32), PAIRS, PAIRS, ((4, 8, 128), F32), ((ROWS, 128), F32), CELLS, EDGE, EDGE,
         ((24 * PEERS, 128), BF16)],
        inputs,
        SCRATCH + (pltpu.VMEM((8 * PEERS, 128), F32),)
        + tuple(pltpu.VMEM(a.shape, a.dtype) for a in inputs) + (pltpu.SemaphoreType.DMA((10,)),),
        name="cell_setup",
        space=pltpu.HBM,
        grant=64 * 1024 * 1024 - 256 * 1024,
    )
    arrived = exchange(message)

    def inside(weighted):
        return call(interior, [CELLS], [weighted, trans], name="interior")[0]

    (table,) = call(well_tables, [((128, CAP * 128), BF16)], [index], name="well_tables")
    fixed.update(rows_of=rows_of, rows_to=rows_to, start=start, weight=weight, scale=scale)
    now = {"near": inside(weighted), "slots": slots}
    now.update(neighbours(toward_low, toward_high))
    now["arrived"], own_weight, state, at_slots, diagonal = call(
        well_setup,
        [MESSAGE, TILE, TILE, TILE, TILE],
        [arrived, index, table, constants],
        [pltpu.VMEM((24 * PEERS, 128), F32), pltpu.VMEM((CAP, PEERS, 128), F32)],
        name="well_setup",
    )
    fixed.update(own_weight=own_weight, table=table, fixed=constants, diagonal=diagonal)
    now.update(at_slots=at_slots, state=state)
    saved = {}

    def advance(kind, now):
        args = [now[name] for name in MOVING]
        args += [fixed[name] for name in STEADY]
        args += [saved[name] for name in MORE_IN[kind]]
        names = results_of(kind)
        out = call(
            functools.partial(sweep, kind),
            [shape_of(kind, name) for name in names],
            args,
            SCRATCH + (pltpu.VMEM(*MESSAGE),),
            name="sweep_" + kind,
        )
        out = dict(zip(names, out))
        out["arrived"] = exchange(out.pop("message"))
        if kind != "final":
            out.update(neighbours(out.pop("toward_low"), out.pop("toward_high")))
            out["near"] = inside(out.pop("weighted"))
        return out

    now = advance("plain", now)
    now = advance("plain", now)
    one = advance("keep", now)
    saved["field"] = one["field"]
    now = advance("last", one)
    saved.update(change=now["change"], seg_change=now["seg_change"], sums=now["sums"])
    now = advance("after", now)
    now = advance("omega", now)
    saved["omega"] = now["omega"]
    two = advance("keep", now)
    saved["field"] = two["field"]
    sums = advance("final", two)
    cells, segments = call(
        finish,
        [CELLS, ((2, 128), F32)],
        [sums["arrived"], saved["omega"], one["field"], two["field"], one["state"], two["state"]],
        name="finish",
    )
    return cells.reshape(3, NZ, CX, CY), segments.reshape(256)


def solution(mesh):
    grid = P(None, None, "gx", "gy")
    pairs = P(AXES, None, None)
    flat = P(AXES)
    return jax.shard_map(
        on_device,
        mesh=mesh,
        in_specs=(grid, grid, grid, grid, pairs, pairs, pairs, flat, flat, flat),
        out_specs=(grid, flat),
        check_vma=False,
    )
```

```python
import functools

import jax
import jax.numpy as jnp
from jax import lax
from jax.experimental import pallas as pl
from jax.experimental.pallas import tpu as pltpu
from jax.sharding import PartitionSpec as P

F32 = jnp.float32
BF16 = jnp.bfloat16
AXES = ("gx", "gy")
NZ, CX, CY = 20, 8, 128
ROWS = NZ * CX
STEP = 16
CHUNKS = ROWS // STEP
PEERS = 128
CAP = 8


def lanes(shape):
    return lax.broadcasted_iota(jnp.int32, shape, 1)


def subs(shape):
    return lax.broadcasted_iota(jnp.int32, shape, 0)


def halves(x):
    high = x.astype(BF16).astype(F32)
    return high, x - high


def pick_rows(onehot, x):
    def dot(part):
        return lax.dot_general(
            onehot, part.astype(BF16), (((1,), (0,)), ((), ())), preferred_element_type=F32
        )

    high, low = halves(x)
    return dot(low) + dot(high)


def is_slot(lane):
    return (lane & 63) >= 60


def slot_values(rows_of, start, first):
    lane = lanes((PEERS, CY))
    number = (lane & 3) + jnp.where(lane >= 64, 4, 0)
    picked = pick_rows(rows_of, first)
    window = jnp.take_along_axis(picked, (start + number) & (CY - 1), axis=1)
    return jnp.where(is_slot(lane), window, 0.0)


def into_cells(rows_to, start, flows):
    number = (lanes((PEERS, CY)) - start) & (CY - 1)
    place = jnp.where(number < 4, number + 60, jnp.where(number < CAP, number + 120, 0))
    return pick_rows(rows_to, jnp.take_along_axis(flows, place, axis=1))


def segment_values(state, index):
    low = index & 127
    first = jnp.take_along_axis(jnp.broadcast_to(state[0:1], (8, 128)), low, axis=1)
    second = jnp.take_along_axis(jnp.broadcast_to(state[1:2], (8, 128)), low, axis=1)
    return jnp.where(index >= 128, second, first)


def into_segments(values, index, table):
    parts = halves(values)
    sub = subs((16, 128))
    upper = (index >= 128).astype(jnp.int32)
    tiles = []
    for k in range(CAP):
        row = [jnp.broadcast_to(part[k : k + 1], (16, 128)) for part in parts]
        mine = jnp.broadcast_to(upper[k : k + 1], (16, 128)) == (sub & 1)
        tile = jnp.where(sub < 2, row[0], row[1])
        tiles.append(jnp.where(mine & (sub < 4), tile, 0.0).astype(BF16))
    left = jnp.concatenate(tiles, axis=1)
    out = lax.dot_general(left, table, (((1,), (1,)), ((), ())), preferred_element_type=F32)[:8]
    return jnp.where(subs((8, 128)) < 2, pltpu.roll(out, 6, 0) + out, 0.0)


def previous(state):
    moved = pltpu.roll(state, 1, 1)
    return jnp.where(lanes((8, 128)) == 0, pltpu.roll(moved, 1, 0), moved)


def following(state):
    moved = pltpu.roll(state, 127, 1)
    return jnp.where(lanes((8, 128)) == 127, pltpu.roll(moved, 7, 0), moved)


def to_columns(values):
    gap = jnp.zeros((60, 128), F32)
    return jnp.concatenate([gap, values[0:4], gap, values[4:8]], axis=0).T


def to_rows(columns):
    turned = columns.T
    return jnp.concatenate([turned[60:64], turned[124:128]], axis=0)


def field(n):
    return pl.ds(n, PEERS, stride=8)


def block(n):
    return pl.ds(n, PEERS, stride=4)


def chunk(t):
    return pl.ds(t * STEP, STEP)


def me():
    return lax.axis_index("gx") * 16 + lax.axis_index("gy")


def peer_rows(shift, pitch=4):
    return pl.ds(pitch * ((me() + shift) & (PEERS - 1)), 4)


def tile_to_rows(tile, pad):
    pad[0:8] = tile
    pad[8:16] = pltpu.roll(tile, 64, 1)
    even = pad[pl.ds(0, 4, stride=2), :]
    odd = pad[pl.ds(9, 4, stride=2), :]
    return jnp.where(lanes((4, 128)) < 64, even, odd)


def rows_to_tile(four, pad):
    pad[0:4] = four
    pad[8:16] = pltpu.roll(pad[0:8], 64, 1)
    low, high = pad[0:4], pad[8:12]
    pad[pl.ds(0, 4, stride=2), :] = low
    pad[pl.ds(1, 4, stride=2), :] = high
    return pad[0:8]


def mix(matrix, rows, vector):
    entry = [matrix[n, rows, :].astype(F32) for n in range(9)]
    x, y, z = vector
    return [entry[3 * n] * x + entry[3 * n + 1] * y + entry[3 * n + 2] * z for n in range(3)]


def invert(diag, rows, inverse):
    a, b, c, d, e, f, g, h, i = [diag[n, rows, :].astype(F32) for n in range(9)]
    p, q, s = e * i - f * h, f * g - d * i, d * h - e * g
    scale = 1.0 / (a * p + b * q + c * s)
    entries = [
        p, c * h - b * i, b * f - c * e,
        q, a * i - c * g, c * d - a * f,
        s, b * g - a * h, a * e - b * d,
    ]
    for n, entry in enumerate(entries):
        inverse[n, rows, :] = entry * scale


def borders(values, mobility, trans, weighted, along, t):
    rows = chunk(t)
    tx = trans[0, rows, :].astype(F32)
    for n, value in enumerate(mix(mobility, rows, values)):
        weighted[n, rows, :] = value
        along[pl.ds(n * ROWS + t * STEP, STEP), :] = tx * value


def send_borders(trans, weighted, along, toward_low, toward_high, message, pad, pitch=4):
    toward_low[...] = along[pl.ds(0, 3 * NZ, stride=CX), :]
    toward_high[...] = along[pl.ds(CX - 1, 3 * NZ, stride=CX), :]
    small = lanes((8, 128))
    high = jnp.zeros((8, 128), F32)
    low = jnp.zeros((8, 128), F32)
    for t in range(CHUNKS):
        ty = trans[1, chunk(t), :].astype(F32)
        for n in range(3):
            py = ty * weighted[n, chunk(t), :]
            for half in range(2):
                j = n * NZ + 2 * t + half
                moved = pltpu.roll(py[8 * half : 8 * half + 8], j + 1, 1)
                high = jnp.where(small == j, moved, high)
                low = jnp.where(small == j + 1, moved, low)
    low = pltpu.roll(low, 127, 1)
    mine = is_slot(lanes((4, 128)))
    for shift, tile in ((1, high), (-1, low)):
        rows = peer_rows(shift, pitch)
        packed = tile_to_rows(tile, pad)
        message[rows, :] = jnp.where(mine, message[rows, :], packed)


def interior(weighted, trans, near):
    lane = lanes((STEP, 128))
    sub = subs((STEP, 128)) & 7
    zero = jnp.zeros((8, 128), F32)
    up = [trans[2, chunk(t), :].astype(F32) for t in range(CHUNKS)]
    for t in range(CHUNKS):
        rows = chunk(t)
        tx, ty = [trans[n, rows, :].astype(F32) for n in range(2)]
        tz = up[t]
        for n in range(3):
            value = weighted[n, rows, :]
            px, py = tx * value, ty * value
            nx = jnp.where(sub == 0, 0.0, pltpu.roll(px, 1, 0)) + jnp.where(
                sub == 7, 0.0, pltpu.roll(px, STEP - 1, 0)
            )
            ny = jnp.where(lane == 0, 0.0, pltpu.roll(py, 1, 1)) + jnp.where(
                lane == 127, 0.0, pltpu.roll(py, 127, 1)
            )
            pz = tz * value
            below = zero
            above = zero
            if t:
                below = up[t - 1][8:16] * weighted[n, pl.ds(t * STEP - 8, 8), :]
            if t + 1 < CHUNKS:
                above = up[t + 1][0:8] * weighted[n, pl.ds(t * STEP + STEP, 8), :]
            nz = jnp.concatenate([below + pz[8:16], pz[0:8] + above], axis=0)
            near[n, rows, :] = tx * nx + ty * ny + tz * nz


def cell_setup(rhs_in, diag_in, mobility_in, trans_in, cells_in, pi_in, index_in, parent_in,
               across_in, source_in,
               rows_of, rows_to, start, weight, slots, fixed, inverse,
               weighted, toward_low, toward_high, message, along, pad, forward, own,
               rhs, diag, mobility, trans, cells, pi, index, parent, across, source, sems):
    pairs = ((cells_in, cells), (pi_in, pi), (index_in, index), (parent_in, parent),
             (across_in, across), (source_in, source), (rhs_in, rhs), (diag_in, diag),
             (mobility_in, mobility), (trans_in, trans))
    copies = [pltpu.make_async_copy(a, b, sems.at[n]) for n, (a, b) in enumerate(pairs)]
    for copy in copies:
        copy.start()
    for copy in copies[:6]:
        copy.wait()
    zeros = jnp.zeros((6, 128), F32)
    linked = jnp.concatenate([(parent[...] >= 0).astype(F32), zeros], axis=0)
    moving = jnp.concatenate([across[...], zeros], axis=0)
    given = jnp.concatenate([source[...], zeros], axis=0)
    partial = moving + following(linked * moving)
    fixed[0] = linked
    fixed[1] = moving
    fixed[2] = given
    fixed[3] = partial
    number = index[...]
    own[field(1), :], own[field(3), :] = halves(to_columns(segment_values(given, number)))
    own[field(4), :], own[field(5), :] = halves(to_columns(segment_values(partial, number)))
    own[field(7), :] = jnp.zeros((PEERS, 128), F32)
    base = cells[0:1, :]
    row = lax.shift_right_logical(base, 7)
    live = pi[...]
    gap = jnp.zeros((44, 128), F32)
    info = jnp.concatenate(
        [jnp.broadcast_to(row.astype(F32), (8, 128)),
         jnp.broadcast_to((base & 127).astype(F32), (8, 128)),
         gap, live[0:4], gap, jnp.zeros((16, 128), F32), live[4:8]],
        axis=0,
    ).T
    rows_to[...] = (subs((ROWS, PEERS)) == jnp.broadcast_to(row, (ROWS, PEERS))).astype(F32).astype(BF16)
    row_column = jnp.broadcast_to(info[:, 0:1], (PEERS, ROWS)).astype(jnp.int32)
    rows_of[...] = (lanes((PEERS, ROWS)) == row_column).astype(F32).astype(BF16)
    begin = jnp.broadcast_to(info[:, 8:9], (PEERS, 128)).astype(jnp.int32)
    start[...] = begin
    weights = jnp.where(is_slot(lanes((PEERS, 128))), info, 0.0)
    weight[...] = weights
    own[field(6), :] = halves(weights)[1]
    high = halves(live)[0]
    order = number.astype(F32)
    common = jnp.concatenate([high, order], axis=0).astype(BF16)
    for d in range(0, PEERS, 2):
        message[pl.ds(24 * d + 32, 16), :] = common
    for copy in copies[6:8]:
        copy.wait()
    for t in range(CHUNKS):
        rows = chunk(t)
        invert(diag, rows, inverse)
        values = mix(inverse, rows, [rhs[n, rows, :] for n in range(3)])
        forward[rows, :] = values[0]
        for n in range(3):
            weighted[n, rows, :] = values[n]
    values = slot_values(rows_of[...], begin, forward[...])
    slots[...] = values
    own[field(0), :], own[field(2), :] = halves(values)
    for copy in copies[8:]:
        copy.wait()
    for t in range(CHUNKS):
        values = [weighted[n, chunk(t), :] for n in range(3)]
        borders(values, mobility, trans, weighted, along, t)
    send_borders(trans, weighted, along, toward_low, toward_high, own, pad, 8)
    for d in range(0, PEERS, 2):
        two = [own[pl.ds(8 * d, 8), :], high, order, own[pl.ds(8 * d + 8, 8), :]]
        message[pl.ds(24 * d, 32), :] = jnp.concatenate(two, axis=0).astype(BF16)


def well_tables(index, table):
    low = index[...] & 127
    for k in range(CAP):
        hit = subs((128, 128)) == jnp.broadcast_to(low[k : k + 1], (128, 128))
        table[:, 128 * k : 128 * (k + 1)] = hit.astype(F32).astype(BF16)


def well_setup(arrived, index, table, fixed, message, weight, state, at_slots, diagonal,
               wide, turned):
    wide[...] = arrived[...].astype(F32)

    def part(n):
        return wide[pl.ds(n, PEERS, stride=24), :]

    lane = lanes((PEERS, 128))
    mine = lane == me()
    for k in range(CAP):
        turned[k] = part(8 + k).T
    total = part(4) + part(5)
    for k in range(CAP):
        target = jnp.sum(jnp.where(mine, part(16 + k), 0.0), axis=1, keepdims=True)
        target = jnp.broadcast_to(target, (PEERS, 128))
        found = jnp.zeros((PEERS, 128), F32)
        for m in range(CAP):
            found += jnp.where(part(16 + m) == target, turned[m], 0.0)
        place = 60 + k if k < 4 else 120 + k
        total += jnp.where(lane == place, jnp.sum(found, axis=1, keepdims=True), 0.0)
    slot = is_slot(lane)
    pressures = (part(1) + part(3)) / jnp.where(slot, total, 1.0)
    message[block(0), :] = jnp.where(slot, part(0) + part(2), part(0))
    message[block(1), :] = jnp.where(slot, pressures, part(1))
    message[block(2), :] = part(2)
    message[block(3), :] = part(3)
    pi = jnp.concatenate([turned[k, pl.ds(me(), 1), :] for k in range(CAP)], axis=0)
    pi += to_rows(part(6))
    weight[...] = pi
    number = index[...]
    total = fixed[3] + into_segments(pi, number, table[...])
    total = jnp.where(subs((8, 128)) < 2, total, 1.0)
    diagonal[...] = total
    now = fixed[2] / total
    state[...] = now
    at_slots[...] = segment_values(now, number)


def ratio(sums, place):
    total = jnp.sum(sums, axis=0, keepdims=True)
    lane = lanes((1, 128))
    numer = jnp.sum(jnp.where(lane == place, total, 0.0), axis=1, keepdims=True)
    denom = jnp.sum(jnp.where(lane == place + 1, total, 0.0), axis=1, keepdims=True)
    return numer / denom


def parts_of(x):
    high, rest = halves(x)
    return (high,) + halves(rest)


def carried(own, relayed):
    lane = lanes((8, 128))
    row = jnp.zeros((8, 128), F32)
    for n, part in enumerate(parts_of(own) + parts_of(relayed)):
        moved = pltpu.roll(part, 2 * n, 1) if n else part
        row = jnp.where((lane >> 1) == n, moved, row)
    return row[0:1]


def collected(rows):
    lane, source = lanes((PEERS, 128)), subs((PEERS, 128))

    def at(shift):
        return source == ((me() + shift) & (PEERS - 1))

    direct = (lane < 6) & ~(at(1) | at(-1))
    through = (lane >= 6) & (lane < 12) & (at(15) | at(17))
    total = jnp.sum(jnp.where(direct | through, rows, 0.0), axis=0, keepdims=True)
    odd = (lanes((1, 128)) & 1) == 1
    numer = jnp.sum(jnp.where(odd, 0.0, total), axis=1, keepdims=True)
    denom = jnp.sum(jnp.where(odd, total, 0.0), axis=1, keepdims=True)
    return numer / denom


def spread_pair(two):
    return jnp.concatenate(
        [jnp.broadcast_to(two[h : h + 1], (8, 128)) for h in range(2)], axis=0
    )


STEADY = ("rhs", "mobility", "trans", "rows_of", "rows_to", "start", "weight",
          "own_weight", "table", "index", "fixed", "diagonal")
MOVING = ("arrived", "near", "from_low", "from_high", "slots", "at_slots", "state")
NEXT = ("weighted", "toward_low", "toward_high", "message", "slots", "at_slots", "state")
MORE_IN = {
    "plain": ("inverse",), "keep": ("inverse",), "last": ("inverse", "diag", "field"),
    "after": ("inverse", "sums"), "omega": ("inverse",),
    "final": ("diag", "field", "change", "seg_change", "omega"),
}
MORE_OUT = {
    "plain": (), "keep": ("field",), "last": ("change", "seg_change", "sums"),
    "after": (), "omega": ("omega",), "final": (),
}


def results_of(kind):
    return ("message",) if kind == "final" else NEXT + MORE_OUT[kind]


def sweep(kind, *refs):
    take = iter(refs)
    now = {name: next(take) for name in MOVING}
    fixed = {name: next(take) for name in STEADY}
    extra = {name: next(take) for name in MORE_IN[kind]}
    out = {name: next(take) for name in results_of(kind)}
    along, pad, forward, wide = take
    weighted = out.get("weighted")
    final = kind == "final"
    gx, gy = lax.axis_index("gx"), lax.axis_index("gy")

    arrived = now["arrived"]
    if arrived.dtype == BF16:
        wide[...] = arrived[...].astype(F32)
        arrived = wide
        heads = arrived[block(0), :] + arrived[block(2), :]
        pressures = arrived[block(1), :] + arrived[block(3), :]
    else:
        heads, pressures = arrived[block(0), :], arrived[block(1), :]
    pull = fixed["weight"][...] * (now["slots"][...] - pressures)
    perforated = into_cells(fixed["rows_to"][...], fixed["start"][...], pull)

    side_low = rows_to_tile(arrived[peer_rows(-1), :], pad)
    side_high = rows_to_tile(arrived[peer_rows(1), :], pad)
    side_low = jnp.where(gy == 0, 0.0, side_low)
    side_high = jnp.where(gy == lax.axis_size("gy") - 1, 0.0, side_high)
    small = lanes((8, 128))
    ahead = pltpu.roll(side_high, 127, 1)
    sides = [jnp.where((small & 1) == odd, side_low, ahead) for odd in range(2)]
    open_low, open_high = gx > 0, gx < lax.axis_size("gx") - 1

    state = now["state"][...]
    linked, across, source = [fixed["fixed"][n] for n in range(3)]
    push = fixed["own_weight"][...] * (to_rows(heads) - now["at_slots"][...])
    number = fixed["index"][...]
    inflow = into_segments(push, number, fixed["table"][...])
    flux = across * (state - linked * previous(state))
    seg_res = source - flux + following(linked * flux) + inflow

    lane = lanes((STEP, 128))
    sub = subs((STEP, 128)) & 7
    numer = jnp.zeros((STEP, 128), F32)
    denom = jnp.zeros((STEP, 128), F32)
    if final:
        omega = extra["omega"][0:1, 0:1]
    for t in range(CHUNKS):
        rows = chunk(t)
        tx, ty = [fixed["trans"][n, rows, :].astype(F32) for n in range(2)]
        tx = jnp.where(
            sub == 0, jnp.where(open_low, tx, 0.0),
            jnp.where((sub == 7) & open_high, tx, 0.0),
        )
        ty = jnp.where((lane == 0) | (lane == 127), ty, 0.0)
        terms = []
        for n in range(3):
            j = n * NZ + 2 * t
            low, high = now["from_low"][j : j + 2, :], now["from_high"][j : j + 2, :]
            nx = jnp.where(sub == 0, spread_pair(low), spread_pair(high))
            ny = jnp.concatenate(
                [pltpu.roll(sides[(j + h) & 1], (128 - j - h) % 128, 1) for h in range(2)], axis=0
            )
            share = fixed["mobility"][3 * n, rows, :].astype(F32)
            value = now["near"][n, rows, :] + tx * nx + ty * ny
            terms.append(value - share * perforated[t * STEP : (t + 1) * STEP])
        if kind in ("last", "final"):
            own = mix(extra["diag"], rows, [extra["field"][n, rows, :] for n in range(3)])
            for n in range(3):
                change = own[n] - terms[n]
                before = fixed["rhs"][n, rows, :]
                if final:
                    kept = extra["change"][n, rows, :]
                    before = before - omega * kept
                    change = kept + omega * (change - 2.0 * kept)
                else:
                    out["change"][n, rows, :] = change
                numer += before * change
                denom += change * change
        if not final:
            total = [fixed["rhs"][n, rows, :] + terms[n] for n in range(3)]
            values = mix(extra["inverse"], rows, total)
            forward[rows, :] = values[0]
            if kind == "keep":
                for n in range(3):
                    out["field"][n, rows, :] = values[n]
            borders(values, fixed["mobility"], fixed["trans"], weighted, along, t)

    if kind in ("last", "final"):
        before = source
        change = source - seg_res
        if final:
            kept = extra["seg_change"][...]
            before = source - omega * kept
            change = kept + omega * (change - 2.0 * kept)
        else:
            out["seg_change"][...] = change
        above = jnp.sum(numer, keepdims=True) + jnp.sum(before * change, keepdims=True)
        below = jnp.sum(denom, keepdims=True) + jnp.sum(change * change, keepdims=True)
        place = lanes((PEERS, 128))
        if final:
            out["message"][...] = jnp.where(
                place == 60, above, jnp.where(place == 61, below, 0.0)
            )
            return
        sums = jnp.where(small == 0, above, jnp.where(small == 1, below, 0.0))
        out["sums"][...] = sums
        out["toward_high"][60:64, :] = sums[0:4]
    if kind == "omega":
        out["omega"][...] = jnp.broadcast_to(collected(arrived[block(0), :]), (8, 128))
    message = wide
    advanced = state + seg_res / fixed["diagonal"][...]
    out["state"][...] = advanced
    values = segment_values(advanced, number)
    out["at_slots"][...] = values
    cells = slot_values(fixed["rows_of"][...], fixed["start"][...], forward[...])
    out["slots"][...] = cells
    high, message[block(2), :] = halves(cells)
    if kind == "after":
        relayed = jnp.broadcast_to(now["from_low"][60:61, :], (8, 128))
        row = jnp.broadcast_to(carried(extra["sums"][...], relayed), (PEERS, 128))
        high = jnp.where(lanes((PEERS, 128)) < 12, row, high)
    message[block(0), :] = high
    message[block(1), :], message[block(3), :] = halves(to_columns(values))
    toward_high = out["toward_high"]
    if kind == "last":
        toward_high = toward_high.at[pl.ds(0, 3 * NZ), :]
    send_borders(fixed["trans"], weighted, along, out["toward_low"], toward_high, message, pad)
    out["message"][...] = message[...].astype(BF16)


def finish(arrived, omega, field_one, field_two, state_one, state_two, cells, segments):
    first = omega[0:1, 0:1]
    second = ratio(arrived[...], 60)

    def blend(one, two):
        kept = first * one
        return kept + second * (one + first * (two - one) - kept)

    for n in range(3):
        for t in range(CHUNKS):
            rows = chunk(t)
            cells[n, rows, :] = blend(field_one[n, rows, :], field_two[n, rows, :])
    segments[...] = blend(state_one[0:2], state_two[0:2])


CELLS = ((3, ROWS, 128), F32)
PAIRS = ((PEERS, 128), F32)
MESSAGE = ((4 * PEERS, 128), F32)
TILE = ((8, 128), F32)
EDGE = ((3 * NZ, 128), F32)
SHAPES = {
    "weighted": CELLS, "toward_low": EDGE, "toward_high": EDGE, "message": MESSAGE, "slots": PAIRS,
    "at_slots": TILE, "state": TILE, "omega": TILE, "field": CELLS, "change": CELLS,
    "seg_change": TILE, "sums": TILE,
}


def shape_of(kind, name):
    if kind == "last" and name == "toward_high":
        return ((64, 128), F32)
    if name != "message":
        return SHAPES[name]
    if kind == "final":
        return PAIRS
    return (MESSAGE[0], BF16)


SCRATCH = (
    pltpu.VMEM((3 * ROWS, 128), F32),
    pltpu.VMEM((16, 128), F32),
    pltpu.VMEM((ROWS, 128), F32),
)


def call(body, outs, args, scratch=(), name=None, space=pltpu.VMEM, grant=24 * 1024 * 1024):
    moved = sum(a.size * a.dtype.itemsize for a in args)
    return pl.pallas_call(
        body,
        out_shape=[jax.ShapeDtypeStruct(*out) for out in outs],
        in_specs=[pl.BlockSpec(memory_space=space)] * len(args),
        out_specs=[pl.BlockSpec(memory_space=pltpu.VMEM)] * len(outs),
        scratch_shapes=list(scratch),
        compiler_params=pltpu.CompilerParams(vmem_limit_bytes=grant),
        cost_estimate=pl.CostEstimate(flops=4_000_000, bytes_accessed=moved, transcendentals=0),
        name=name,
    )(*args)


def exchange(message):
    return lax.all_to_all(message, AXES, split_axis=0, concat_axis=0, tiled=True)


def neighbours(toward_low, toward_high):
    count = lax.axis_size("gx")
    up = [(i, (i + 1) % count) for i in range(count)]
    down = [(b, a) for a, b in up]
    return {
        "from_low": lax.ppermute(toward_high, "gx", up),
        "from_high": lax.ppermute(toward_low, "gx", down),
    }


def on_device(
    rhs, diag_block, mobility, trans, perf_cell, perf_pi, perf_seg, seg_parent, seg_trans, seg_rhs
):
    rhs = rhs.reshape(3, ROWS, 128)
    diag = diag_block.reshape(9, ROWS, 128)
    mobility = mobility.reshape(9, ROWS, 128)
    trans = trans.reshape(3, ROWS, 128)
    index = perf_seg[0]

    fixed = {"rhs": rhs, "mobility": mobility, "trans": trans, "index": index}
    inputs = [rhs, diag, mobility, trans, perf_cell[0], perf_pi[0], index]
    inputs += [a.reshape(2, 128) for a in (seg_parent, seg_trans, seg_rhs)]
    (rows_of, rows_to, start, weight, slots, constants, inverse, weighted, toward_low, toward_high,
     message) = call(
        cell_setup,
        [((PEERS, ROWS), BF16), ((ROWS, PEERS), BF16),
         ((PEERS, 128), jnp.int32), PAIRS, PAIRS, ((4, 8, 128), F32), ((9, ROWS, 128), F32), CELLS, EDGE, EDGE,
         ((24 * PEERS, 128), BF16)],
        inputs,
        SCRATCH + (pltpu.VMEM((8 * PEERS, 128), F32),)
        + tuple(pltpu.VMEM(a.shape, a.dtype) for a in inputs) + (pltpu.SemaphoreType.DMA((10,)),),
        name="cell_setup",
        space=pltpu.HBM,
        grant=64 * 1024 * 1024 - 256 * 1024,
    )
    arrived = exchange(message)

    def inside(weighted):
        return call(interior, [CELLS], [weighted, trans], name="interior")[0]

    (table,) = call(well_tables, [((128, CAP * 128), BF16)], [index], name="well_tables")
    fixed.update(rows_of=rows_of, rows_to=rows_to, start=start, weight=weight)
    now = {"near": inside(weighted), "slots": slots}
    now.update(neighbours(toward_low, toward_high))
    now["arrived"], own_weight, state, at_slots, diagonal = call(
        well_setup,
        [MESSAGE, TILE, TILE, TILE, TILE],
        [arrived, index, table, constants],
        [pltpu.VMEM((24 * PEERS, 128), F32), pltpu.VMEM((CAP, PEERS, 128), F32)],
        name="well_setup",
    )
    fixed.update(own_weight=own_weight, table=table, fixed=constants, diagonal=diagonal)
    now.update(at_slots=at_slots, state=state)
    saved = {"inverse": inverse, "diag": diag}

    def advance(kind, now):
        args = [now[name] for name in MOVING]
        args += [fixed[name] for name in STEADY]
        args += [saved[name] for name in MORE_IN[kind]]
        names = results_of(kind)
        out = call(
            functools.partial(sweep, kind),
            [shape_of(kind, name) for name in names],
            args,
            SCRATCH + (pltpu.VMEM(*MESSAGE),),
            name="sweep_" + kind,
        )
        out = dict(zip(names, out))
        out["arrived"] = exchange(out.pop("message"))
        if kind != "final":
            out.update(neighbours(out.pop("toward_low"), out.pop("toward_high")))
            out["near"] = inside(out.pop("weighted"))
        return out

    now = advance("plain", now)
    now = advance("plain", now)
    one = advance("keep", now)
    saved["field"] = one["field"]
    now = advance("last", one)
    saved.update(change=now["change"], seg_change=now["seg_change"], sums=now["sums"])
    now = advance("after", now)
    now = advance("omega", now)
    saved["omega"] = now["omega"]
    two = advance("keep", now)
    saved["field"] = two["field"]
    sums = advance("final", two)
    cells, segments = call(
        finish,
        [CELLS, ((2, 128), F32)],
        [sums["arrived"], saved["omega"], one["field"], two["field"], one["state"], two["state"]],
        name="finish",
    )
    return cells.reshape(3, NZ, CX, CY), segments.reshape(256)


def solution(mesh):
    grid = P(None, None, "gx", "gy")
    pairs = P(AXES, None, None)
    flat = P(AXES)
    return jax.shard_map(
        on_device,
        mesh=mesh,
        in_specs=(grid, grid, grid, grid, pairs, pairs, pairs, flat, flat, flat),
        out_specs=(grid, flat),
        check_vma=False,
    )
```

```python
import functools

import jax
import jax.numpy as jnp
from jax import lax
from jax.experimental import pallas as pl
from jax.experimental.pallas import tpu as pltpu
from jax.sharding import PartitionSpec as P

F32 = jnp.float32
BF16 = jnp.bfloat16
AXES = ("gx", "gy")
NZ, CX, CY = 20, 8, 128
ROWS = NZ * CX
STEP = 16
CHUNKS = ROWS // STEP
PEERS = 128
CAP = 8


def lanes(shape):
    return lax.broadcasted_iota(jnp.int32, shape, 1)


def subs(shape):
    return lax.broadcasted_iota(jnp.int32, shape, 0)


def halves(x):
    high = x.astype(BF16).astype(F32)
    return high, x - high


def pick_rows(onehot, x):
    def dot(part):
        return lax.dot_general(
            onehot, part.astype(BF16), (((1,), (0,)), ((), ())), preferred_element_type=F32
        )

    high, low = halves(x)
    return dot(low) + dot(high)


def is_slot(lane):
    return (lane & 63) >= 60


def slot_values(rows_of, start, first):
    lane = lanes((PEERS, CY))
    number = (lane & 3) + jnp.where(lane >= 64, 4, 0)
    picked = pick_rows(rows_of, first)
    window = jnp.take_along_axis(picked, (start + number) & (CY - 1), axis=1)
    return jnp.where(is_slot(lane), window, 0.0)


def into_cells(rows_to, start, flows):
    number = (lanes((PEERS, CY)) - start) & (CY - 1)
    place = jnp.where(number < 4, number + 60, jnp.where(number < CAP, number + 120, 0))
    return pick_rows(rows_to, jnp.take_along_axis(flows, place, axis=1))


def segment_values(state, index):
    low = index & 127
    first = jnp.take_along_axis(jnp.broadcast_to(state[0:1], (8, 128)), low, axis=1)
    second = jnp.take_along_axis(jnp.broadcast_to(state[1:2], (8, 128)), low, axis=1)
    return jnp.where(index >= 128, second, first)


def into_segments(values, index, table):
    parts = halves(values)
    sub = subs((16, 128))
    upper = (index >= 128).astype(jnp.int32)
    tiles = []
    for k in range(CAP):
        row = [jnp.broadcast_to(part[k : k + 1], (16, 128)) for part in parts]
        mine = jnp.broadcast_to(upper[k : k + 1], (16, 128)) == (sub & 1)
        tile = jnp.where(sub < 2, row[0], row[1])
        tiles.append(jnp.where(mine & (sub < 4), tile, 0.0).astype(BF16))
    left = jnp.concatenate(tiles, axis=1)
    out = lax.dot_general(left, table, (((1,), (1,)), ((), ())), preferred_element_type=F32)[:8]
    return jnp.where(subs((8, 128)) < 2, pltpu.roll(out, 6, 0) + out, 0.0)


def previous(state):
    moved = pltpu.roll(state, 1, 1)
    return jnp.where(lanes((8, 128)) == 0, pltpu.roll(moved, 1, 0), moved)


def following(state):
    moved = pltpu.roll(state, 127, 1)
    return jnp.where(lanes((8, 128)) == 127, pltpu.roll(moved, 7, 0), moved)


def to_columns(values):
    gap = jnp.zeros((60, 128), F32)
    return jnp.concatenate([gap, values[0:4], gap, values[4:8]], axis=0).T


def to_rows(columns):
    turned = columns.T
    return jnp.concatenate([turned[60:64], turned[124:128]], axis=0)


def field(n):
    return pl.ds(n, PEERS, stride=8)


def block(n):
    return pl.ds(n, PEERS, stride=4)


def chunk(t):
    return pl.ds(t * STEP, STEP)


def me():
    return lax.axis_index("gx") * 16 + lax.axis_index("gy")


def peer_rows(shift, pitch=4):
    return pl.ds(pitch * ((me() + shift) & (PEERS - 1)), 4)


def tile_to_rows(tile, pad):
    pad[0:8] = tile
    pad[8:16] = pltpu.roll(tile, 64, 1)
    even = pad[pl.ds(0, 4, stride=2), :]
    odd = pad[pl.ds(9, 4, stride=2), :]
    return jnp.where(lanes((4, 128)) < 64, even, odd)


def rows_to_tile(four, pad):
    pad[0:4] = four
    pad[8:16] = pltpu.roll(pad[0:8], 64, 1)
    low, high = pad[0:4], pad[8:12]
    pad[pl.ds(0, 4, stride=2), :] = low
    pad[pl.ds(1, 4, stride=2), :] = high
    return pad[0:8]


def mix(matrix, rows, vector):
    entry = [matrix[n, rows, :].astype(F32) for n in range(9)]
    x, y, z = vector
    return [entry[3 * n] * x + entry[3 * n + 1] * y + entry[3 * n + 2] * z for n in range(3)]


def solve(diag, rows, vector, scale=None):
    a, b, c, d, e, f, g, h, i = [diag[n, rows, :].astype(F32) for n in range(9)]
    x, y, z = vector
    p, q, s = e * i - f * h, f * g - d * i, d * h - e * g
    if scale is None:
        scale = 1.0 / (a * p + b * q + c * s)
    return [
        (p * x + (c * h - b * i) * y + (b * f - c * e) * z) * scale,
        (q * x + (a * i - c * g) * y + (c * d - a * f) * z) * scale,
        (s * x + (b * g - a * h) * y + (a * e - b * d) * z) * scale,
    ], scale


def borders(values, mobility, trans, weighted, along, t):
    rows = chunk(t)
    tx = trans[0, rows, :].astype(F32)
    for n, value in enumerate(mix(mobility, rows, values)):
        weighted[n, rows, :] = value
        along[pl.ds(n * ROWS + t * STEP, STEP), :] = tx * value


def send_borders(trans, weighted, along, toward_low, toward_high, message, pad, pitch=4):
    toward_low[...] = along[pl.ds(0, 3 * NZ, stride=CX), :]
    toward_high[...] = along[pl.ds(CX - 1, 3 * NZ, stride=CX), :]
    small = lanes((8, 128))
    high = jnp.zeros((8, 128), F32)
    low = jnp.zeros((8, 128), F32)
    for t in range(CHUNKS):
        ty = trans[1, chunk(t), :].astype(F32)
        for n in range(3):
            py = ty * weighted[n, chunk(t), :]
            for half in range(2):
                j = n * NZ + 2 * t + half
                moved = pltpu.roll(py[8 * half : 8 * half + 8], j + 1, 1)
                high = jnp.where(small == j, moved, high)
                low = jnp.where(small == j + 1, moved, low)
    low = pltpu.roll(low, 127, 1)
    mine = is_slot(lanes((4, 128)))
    for shift, tile in ((1, high), (-1, low)):
        rows = peer_rows(shift, pitch)
        packed = tile_to_rows(tile, pad)
        message[rows, :] = jnp.where(mine, message[rows, :], packed)


def interior(weighted, trans, rhs, near):
    lane = lanes((STEP, 128))
    sub = subs((STEP, 128)) & 7
    zero = jnp.zeros((8, 128), F32)
    up = [trans[2, chunk(t), :].astype(F32) for t in range(CHUNKS)]
    for t in range(CHUNKS):
        rows = chunk(t)
        tx, ty = [trans[n, rows, :].astype(F32) for n in range(2)]
        tz = up[t]
        for n in range(3):
            value = weighted[n, rows, :]
            px, py = tx * value, ty * value
            nx = jnp.where(sub == 0, 0.0, pltpu.roll(px, 1, 0)) + jnp.where(
                sub == 7, 0.0, pltpu.roll(px, STEP - 1, 0)
            )
            ny = jnp.where(lane == 0, 0.0, pltpu.roll(py, 1, 1)) + jnp.where(
                lane == 127, 0.0, pltpu.roll(py, 127, 1)
            )
            pz = tz * value
            below = zero
            above = zero
            if t:
                below = up[t - 1][8:16] * weighted[n, pl.ds(t * STEP - 8, 8), :]
            if t + 1 < CHUNKS:
                above = up[t + 1][0:8] * weighted[n, pl.ds(t * STEP + STEP, 8), :]
            nz = jnp.concatenate([below + pz[8:16], pz[0:8] + above], axis=0)
            near[n, rows, :] = rhs[n, rows, :] + (tx * nx + ty * ny + tz * nz)


def cell_setup(rhs_in, diag_in, mobility_in, trans_in, cells_in, pi_in, index_in, parent_in,
               across_in, source_in,
               rows_of, rows_to, start, weight, slots, fixed, scale,
               weighted, toward_low, toward_high, message, along, pad, forward, own,
               rhs, diag, mobility, trans, cells, pi, index, parent, across, source, sems):
    pairs = ((cells_in, cells), (pi_in, pi), (index_in, index), (parent_in, parent),
             (across_in, across), (source_in, source), (rhs_in, rhs), (diag_in, diag),
             (mobility_in, mobility), (trans_in, trans))
    copies = [pltpu.make_async_copy(a, b, sems.at[n]) for n, (a, b) in enumerate(pairs)]
    for copy in copies:
        copy.start()
    for copy in copies[:6]:
        copy.wait()
    zeros = jnp.zeros((6, 128), F32)
    linked = jnp.concatenate([(parent[...] >= 0).astype(F32), zeros], axis=0)
    moving = jnp.concatenate([across[...], zeros], axis=0)
    given = jnp.concatenate([source[...], zeros], axis=0)
    partial = moving + following(linked * moving)
    fixed[0] = linked
    fixed[1] = moving
    fixed[2] = given
    fixed[3] = partial
    number = index[...]
    own[field(1), :], own[field(3), :] = halves(to_columns(segment_values(given, number)))
    own[field(4), :], own[field(5), :] = halves(to_columns(segment_values(partial, number)))
    own[field(7), :] = jnp.zeros((PEERS, 128), F32)
    base = cells[0:1, :]
    row = lax.shift_right_logical(base, 7)
    live = pi[...]
    gap = jnp.zeros((44, 128), F32)
    info = jnp.concatenate(
        [jnp.broadcast_to(row.astype(F32), (8, 128)),
         jnp.broadcast_to((base & 127).astype(F32), (8, 128)),
         gap, live[0:4], gap, jnp.zeros((16, 128), F32), live[4:8]],
        axis=0,
    ).T
    rows_to[...] = (subs((ROWS, PEERS)) == jnp.broadcast_to(row, (ROWS, PEERS))).astype(F32).astype(BF16)
    row_column = jnp.broadcast_to(info[:, 0:1], (PEERS, ROWS)).astype(jnp.int32)
    rows_of[...] = (lanes((PEERS, ROWS)) == row_column).astype(F32).astype(BF16)
    begin = jnp.broadcast_to(info[:, 8:9], (PEERS, 128)).astype(jnp.int32)
    start[...] = begin
    weights = jnp.where(is_slot(lanes((PEERS, 128))), info, 0.0)
    weight[...] = weights
    own[field(6), :] = halves(weights)[1]
    high = halves(live)[0]
    order = number.astype(F32)
    common = jnp.concatenate([high, order], axis=0).astype(BF16)
    for d in range(0, PEERS, 2):
        message[pl.ds(24 * d + 32, 16), :] = common
    for copy in copies[6:8]:
        copy.wait()
    for t in range(CHUNKS):
        rows = chunk(t)
        values, scale[rows, :] = solve(diag, rows, [rhs[n, rows, :] for n in range(3)])
        forward[rows, :] = values[0]
        for n in range(3):
            weighted[n, rows, :] = values[n]
    values = slot_values(rows_of[...], begin, forward[...])
    slots[...] = values
    own[field(0), :], own[field(2), :] = halves(values)
    for copy in copies[8:]:
        copy.wait()
    for t in range(CHUNKS):
        values = [weighted[n, chunk(t), :] for n in range(3)]
        borders(values, mobility, trans, weighted, along, t)
    send_borders(trans, weighted, along, toward_low, toward_high, own, pad, 8)
    for d in range(0, PEERS, 2):
        two = [own[pl.ds(8 * d, 8), :], high, order, own[pl.ds(8 * d + 8, 8), :]]
        message[pl.ds(24 * d, 32), :] = jnp.concatenate(two, axis=0).astype(BF16)


def well_tables(index, table):
    low = index[...] & 127
    for k in range(CAP):
        hit = subs((128, 128)) == jnp.broadcast_to(low[k : k + 1], (128, 128))
        table[:, 128 * k : 128 * (k + 1)] = hit.astype(F32).astype(BF16)


def well_setup(arrived, index, table, fixed, message, weight, state, at_slots, diagonal,
               wide, turned):
    wide[...] = arrived[...].astype(F32)

    def part(n):
        return wide[pl.ds(n, PEERS, stride=24), :]

    lane = lanes((PEERS, 128))
    mine = lane == me()
    for k in range(CAP):
        turned[k] = part(8 + k).T
    total = part(4) + part(5)
    for k in range(CAP):
        target = jnp.sum(jnp.where(mine, part(16 + k), 0.0), axis=1, keepdims=True)
        target = jnp.broadcast_to(target, (PEERS, 128))
        found = jnp.zeros((PEERS, 128), F32)
        for m in range(CAP):
            found += jnp.where(part(16 + m) == target, turned[m], 0.0)
        place = 60 + k if k < 4 else 120 + k
        total += jnp.where(lane == place, jnp.sum(found, axis=1, keepdims=True), 0.0)
    slot = is_slot(lane)
    pressures = (part(1) + part(3)) / jnp.where(slot, total, 1.0)
    message[block(0), :] = jnp.where(slot, part(0) + part(2), part(0))
    message[block(1), :] = jnp.where(slot, pressures, part(1))
    message[block(2), :] = part(2)
    message[block(3), :] = part(3)
    pi = jnp.concatenate([turned[k, pl.ds(me(), 1), :] for k in range(CAP)], axis=0)
    pi += to_rows(part(6))
    weight[...] = pi
    number = index[...]
    total = fixed[3] + into_segments(pi, number, table[...])
    total = jnp.where(subs((8, 128)) < 2, total, 1.0)
    diagonal[...] = total
    now = fixed[2] / total
    state[...] = now
    at_slots[...] = segment_values(now, number)


def ratio(sums, place):
    total = jnp.sum(sums, axis=0, keepdims=True)
    lane = lanes((1, 128))
    numer = jnp.sum(jnp.where(lane == place, total, 0.0), axis=1, keepdims=True)
    denom = jnp.sum(jnp.where(lane == place + 1, total, 0.0), axis=1, keepdims=True)
    return numer / denom


def parts_of(x):
    high, rest = halves(x)
    return (high,) + halves(rest)


def carried(own, relayed):
    lane = lanes((8, 128))
    row = jnp.zeros((8, 128), F32)
    for n, part in enumerate(parts_of(own) + parts_of(relayed)):
        moved = pltpu.roll(part, 2 * n, 1) if n else part
        row = jnp.where((lane >> 1) == n, moved, row)
    return row[0:1]


def collected(rows):
    lane, source = lanes((PEERS, 128)), subs((PEERS, 128))

    def at(shift):
        return source == ((me() + shift) & (PEERS - 1))

    direct = (lane < 6) & ~(at(1) | at(-1))
    through = (lane >= 6) & (lane < 12) & (at(15) | at(17))
    total = jnp.sum(jnp.where(direct | through, rows, 0.0), axis=0, keepdims=True)
    odd = (lanes((1, 128)) & 1) == 1
    numer = jnp.sum(jnp.where(odd, 0.0, total), axis=1, keepdims=True)
    denom = jnp.sum(jnp.where(odd, total, 0.0), axis=1, keepdims=True)
    return numer / denom


def spread_pair(two):
    return jnp.concatenate(
        [jnp.broadcast_to(two[h : h + 1], (8, 128)) for h in range(2)], axis=0
    )


STEADY = ("diag", "mobility", "trans", "rows_of", "rows_to", "start", "weight",
          "own_weight", "table", "index", "fixed", "diagonal", "scale")
MOVING = ("arrived", "near", "from_low", "from_high", "slots", "at_slots", "state")
NEXT = ("weighted", "toward_low", "toward_high", "message", "slots", "at_slots", "state")
MORE_IN = {
    "plain": (), "keep": (), "last": ("rhs", "field"), "after": ("sums",), "omega": (),
    "final": ("rhs", "field", "change", "seg_change", "omega"),
}
MORE_OUT = {
    "plain": (), "keep": ("field",), "last": ("change", "seg_change", "sums"),
    "after": (), "omega": ("omega",), "final": (),
}


def results_of(kind):
    return ("message",) if kind == "final" else NEXT + MORE_OUT[kind]


def sweep(kind, *refs):
    take = iter(refs)
    now = {name: next(take) for name in MOVING}
    fixed = {name: next(take) for name in STEADY}
    extra = {name: next(take) for name in MORE_IN[kind]}
    out = {name: next(take) for name in results_of(kind)}
    along, pad, forward, wide = take
    weighted = out.get("weighted")
    final = kind == "final"
    gx, gy = lax.axis_index("gx"), lax.axis_index("gy")

    arrived = now["arrived"]
    if arrived.dtype == BF16:
        wide[...] = arrived[...].astype(F32)
        arrived = wide
        heads = arrived[block(0), :] + arrived[block(2), :]
        pressures = arrived[block(1), :] + arrived[block(3), :]
    else:
        heads, pressures = arrived[block(0), :], arrived[block(1), :]
    pull = fixed["weight"][...] * (now["slots"][...] - pressures)
    perforated = into_cells(fixed["rows_to"][...], fixed["start"][...], pull)

    side_low = rows_to_tile(arrived[peer_rows(-1), :], pad)
    side_high = rows_to_tile(arrived[peer_rows(1), :], pad)
    side_low = jnp.where(gy == 0, 0.0, side_low)
    side_high = jnp.where(gy == lax.axis_size("gy") - 1, 0.0, side_high)
    small = lanes((8, 128))
    ahead = pltpu.roll(side_high, 127, 1)
    sides = [jnp.where((small & 1) == odd, side_low, ahead) for odd in range(2)]
    open_low, open_high = gx > 0, gx < lax.axis_size("gx") - 1

    state = now["state"][...]
    linked, across, source = [fixed["fixed"][n] for n in range(3)]
    push = fixed["own_weight"][...] * (to_rows(heads) - now["at_slots"][...])
    number = fixed["index"][...]
    inflow = into_segments(push, number, fixed["table"][...])
    flux = across * (state - linked * previous(state))
    seg_res = source - flux + following(linked * flux) + inflow

    lane = lanes((STEP, 128))
    sub = subs((STEP, 128)) & 7
    numer = jnp.zeros((STEP, 128), F32)
    denom = jnp.zeros((STEP, 128), F32)
    if final:
        omega = extra["omega"][0:1, 0:1]
    for t in range(CHUNKS):
        rows = chunk(t)
        tx, ty = [fixed["trans"][n, rows, :].astype(F32) for n in range(2)]
        tx = jnp.where(
            sub == 0, jnp.where(open_low, tx, 0.0),
            jnp.where((sub == 7) & open_high, tx, 0.0),
        )
        ty = jnp.where((lane == 0) | (lane == 127), ty, 0.0)
        terms = []
        for n in range(3):
            j = n * NZ + 2 * t
            low, high = now["from_low"][j : j + 2, :], now["from_high"][j : j + 2, :]
            nx = jnp.where(sub == 0, spread_pair(low), spread_pair(high))
            ny = jnp.concatenate(
                [pltpu.roll(sides[(j + h) & 1], (128 - j - h) % 128, 1) for h in range(2)], axis=0
            )
            share = fixed["mobility"][3 * n, rows, :].astype(F32)
            value = now["near"][n, rows, :] + tx * nx + ty * ny
            terms.append(value - share * perforated[t * STEP : (t + 1) * STEP])
        if kind in ("last", "final"):
            own = mix(fixed["diag"], rows, [extra["field"][n, rows, :] for n in range(3)])
            for n in range(3):
                before = extra["rhs"][n, rows, :]
                change = (own[n] + before) - terms[n]
                if final:
                    kept = extra["change"][n, rows, :]
                    before = before - omega * kept
                    change = kept + omega * (change - 2.0 * kept)
                else:
                    out["change"][n, rows, :] = change
                numer += before * change
                denom += change * change
        if not final:
            values = solve(fixed["diag"], rows, terms, fixed["scale"][rows, :])[0]
            forward[rows, :] = values[0]
            if kind == "keep":
                for n in range(3):
                    out["field"][n, rows, :] = values[n]
            borders(values, fixed["mobility"], fixed["trans"], weighted, along, t)

    if kind in ("last", "final"):
        before = source
        change = source - seg_res
        if final:
            kept = extra["seg_change"][...]
            before = source - omega * kept
            change = kept + omega * (change - 2.0 * kept)
        else:
            out["seg_change"][...] = change
        above = jnp.sum(numer, keepdims=True) + jnp.sum(before * change, keepdims=True)
        below = jnp.sum(denom, keepdims=True) + jnp.sum(change * change, keepdims=True)
        place = lanes((PEERS, 128))
        if final:
            out["message"][...] = jnp.where(
                place == 60, above, jnp.where(place == 61, below, 0.0)
            )
            return
        sums = jnp.where(small == 0, above, jnp.where(small == 1, below, 0.0))
        out["sums"][...] = sums
        out["toward_high"][60:64, :] = sums[0:4]
    if kind == "omega":
        out["omega"][...] = jnp.broadcast_to(collected(arrived[block(0), :]), (8, 128))
    message = wide
    advanced = state + seg_res / fixed["diagonal"][...]
    out["state"][...] = advanced
    values = segment_values(advanced, number)
    out["at_slots"][...] = values
    cells = slot_values(fixed["rows_of"][...], fixed["start"][...], forward[...])
    out["slots"][...] = cells
    high, message[block(2), :] = halves(cells)
    if kind == "after":
        relayed = jnp.broadcast_to(now["from_low"][60:61, :], (8, 128))
        row = jnp.broadcast_to(carried(extra["sums"][...], relayed), (PEERS, 128))
        high = jnp.where(lanes((PEERS, 128)) < 12, row, high)
    message[block(0), :] = high
    message[block(1), :], message[block(3), :] = halves(to_columns(values))
    toward_high = out["toward_high"]
    if kind == "last":
        toward_high = toward_high.at[pl.ds(0, 3 * NZ), :]
    send_borders(fixed["trans"], weighted, along, out["toward_low"], toward_high, message, pad)
    out["message"][...] = message[...].astype(BF16)


def finish(arrived, omega, field_one, field_two, state_one, state_two, cells, segments):
    first = omega[0:1, 0:1]
    second = ratio(arrived[...], 60)

    def blend(one, two):
        kept = first * one
        return kept + second * (one + first * (two - one) - kept)

    for n in range(3):
        for t in range(CHUNKS):
            rows = chunk(t)
            cells[n, rows, :] = blend(field_one[n, rows, :], field_two[n, rows, :])
    segments[...] = blend(state_one[0:2], state_two[0:2])


CELLS = ((3, ROWS, 128), F32)
PAIRS = ((PEERS, 128), F32)
MESSAGE = ((4 * PEERS, 128), F32)
TILE = ((8, 128), F32)
EDGE = ((3 * NZ, 128), F32)
SHAPES = {
    "weighted": CELLS, "toward_low": EDGE, "toward_high": EDGE, "message": MESSAGE, "slots": PAIRS,
    "at_slots": TILE, "state": TILE, "omega": TILE, "field": CELLS, "change": CELLS,
    "seg_change": TILE, "sums": TILE,
}


def shape_of(kind, name):
    if kind == "last" and name == "toward_high":
        return ((64, 128), F32)
    if name != "message":
        return SHAPES[name]
    if kind == "final":
        return PAIRS
    return (MESSAGE[0], BF16)


SCRATCH = (
    pltpu.VMEM((3 * ROWS, 128), F32),
    pltpu.VMEM((16, 128), F32),
    pltpu.VMEM((ROWS, 128), F32),
)


def call(body, outs, args, scratch=(), name=None, space=pltpu.VMEM, grant=24 * 1024 * 1024):
    moved = sum(a.size * a.dtype.itemsize for a in args)
    return pl.pallas_call(
        body,
        out_shape=[jax.ShapeDtypeStruct(*out) for out in outs],
        in_specs=[pl.BlockSpec(memory_space=space)] * len(args),
        out_specs=[pl.BlockSpec(memory_space=pltpu.VMEM)] * len(outs),
        scratch_shapes=list(scratch),
        compiler_params=pltpu.CompilerParams(vmem_limit_bytes=grant),
        cost_estimate=pl.CostEstimate(flops=4_000_000, bytes_accessed=moved, transcendentals=0),
        name=name,
    )(*args)


def exchange(message):
    return lax.all_to_all(message, AXES, split_axis=0, concat_axis=0, tiled=True)


def neighbours(toward_low, toward_high):
    count = lax.axis_size("gx")
    up = [(i, (i + 1) % count) for i in range(count)]
    down = [(b, a) for a, b in up]
    return {
        "from_low": lax.ppermute(toward_high, "gx", up),
        "from_high": lax.ppermute(toward_low, "gx", down),
    }


def on_device(
    rhs, diag_block, mobility, trans, perf_cell, perf_pi, perf_seg, seg_parent, seg_trans, seg_rhs
):
    rhs = rhs.reshape(3, ROWS, 128)
    diag = diag_block.reshape(9, ROWS, 128)
    mobility = mobility.reshape(9, ROWS, 128)
    trans = trans.reshape(3, ROWS, 128)
    index = perf_seg[0]

    fixed = {"diag": diag, "mobility": mobility, "trans": trans, "index": index}
    inputs = [rhs, diag, mobility, trans, perf_cell[0], perf_pi[0], index]
    inputs += [a.reshape(2, 128) for a in (seg_parent, seg_trans, seg_rhs)]
    (rows_of, rows_to, start, weight, slots, constants, scale, weighted, toward_low, toward_high,
     message) = call(
        cell_setup,
        [((PEERS, ROWS), BF16), ((ROWS, PEERS), BF16),
         ((PEERS, 128), jnp.int32), PAIRS, PAIRS, ((4, 8, 128), F32), ((ROWS, 128), F32), CELLS, EDGE, EDGE,
         ((24 * PEERS, 128), BF16)],
        inputs,
        SCRATCH + (pltpu.VMEM((8 * PEERS, 128), F32),)
        + tuple(pltpu.VMEM(a.shape, a.dtype) for a in inputs) + (pltpu.SemaphoreType.DMA((10,)),),
        name="cell_setup",
        space=pltpu.HBM,
        grant=64 * 1024 * 1024 - 256 * 1024,
    )
    arrived = exchange(message)

    def inside(weighted):
        return call(interior, [CELLS], [weighted, trans, rhs], name="interior")[0]

    (table,) = call(well_tables, [((128, CAP * 128), BF16)], [index], name="well_tables")
    fixed.update(rows_of=rows_of, rows_to=rows_to, start=start, weight=weight, scale=scale)
    now = {"near": inside(weighted), "slots": slots}
    now.update(neighbours(toward_low, toward_high))
    now["arrived"], own_weight, state, at_slots, diagonal = call(
        well_setup,
        [MESSAGE, TILE, TILE, TILE, TILE],
        [arrived, index, table, constants],
        [pltpu.VMEM((24 * PEERS, 128), F32), pltpu.VMEM((CAP, PEERS, 128), F32)],
        name="well_setup",
    )
    fixed.update(own_weight=own_weight, table=table, fixed=constants, diagonal=diagonal)
    now.update(at_slots=at_slots, state=state)
    saved = {"rhs": rhs}

    def advance(kind, now):
        args = [now[name] for name in MOVING]
        args += [fixed[name] for name in STEADY]
        args += [saved[name] for name in MORE_IN[kind]]
        names = results_of(kind)
        out = call(
            functools.partial(sweep, kind),
            [shape_of(kind, name) for name in names],
            args,
            SCRATCH + (pltpu.VMEM(*MESSAGE),),
            name="sweep_" + kind,
        )
        out = dict(zip(names, out))
        out["arrived"] = exchange(out.pop("message"))
        if kind != "final":
            out.update(neighbours(out.pop("toward_low"), out.pop("toward_high")))
            out["near"] = inside(out.pop("weighted"))
        return out

    now = advance("plain", now)
    now = advance("plain", now)
    one = advance("keep", now)
    saved["field"] = one["field"]
    now = advance("last", one)
    saved.update(change=now["change"], seg_change=now["seg_change"], sums=now["sums"])
    now = advance("after", now)
    now = advance("omega", now)
    saved["omega"] = now["omega"]
    two = advance("keep", now)
    saved["field"] = two["field"]
    sums = advance("final", two)
    cells, segments = call(
        finish,
        [CELLS, ((2, 128), F32)],
        [sums["arrived"], saved["omega"], one["field"], two["field"], one["state"], two["state"]],
        name="finish",
    )
    return cells.reshape(3, NZ, CX, CY), segments.reshape(256)


def solution(mesh):
    grid = P(None, None, "gx", "gy")
    pairs = P(AXES, None, None)
    flat = P(AXES)
    return jax.shard_map(
        on_device,
        mesh=mesh,
        in_specs=(grid, grid, grid, grid, pairs, pairs, pairs, flat, flat, flat),
        out_specs=(grid, flat),
        check_vma=False,
    )
```

```python
import functools

import jax
import jax.numpy as jnp
from jax import lax
from jax.experimental import pallas as pl
from jax.experimental.pallas import tpu as pltpu
from jax.sharding import PartitionSpec as P

F32 = jnp.float32
BF16 = jnp.bfloat16
AXES = ("gx", "gy")
NZ, CX, CY = 20, 8, 128
ROWS = NZ * CX
STEP = 16
CHUNKS = ROWS // STEP
PEERS = 128
CAP = 8


def lanes(shape):
    return lax.broadcasted_iota(jnp.int32, shape, 1)


def subs(shape):
    return lax.broadcasted_iota(jnp.int32, shape, 0)


def halves(x):
    high = x.astype(BF16).astype(F32)
    return high, x - high


def pick_rows(onehot, x):
    def dot(part):
        return lax.dot_general(
            onehot, part.astype(BF16), (((1,), (0,)), ((), ())), preferred_element_type=F32
        )

    high, low = halves(x)
    return dot(low) + dot(high)


def is_slot(lane):
    return (lane & 63) >= 60


def slot_values(rows_of, start, first):
    lane = lanes((PEERS, CY))
    number = (lane & 3) + jnp.where(lane >= 64, 4, 0)
    picked = pick_rows(rows_of, first)
    window = jnp.take_along_axis(picked, (start + number) & (CY - 1), axis=1)
    return jnp.where(is_slot(lane), window, 0.0)


def into_cells(rows_to, start, flows):
    number = (lanes((PEERS, CY)) - start) & (CY - 1)
    place = jnp.where(number < 4, number + 60, jnp.where(number < CAP, number + 120, 0))
    return pick_rows(rows_to, jnp.take_along_axis(flows, place, axis=1))


def segment_values(state, index):
    low = index & 127
    first = jnp.take_along_axis(jnp.broadcast_to(state[0:1], (8, 128)), low, axis=1)
    second = jnp.take_along_axis(jnp.broadcast_to(state[1:2], (8, 128)), low, axis=1)
    return jnp.where(index >= 128, second, first)


def into_segments(values, index, table):
    parts = halves(values)
    sub = subs((16, 128))
    upper = (index >= 128).astype(jnp.int32)
    tiles = []
    for k in range(CAP):
        row = [jnp.broadcast_to(part[k : k + 1], (16, 128)) for part in parts]
        mine = jnp.broadcast_to(upper[k : k + 1], (16, 128)) == (sub & 1)
        tile = jnp.where(sub < 2, row[0], row[1])
        tiles.append(jnp.where(mine & (sub < 4), tile, 0.0).astype(BF16))
    left = jnp.concatenate(tiles, axis=1)
    out = lax.dot_general(left, table, (((1,), (1,)), ((), ())), preferred_element_type=F32)[:8]
    return jnp.where(subs((8, 128)) < 2, pltpu.roll(out, 6, 0) + out, 0.0)


def previous(state):
    moved = pltpu.roll(state, 1, 1)
    return jnp.where(lanes((8, 128)) == 0, pltpu.roll(moved, 1, 0), moved)


def following(state):
    moved = pltpu.roll(state, 127, 1)
    return jnp.where(lanes((8, 128)) == 127, pltpu.roll(moved, 7, 0), moved)


def to_columns(values):
    gap = jnp.zeros((60, 128), F32)
    return jnp.concatenate([gap, values[0:4], gap, values[4:8]], axis=0).T


def to_rows(columns):
    turned = columns.T
    return jnp.concatenate([turned[60:64], turned[124:128]], axis=0)


def field(n):
    return pl.ds(n, PEERS, stride=8)


def block(n):
    return pl.ds(n, PEERS, stride=4)


def chunk(t):
    return pl.ds(t * STEP, STEP)


def me():
    return lax.axis_index("gx") * 16 + lax.axis_index("gy")


def peer_rows(shift, pitch=4):
    return pl.ds(pitch * ((me() + shift) & (PEERS - 1)), 4)


def tile_to_rows(tile, pad):
    pad[0:8] = tile
    pad[8:16] = pltpu.roll(tile, 64, 1)
    even = pad[pl.ds(0, 4, stride=2), :]
    odd = pad[pl.ds(9, 4, stride=2), :]
    return jnp.where(lanes((4, 128)) < 64, even, odd)


def rows_to_tile(four, pad):
    pad[0:4] = four
    pad[8:16] = pltpu.roll(pad[0:8], 64, 1)
    low, high = pad[0:4], pad[8:12]
    pad[pl.ds(0, 4, stride=2), :] = low
    pad[pl.ds(1, 4, stride=2), :] = high
    return pad[0:8]


def mix(matrix, rows, vector):
    entry = [matrix[n, rows, :].astype(F32) for n in range(9)]
    x, y, z = vector
    return [entry[3 * n] * x + entry[3 * n + 1] * y + entry[3 * n + 2] * z for n in range(3)]


def solve(diag, rows, vector, scale=None):
    a, b, c, d, e, f, g, h, i = [diag[n, rows, :].astype(F32) for n in range(9)]
    x, y, z = vector
    p, q, s = e * i - f * h, f * g - d * i, d * h - e * g
    if scale is None:
        scale = 1.0 / (a * p + b * q + c * s)
    return [
        (p * x + (c * h - b * i) * y + (b * f - c * e) * z) * scale,
        (q * x + (a * i - c * g) * y + (c * d - a * f) * z) * scale,
        (s * x + (b * g - a * h) * y + (a * e - b * d) * z) * scale,
    ], scale


def borders(values, mobility, trans, weighted, along, t):
    rows = chunk(t)
    tx = trans[0, rows, :].astype(F32)
    for n, value in enumerate(mix(mobility, rows, values)):
        weighted[n, rows, :] = value
        along[pl.ds(n * ROWS + t * STEP, STEP), :] = tx * value


def send_borders(trans, weighted, along, toward_low, toward_high, message, pad, pitch=4):
    toward_low[...] = along[pl.ds(0, 3 * NZ, stride=CX), :]
    toward_high[...] = along[pl.ds(CX - 1, 3 * NZ, stride=CX), :]
    small = lanes((8, 128))
    packed = jnp.zeros((8, 128), F32)
    for t in range(CHUNKS):
        ty = trans[1, chunk(t), :].astype(F32)
        for n in range(3):
            py = ty * weighted[n, chunk(t), :]
            for half in range(2):
                j = n * NZ + 2 * t + half
                moved = pltpu.roll(py[8 * half : 8 * half + 8], 2 * j + 1, 1)
                packed = jnp.where((small >> 1) == j, moved, packed)
    high = jnp.take_along_axis(packed, (2 * small) & 127, axis=1)
    low = jnp.take_along_axis(packed, (2 * small + 1) & 127, axis=1)
    mine = is_slot(lanes((4, 128)))
    for shift, tile in ((1, high), (-1, low)):
        rows = peer_rows(shift, pitch)
        packed = tile_to_rows(tile, pad)
        message[rows, :] = jnp.where(mine, message[rows, :], packed)


def interior(weighted, trans, near):
    lane = lanes((STEP, 128))
    sub = subs((STEP, 128)) & 7
    zero = jnp.zeros((8, 128), F32)
    up = [trans[2, chunk(t), :].astype(F32) for t in range(CHUNKS)]
    for t in range(CHUNKS):
        rows = chunk(t)
        tx, ty = [trans[n, rows, :].astype(F32) for n in range(2)]
        tz = up[t]
        for n in range(3):
            value = weighted[n, rows, :]
            px, py = tx * value, ty * value
            nx = jnp.where(sub == 0, 0.0, pltpu.roll(px, 1, 0)) + jnp.where(
                sub == 7, 0.0, pltpu.roll(px, STEP - 1, 0)
            )
            ny = jnp.where(lane == 0, 0.0, pltpu.roll(py, 1, 1)) + jnp.where(
                lane == 127, 0.0, pltpu.roll(py, 127, 1)
            )
            pz = tz * value
            below = zero
            above = zero
            if t:
                below = up[t - 1][8:16] * weighted[n, pl.ds(t * STEP - 8, 8), :]
            if t + 1 < CHUNKS:
                above = up[t + 1][0:8] * weighted[n, pl.ds(t * STEP + STEP, 8), :]
            nz = jnp.concatenate([below + pz[8:16], pz[0:8] + above], axis=0)
            near[n, rows, :] = tx * nx + ty * ny + tz * nz


def cell_setup(rhs_in, diag_in, mobility_in, trans_in, cells_in, pi_in, index_in, parent_in,
               across_in, source_in,
               rows_of, rows_to, start, weight, slots, fixed, scale,
               weighted, toward_low, toward_high, message, along, pad, forward, own,
               rhs, diag, mobility, trans, cells, pi, index, parent, across, source, sems):
    pairs = ((cells_in, cells), (pi_in, pi), (index_in, index), (parent_in, parent),
             (across_in, across), (source_in, source), (rhs_in, rhs), (diag_in, diag),
             (mobility_in, mobility), (trans_in, trans))
    copies = [pltpu.make_async_copy(a, b, sems.at[n]) for n, (a, b) in enumerate(pairs)]
    for copy in copies:
        copy.start()
    for copy in copies[:6]:
        copy.wait()
    zeros = jnp.zeros((6, 128), F32)
    linked = jnp.concatenate([(parent[...] >= 0).astype(F32), zeros], axis=0)
    moving = jnp.concatenate([across[...], zeros], axis=0)
    given = jnp.concatenate([source[...], zeros], axis=0)
    partial = moving + following(linked * moving)
    fixed[0] = linked
    fixed[1] = moving
    fixed[2] = given
    fixed[3] = partial
    number = index[...]
    own[field(1), :], own[field(3), :] = halves(to_columns(segment_values(given, number)))
    own[field(4), :], own[field(5), :] = halves(to_columns(segment_values(partial, number)))
    own[field(7), :] = jnp.zeros((PEERS, 128), F32)
    base = cells[0:1, :]
    row = lax.shift_right_logical(base, 7)
    live = pi[...]
    gap = jnp.zeros((44, 128), F32)
    info = jnp.concatenate(
        [jnp.broadcast_to(row.astype(F32), (8, 128)),
         jnp.broadcast_to((base & 127).astype(F32), (8, 128)),
         gap, live[0:4], gap, jnp.zeros((16, 128), F32), live[4:8]],
        axis=0,
    ).T
    rows_to[...] = (subs((ROWS, PEERS)) == jnp.broadcast_to(row, (ROWS, PEERS))).astype(F32).astype(BF16)
    row_column = jnp.broadcast_to(info[:, 0:1], (PEERS, ROWS)).astype(jnp.int32)
    rows_of[...] = (lanes((PEERS, ROWS)) == row_column).astype(F32).astype(BF16)
    begin = jnp.broadcast_to(info[:, 8:9], (PEERS, 128)).astype(jnp.int32)
    start[...] = begin
    weights = jnp.where(is_slot(lanes((PEERS, 128))), info, 0.0)
    weight[...] = weights
    own[field(6), :] = halves(weights)[1]
    high = halves(live)[0]
    order = number.astype(F32)
    common = jnp.concatenate([high, order], axis=0).astype(BF16)
    for d in range(0, PEERS, 2):
        message[pl.ds(24 * d + 32, 16), :] = common
    for copy in copies[6:8]:
        copy.wait()
    for t in range(CHUNKS):
        rows = chunk(t)
        values, scale[rows, :] = solve(diag, rows, [rhs[n, rows, :] for n in range(3)])
        forward[rows, :] = values[0]
        for n in range(3):
            weighted[n, rows, :] = values[n]
    values = slot_values(rows_of[...], begin, forward[...])
    slots[...] = values
    own[field(0), :], own[field(2), :] = halves(values)
    for copy in copies[8:]:
        copy.wait()
    for t in range(CHUNKS):
        values = [weighted[n, chunk(t), :] for n in range(3)]
        borders(values, mobility, trans, weighted, along, t)
    send_borders(trans, weighted, along, toward_low, toward_high, own, pad, 8)
    for d in range(0, PEERS, 2):
        two = [own[pl.ds(8 * d, 8), :], high, order, own[pl.ds(8 * d + 8, 8), :]]
        message[pl.ds(24 * d, 32), :] = jnp.concatenate(two, axis=0).astype(BF16)


def well_tables(index, table):
    low = index[...] & 127
    for k in range(CAP):
        hit = subs((128, 128)) == jnp.broadcast_to(low[k : k + 1], (128, 128))
        table[:, 128 * k : 128 * (k + 1)] = hit.astype(F32).astype(BF16)


def well_setup(arrived, index, table, fixed, message, weight, state, at_slots, diagonal,
               wide, turned):
    wide[...] = arrived[...].astype(F32)

    def part(n):
        return wide[pl.ds(n, PEERS, stride=24), :]

    lane = lanes((PEERS, 128))
    mine = lane == me()
    for k in range(CAP):
        turned[k] = part(8 + k).T
    total = part(4) + part(5)
    for k in range(CAP):
        target = jnp.sum(jnp.where(mine, part(16 + k), 0.0), axis=1, keepdims=True)
        target = jnp.broadcast_to(target, (PEERS, 128))
        found = jnp.zeros((PEERS, 128), F32)
        for m in range(CAP):
            found += jnp.where(part(16 + m) == target, turned[m], 0.0)
        place = 60 + k if k < 4 else 120 + k
        total += jnp.where(lane == place, jnp.sum(found, axis=1, keepdims=True), 0.0)
    slot = is_slot(lane)
    pressures = (part(1) + part(3)) / jnp.where(slot, total, 1.0)
    message[block(0), :] = jnp.where(slot, part(0) + part(2), part(0))
    message[block(1), :] = jnp.where(slot, pressures, part(1))
    message[block(2), :] = part(2)
    message[block(3), :] = part(3)
    pi = jnp.concatenate([turned[k, pl.ds(me(), 1), :] for k in range(CAP)], axis=0)
    pi += to_rows(part(6))
    weight[...] = pi
    number = index[...]
    total = fixed[3] + into_segments(pi, number, table[...])
    total = jnp.where(subs((8, 128)) < 2, total, 1.0)
    diagonal[...] = total
    now = fixed[2] / total
    state[...] = now
    at_slots[...] = segment_values(now, number)


def ratio(sums, place):
    total = jnp.sum(sums, axis=0, keepdims=True)
    lane = lanes((1, 128))
    numer = jnp.sum(jnp.where(lane == place, total, 0.0), axis=1, keepdims=True)
    denom = jnp.sum(jnp.where(lane == place + 1, total, 0.0), axis=1, keepdims=True)
    return numer / denom


def parts_of(x):
    high, rest = halves(x)
    return (high,) + halves(rest)


def carried(own, relayed):
    lane = lanes((8, 128))
    row = jnp.zeros((8, 128), F32)
    for n, part in enumerate(parts_of(own) + parts_of(relayed)):
        moved = pltpu.roll(part, 2 * n, 1) if n else part
        row = jnp.where((lane >> 1) == n, moved, row)
    return row[0:1]


def collected(rows):
    lane, source = lanes((PEERS, 128)), subs((PEERS, 128))

    def at(shift):
        return source == ((me() + shift) & (PEERS - 1))

    direct = (lane < 6) & ~(at(1) | at(-1))
    through = (lane >= 6) & (lane < 12) & (at(15) | at(17))
    total = jnp.sum(jnp.where(direct | through, rows, 0.0), axis=0, keepdims=True)
    odd = (lanes((1, 128)) & 1) == 1
    numer = jnp.sum(jnp.where(odd, 0.0, total), axis=1, keepdims=True)
    denom = jnp.sum(jnp.where(odd, total, 0.0), axis=1, keepdims=True)
    return numer / denom


def spread_pair(two):
    return jnp.concatenate(
        [jnp.broadcast_to(two[h : h + 1], (8, 128)) for h in range(2)], axis=0
    )


STEADY = ("rhs", "diag", "mobility", "trans", "rows_of", "rows_to", "start", "weight",
          "own_weight", "table", "index", "fixed", "diagonal", "scale")
MOVING = ("arrived", "near", "from_low", "from_high", "slots", "at_slots", "state")
NEXT = ("weighted", "toward_low", "toward_high", "message", "slots", "at_slots", "state")
MORE_IN = {
    "plain": (), "keep": (), "last": ("field",), "after": ("sums",), "omega": (),
    "final": ("field", "change", "seg_change", "omega"),
}
MORE_OUT = {
    "plain": (), "keep": ("field",), "last": ("change", "seg_change", "sums"),
    "after": (), "omega": ("omega",), "final": (),
}


def results_of(kind):
    return ("message",) if kind == "final" else NEXT + MORE_OUT[kind]


def sweep(kind, *refs):
    take = iter(refs)
    now = {name: next(take) for name in MOVING}
    fixed = {name: next(take) for name in STEADY}
    extra = {name: next(take) for name in MORE_IN[kind]}
    out = {name: next(take) for name in results_of(kind)}
    along, pad, forward, wide = take
    weighted = out.get("weighted")
    final = kind == "final"
    gx, gy = lax.axis_index("gx"), lax.axis_index("gy")

    arrived = now["arrived"]
    if arrived.dtype == BF16:
        wide[...] = arrived[...].astype(F32)
        arrived = wide
        heads = arrived[block(0), :] + arrived[block(2), :]
        pressures = arrived[block(1), :] + arrived[block(3), :]
    else:
        heads, pressures = arrived[block(0), :], arrived[block(1), :]
    pull = fixed["weight"][...] * (now["slots"][...] - pressures)
    perforated = into_cells(fixed["rows_to"][...], fixed["start"][...], pull)

    side_low = rows_to_tile(arrived[peer_rows(-1), :], pad)
    side_high = rows_to_tile(arrived[peer_rows(1), :], pad)
    side_low = jnp.where(gy == 0, 0.0, side_low)
    side_high = jnp.where(gy == lax.axis_size("gy") - 1, 0.0, side_high)
    small = lanes((8, 128))
    ahead = pltpu.roll(side_high, 127, 1)
    sides = [jnp.where((small & 1) == odd, side_low, ahead) for odd in range(2)]
    open_low, open_high = gx > 0, gx < lax.axis_size("gx") - 1

    state = now["state"][...]
    linked, across, source = [fixed["fixed"][n] for n in range(3)]
    push = fixed["own_weight"][...] * (to_rows(heads) - now["at_slots"][...])
    number = fixed["index"][...]
    inflow = into_segments(push, number, fixed["table"][...])
    flux = across * (state - linked * previous(state))
    seg_res = source - flux + following(linked * flux) + inflow

    lane = lanes((STEP, 128))
    sub = subs((STEP, 128)) & 7
    numer = jnp.zeros((STEP, 128), F32)
    denom = jnp.zeros((STEP, 128), F32)
    if final:
        omega = extra["omega"][0:1, 0:1]
    for t in range(CHUNKS):
        rows = chunk(t)
        tx, ty = [fixed["trans"][n, rows, :].astype(F32) for n in range(2)]
        tx = jnp.where(
            sub == 0, jnp.where(open_low, tx, 0.0),
            jnp.where((sub == 7) & open_high, tx, 0.0),
        )
        ty = jnp.where((lane == 0) | (lane == 127), ty, 0.0)
        terms = []
        for n in range(3):
            j = n * NZ + 2 * t
            low, high = now["from_low"][j : j + 2, :], now["from_high"][j : j + 2, :]
            nx = jnp.where(sub == 0, spread_pair(low), spread_pair(high))
            ny = jnp.concatenate(
                [pltpu.roll(sides[(j + h) & 1], (128 - j - h) % 128, 1) for h in range(2)], axis=0
            )
            share = fixed["mobility"][3 * n, rows, :].astype(F32)
            value = now["near"][n, rows, :] + tx * nx + ty * ny
            terms.append(value - share * perforated[t * STEP : (t + 1) * STEP])
        if kind in ("last", "final"):
            own = mix(fixed["diag"], rows, [extra["field"][n, rows, :] for n in range(3)])
            for n in range(3):
                change = own[n] - terms[n]
                before = fixed["rhs"][n, rows, :]
                if final:
                    kept = extra["change"][n, rows, :]
                    before = before - omega * kept
                    change = kept + omega * (change - 2.0 * kept)
                else:
                    out["change"][n, rows, :] = change
                numer += before * change
                denom += change * change
        if not final:
            total = [fixed["rhs"][n, rows, :] + terms[n] for n in range(3)]
            values = solve(fixed["diag"], rows, total, fixed["scale"][rows, :])[0]
            forward[rows, :] = values[0]
            if kind == "keep":
                for n in range(3):
                    out["field"][n, rows, :] = values[n]
            borders(values, fixed["mobility"], fixed["trans"], weighted, along, t)

    if kind in ("last", "final"):
        before = source
        change = source - seg_res
        if final:
            kept = extra["seg_change"][...]
            before = source - omega * kept
            change = kept + omega * (change - 2.0 * kept)
        else:
            out["seg_change"][...] = change
        above = jnp.sum(numer, keepdims=True) + jnp.sum(before * change, keepdims=True)
        below = jnp.sum(denom, keepdims=True) + jnp.sum(change * change, keepdims=True)
        place = lanes((PEERS, 128))
        if final:
            out["message"][...] = jnp.where(
                place == 60, above, jnp.where(place == 61, below, 0.0)
            )
            return
        sums = jnp.where(small == 0, above, jnp.where(small == 1, below, 0.0))
        out["sums"][...] = sums
        out["toward_high"][60:64, :] = sums[0:4]
    if kind == "omega":
        out["omega"][...] = jnp.broadcast_to(collected(arrived[block(0), :]), (8, 128))
    message = wide
    advanced = state + seg_res / fixed["diagonal"][...]
    out["state"][...] = advanced
    values = segment_values(advanced, number)
    out["at_slots"][...] = values
    cells = slot_values(fixed["rows_of"][...], fixed["start"][...], forward[...])
    out["slots"][...] = cells
    high, message[block(2), :] = halves(cells)
    if kind == "after":
        relayed = jnp.broadcast_to(now["from_low"][60:61, :], (8, 128))
        row = jnp.broadcast_to(carried(extra["sums"][...], relayed), (PEERS, 128))
        high = jnp.where(lanes((PEERS, 128)) < 12, row, high)
    message[block(0), :] = high
    message[block(1), :], message[block(3), :] = halves(to_columns(values))
    toward_high = out["toward_high"]
    if kind == "last":
        toward_high = toward_high.at[pl.ds(0, 3 * NZ), :]
    send_borders(fixed["trans"], weighted, along, out["toward_low"], toward_high, message, pad)
    out["message"][...] = message[...].astype(BF16)


def finish(arrived, omega, field_one, field_two, state_one, state_two, cells, segments):
    first = omega[0:1, 0:1]
    second = ratio(arrived[...], 60)

    def blend(one, two):
        kept = first * one
        return kept + second * (one + first * (two - one) - kept)

    for n in range(3):
        for t in range(CHUNKS):
            rows = chunk(t)
            cells[n, rows, :] = blend(field_one[n, rows, :], field_two[n, rows, :])
    segments[...] = blend(state_one[0:2], state_two[0:2])


CELLS = ((3, ROWS, 128), F32)
PAIRS = ((PEERS, 128), F32)
MESSAGE = ((4 * PEERS, 128), F32)
TILE = ((8, 128), F32)
EDGE = ((3 * NZ, 128), F32)
SHAPES = {
    "weighted": CELLS, "toward_low": EDGE, "toward_high": EDGE, "message": MESSAGE, "slots": PAIRS,
    "at_slots": TILE, "state": TILE, "omega": TILE, "field": CELLS, "change": CELLS,
    "seg_change": TILE, "sums": TILE,
}


def shape_of(kind, name):
    if kind == "last" and name == "toward_high":
        return ((64, 128), F32)
    if name != "message":
        return SHAPES[name]
    if kind == "final":
        return PAIRS
    return (MESSAGE[0], BF16)


SCRATCH = (
    pltpu.VMEM((3 * ROWS, 128), F32),
    pltpu.VMEM((16, 128), F32),
    pltpu.VMEM((ROWS, 128), F32),
)


def call(body, outs, args, scratch=(), name=None, space=pltpu.VMEM, grant=24 * 1024 * 1024):
    moved = sum(a.size * a.dtype.itemsize for a in args)
    return pl.pallas_call(
        body,
        out_shape=[jax.ShapeDtypeStruct(*out) for out in outs],
        in_specs=[pl.BlockSpec(memory_space=space)] * len(args),
        out_specs=[pl.BlockSpec(memory_space=pltpu.VMEM)] * len(outs),
        scratch_shapes=list(scratch),
        compiler_params=pltpu.CompilerParams(vmem_limit_bytes=grant),
        cost_estimate=pl.CostEstimate(flops=4_000_000, bytes_accessed=moved, transcendentals=0),
        name=name,
    )(*args)


def exchange(message):
    return lax.all_to_all(message, AXES, split_axis=0, concat_axis=0, tiled=True)


def neighbours(toward_low, toward_high):
    count = lax.axis_size("gx")
    up = [(i, (i + 1) % count) for i in range(count)]
    down = [(b, a) for a, b in up]
    return {
        "from_low": lax.ppermute(toward_high, "gx", up),
        "from_high": lax.ppermute(toward_low, "gx", down),
    }


def on_device(
    rhs, diag_block, mobility, trans, perf_cell, perf_pi, perf_seg, seg_parent, seg_trans, seg_rhs
):
    rhs = rhs.reshape(3, ROWS, 128)
    diag = diag_block.reshape(9, ROWS, 128)
    mobility = mobility.reshape(9, ROWS, 128)
    trans = trans.reshape(3, ROWS, 128)
    index = perf_seg[0]

    fixed = {"rhs": rhs, "diag": diag, "mobility": mobility, "trans": trans, "index": index}
    inputs = [rhs, diag, mobility, trans, perf_cell[0], perf_pi[0], index]
    inputs += [a.reshape(2, 128) for a in (seg_parent, seg_trans, seg_rhs)]
    (rows_of, rows_to, start, weight, slots, constants, scale, weighted, toward_low, toward_high,
     message) = call(
        cell_setup,
        [((PEERS, ROWS), BF16), ((ROWS, PEERS), BF16),
         ((PEERS, 128), jnp.int32), PAIRS, PAIRS, ((4, 8, 128), F32), ((ROWS, 128), F32), CELLS, EDGE, EDGE,
         ((24 * PEERS, 128), BF16)],
        inputs,
        SCRATCH + (pltpu.VMEM((8 * PEERS, 128), F32),)
        + tuple(pltpu.VMEM(a.shape, a.dtype) for a in inputs) + (pltpu.SemaphoreType.DMA((10,)),),
        name="cell_setup",
        space=pltpu.HBM,
        grant=64 * 1024 * 1024 - 256 * 1024,
    )
    arrived = exchange(message)

    def inside(weighted):
        return call(interior, [CELLS], [weighted, trans], name="interior")[0]

    (table,) = call(well_tables, [((128, CAP * 128), BF16)], [index], name="well_tables")
    fixed.update(rows_of=rows_of, rows_to=rows_to, start=start, weight=weight, scale=scale)
    now = {"near": inside(weighted), "slots": slots}
    now.update(neighbours(toward_low, toward_high))
    now["arrived"], own_weight, state, at_slots, diagonal = call(
        well_setup,
        [MESSAGE, TILE, TILE, TILE, TILE],
        [arrived, index, table, constants],
        [pltpu.VMEM((24 * PEERS, 128), F32), pltpu.VMEM((CAP, PEERS, 128), F32)],
        name="well_setup",
    )
    fixed.update(own_weight=own_weight, table=table, fixed=constants, diagonal=diagonal)
    now.update(at_slots=at_slots, state=state)
    saved = {}

    def advance(kind, now):
        args = [now[name] for name in MOVING]
        args += [fixed[name] for name in STEADY]
        args += [saved[name] for name in MORE_IN[kind]]
        names = results_of(kind)
        out = call(
            functools.partial(sweep, kind),
            [shape_of(kind, name) for name in names],
            args,
            SCRATCH + (pltpu.VMEM(*MESSAGE),),
            name="sweep_" + kind,
        )
        out = dict(zip(names, out))
        out["arrived"] = exchange(out.pop("message"))
        if kind != "final":
            out.update(neighbours(out.pop("toward_low"), out.pop("toward_high")))
            out["near"] = inside(out.pop("weighted"))
        return out

    now = advance("plain", now)
    now = advance("plain", now)
    one = advance("keep", now)
    saved["field"] = one["field"]
    now = advance("last", one)
    saved.update(change=now["change"], seg_change=now["seg_change"], sums=now["sums"])
    now = advance("after", now)
    now = advance("omega", now)
    saved["omega"] = now["omega"]
    two = advance("keep", now)
    saved["field"] = two["field"]
    sums = advance("final", two)
    cells, segments = call(
        finish,
        [CELLS, ((2, 128), F32)],
        [sums["arrived"], saved["omega"], one["field"], two["field"], one["state"], two["state"]],
        name="finish",
    )
    return cells.reshape(3, NZ, CX, CY), segments.reshape(256)


def solution(mesh):
    grid = P(None, None, "gx", "gy")
    pairs = P(AXES, None, None)
    flat = P(AXES)
    return jax.shard_map(
        on_device,
        mesh=mesh,
        in_specs=(grid, grid, grid, grid, pairs, pairs, pairs, flat, flat, flat),
        out_specs=(grid, flat),
        check_vma=False,
    )
```
